32 devices in a mesh: dp: 16 (over z, y, x), fsdp: 2 (over core).
Axes of the slice: x: 2, y: 2, z: 4, core: 2. Of those that a mesh axis runs over, the one named last changes fastest.
Arguments:
- tokens: bfloat16 [128, 512, 768], P(('dp', 'fsdp')), may hold values from -6 to 6
- segment_ids: int32 [128, 512], P(('dp', 'fsdp')), may hold values from 0 to 3, never falling along the last dimension, each value on 1 to 256 neighbouring positions
- cotangent: bfloat16 [128, 512, 768], P(('dp', 'fsdp')), may hold values from -6 to 6
- w_proj: float32 [768, 1536], P(('dp', 'fsdp')), may hold values from -0.3125 to 0.3125
- w_point: float32 [768, 384], P(('dp', 'fsdp')), may hold values from -0.21875 to 0.21875
- w_out: float32 [768, 768], P(('dp', 'fsdp')), may hold values from -0.875 to 0.875
- w_up: float32 [2, 384, 1536], P(None, None, ('dp', 'fsdp')), may hold values from -0.3125 to 0.3125
- w_down: float32 [2, 1536, 384], P(None, ('dp', 'fsdp')), may hold values from -0.15625 to 0.15625
- proj_bias: float32 [4, 384], replicated, may hold values from -1.2 to 1.2
- conv_depth: float32 [9, 768], replicated, may hold values from -2 to 2
- kernel_weight: float32 [384, 54], replicated, may hold values from -0.3125 to 0.3125
- kernel_bias: float32 [54], replicated, may hold values from -3 to 3
- hidden_bias: float32 [4, 768], replicated, may hold values from -1.2 to 1.2
- up_bias: float32 [3072], replicated, may hold values from -1.2 to 1.2
- norm_gain: float32 [2, 768], replicated, may hold values from 0.25 to 1.75
Outputs:
- layer_out: bfloat16 [128, 512, 768], P(('dp', 'fsdp'))
- tokens_grad: float32 [128, 512, 768], P(('dp', 'fsdp'))
- w_proj_grad: float32 [768, 1536], P(('dp', 'fsdp'))
- w_point_grad: float32 [768, 384], P(('dp', 'fsdp'))
- w_out_grad: float32 [768, 768], P(('dp', 'fsdp'))
- w_up_grad: float32 [2, 384, 1536], P(None, None, ('dp', 'fsdp'))
- w_down_grad: float32 [2, 1536, 384], P(None, ('dp', 'fsdp'))
- proj_bias_grad: float32 [4, 384], replicated
- conv_depth_grad: float32 [9, 768], replicated
- kernel_weight_grad: float32 [384, 54], replicated
- kernel_bias_grad: float32 [54], replicated
- hidden_bias_grad: float32 [4, 768], replicated
- up_bias_grad: float32 [3072], replicated
- norm_gain_grad: float32 [2, 768], replicated
The draws below stay inside these ranges and needn't reach their ends.
Inputs may be any that keep to these rules, and one draw needn't show every extreme that they name: `segment_ids`: document ids never fall along a row; each document holds 1 to 256 tokens, and one document of every row exactly 256.
All inputs are finite; a program needn't handle non-finite values.
Results may differ from the reference program's by a relative error of at most 0.012.
The reference program's roundings to bfloat16 on the way count: a program that leaves them out, or rounds other values in their place, can miss the bound.
Values may be sent and summed in bfloat16 or wider, within the bound.
No kernel may reach another device: no remote copies, remote signals or barrier semaphores. Data moves between devices by JAX's collectives and lax.ppermute only.
A program may use at most 256 MiB of HBM per device.

```python
import math
import jax
import jax.numpy as jnp
import numpy as np
from jax import lax

D = 768
FF = 3072
HEADS = 6
HEAD_DIM = 64
KERNEL = 9
GROUPS = 2
SEQ = 512
ATT = 384
ROWS = 128


def strengthened(values, own_key, source, target, shards_of, factor):
    def block_of(dim):
        return (jnp.arange(values.shape[dim]) // (values.shape[dim] // shards_of)).reshape((-1,) + (1,) * (values.ndim - 1 - dim))

    first = jax.random.permutation(own_key, shards_of)[block_of(target)]
    far = (block_of(target) + shards_of // 2) % shards_of
    return jnp.where((block_of(source) == first) | (block_of(source) == far), factor * values, values)


def block_scale(own_key, shape, shards, smallest, top_value):
    factor_of = 1.0
    for dim, shards_of in shards:
        draws = jax.random.uniform(jax.random.fold_in(jax.random.fold_in(own_key, 6), dim), (shards_of,), jnp.float32, smallest / len(shards), top_value / len(shards))
        factor_of = factor_of * jnp.repeat(jnp.exp(draws), shape[dim] // shards_of).reshape((-1,) + (1,) * (len(shape) - 1 - dim))
    return factor_of


def length_profile(amount, total, limit, lean):
    loads = [(1 << 20) // math.isqrt(standing ** lean) + 1 for standing in range(2, amount + 1)]
    rest, counts = total - limit - (amount - 1), [1] * (amount - 1)
    while rest > 0:
        movable = [i for i in range(amount - 1) if counts[i] < limit]
        whole, left = sum([loads[i] for i in movable]), rest
        for i in movable:
            extra = min(limit - counts[i], max(1, left * loads[i] // whole), rest)
            counts[i] = counts[i] + extra
            rest = rest - extra
    return np.array([limit] + counts)


def uneven_parts(own_key, count, total, most, skew):
    if count == 2:
        one = jax.random.randint(own_key, (), max(1, total - most), min(most, total - 1) + 1)
        return jnp.stack([one, total - one])
    tallies = jnp.asarray(length_profile(count, total, most, skew), jnp.int32)
    pairs = (count - 1) // 2
    donor, sink = tallies[1:1 + 2 * pairs:2], tallies[2:2 + 2 * pairs:2]
    slack = jnp.minimum(donor - 1, most - sink)
    moved = jax.random.randint(jax.random.fold_in(own_key, 1), (pairs,), 0, 1 << 20) % (slack + 1)
    tallies = tallies.at[1:1 + 2 * pairs:2].set(donor - moved).at[2:2 + 2 * pairs:2].set(sink + moved)
    return tallies[jax.random.permutation(jax.random.fold_in(own_key, 2), count)]


def scatter_about(key, shape, deviation, most, cuts=(), dtype=jnp.bfloat16):
    array = jax.random.normal(key, shape, jnp.float32) * deviation
    if len(cuts) > 0:
        array = block_scale(key, shape, cuts, -0.22, 0.18) * array
    return jnp.clip(array, min=-most, max=most).astype(dtype)


def gaussian_with(stream_key, shape, width, limit, cuts, heavy, dtype=jnp.bfloat16):
    drawn = width * jax.random.normal(stream_key, shape, jnp.float32)
    if cuts:
        drawn = drawn * block_scale(stream_key, shape, cuts, -0.22, 0.18)
    return jnp.clip(strengthened(drawn, jax.random.fold_in(stream_key, 3), *heavy), -limit, limit).astype(dtype)


def setup_inputs(seed: int = 0) -> dict:
    arg_keys = jax.random.split(jax.random.key(seed), 16)
    tokens = gaussian_with(arg_keys[0], (ROWS, SEQ, D), 1.0, 6.0, ((0, 32),), (0, 2, 32, 2.75))
    segment_ids = jax.vmap(lambda own: jnp.searchsorted(jnp.cumsum(uneven_parts(own, 4, SEQ, SEQ // 2, 0)), jnp.arange(SEQ), side="right"))(jax.random.split(arg_keys[1], ROWS)).reshape((ROWS, SEQ)).astype(jnp.int32)
    cotangent = scatter_about(arg_keys[2], (ROWS, SEQ, D), 1.0, 6.0, ((0, 32),))
    w_proj = scatter_about(arg_keys[3], (D, 4 * ATT), (D // 2) ** -0.5, 0.3125, ((0, 32),), jnp.float32)
    w_point = scatter_about(arg_keys[4], (D, ATT), D ** -0.5, 0.21875, ((0, 32),), jnp.float32)
    w_out = scatter_about(arg_keys[5], (D, D), (D // 16) ** -0.5, 0.875, ((0, 32),), jnp.float32)
    w_up = scatter_about(arg_keys[6], (GROUPS, D // GROUPS, FF // GROUPS), (D // GROUPS) ** -0.5, 0.3125, ((2, 32),), jnp.float32)
    w_down = scatter_about(arg_keys[7], (GROUPS, FF // GROUPS, D // GROUPS), (FF // GROUPS) ** -0.5, 0.15625, ((1, 32),), jnp.float32)
    proj_bias = scatter_about(arg_keys[8], (4, ATT), 0.2, 1.2, (), jnp.float32)
    conv_depth = scatter_about(arg_keys[9], (KERNEL, D), KERNEL ** -0.5, 2.0, (), jnp.float32)
    kernel_weight = scatter_about(arg_keys[10], (ATT, HEADS * KERNEL), ATT ** -0.5, 0.3125, (), jnp.float32)
    kernel_bias = scatter_about(arg_keys[11], (HEADS * KERNEL,), 0.5, 3.0, (), jnp.float32)
    hidden_bias = scatter_about(arg_keys[12], (4, D), 0.2, 1.2, (), jnp.float32)
    up_bias = scatter_about(arg_keys[13], (FF,), 0.2, 1.2, (), jnp.float32)
    norm_gain = jnp.clip(1.0 + 0.15 * jax.random.normal(arg_keys[14], (2, D), jnp.float32), 0.25, 1.75)
    return dict(tokens=tokens, segment_ids=segment_ids, cotangent=cotangent, w_proj=w_proj, w_point=w_point, w_out=w_out, w_up=w_up, w_down=w_down, proj_bias=proj_bias, conv_depth=conv_depth, kernel_weight=kernel_weight, kernel_bias=kernel_bias, hidden_bias=hidden_bias, up_bias=up_bias, norm_gain=norm_gain)


@jax.custom_vjp
def low(v):
    return lax.optimization_barrier(v.astype(jnp.bfloat16)).astype(jnp.float32)

@jax.custom_vjp
def low_back(v):
    return v

def low_keep(v):
    return (low(v), None)

def low_pass(kept, grad):
    return (grad,)

def back_keep(v):
    return (v, None)

def back_low(kept, grad):
    return (low(grad),)
low.defvjp(low_keep, low_pass)
low_back.defvjp(back_keep, back_low)
precise = lax.Precision.HIGHEST
masked_score = -1000000000.0
norm_eps = 1e-12

def shifted(values, offset):
    half_width = KERNEL // 2
    widths = [(0, 0), (half_width, half_width)] + [(0, 0)] * (values.ndim - 2)
    padded = jnp.pad(values, widths)
    return lax.slice_in_dim(padded, half_width + offset, half_width + offset + values.shape[1], axis=1)

def tap_mask(segment_ids):
    half_width = KERNEL // 2
    padded = jnp.pad(segment_ids, ((0, 0), (half_width, half_width)), constant_values=-1)
    columns = [lax.slice_in_dim(padded, tap_index, tap_index + segment_ids.shape[1], axis=1) == segment_ids for tap_index in range(KERNEL)]
    return jnp.stack(columns, axis=-1).astype(jnp.float32)

def layer_norm(values, gain_vec, bias_vec):
    row_mean = lax.optimization_barrier(jnp.mean(values, axis=-1, keepdims=True))
    centered = values - row_mean
    variance = lax.optimization_barrier(jnp.mean(centered * centered, axis=-1, keepdims=True))
    return centered * lax.rsqrt(variance + norm_eps) * gain_vec + bias_vec

def forward(tokens, segment_ids, weights):
    w_proj, w_point, w_out, w_up, w_down, proj_bias, conv_depth, kernel_weight, kernel_bias, hidden_bias, up_bias, norm_gain = weights
    row_count, seq_length = segment_ids.shape
    half_width = KERNEL // 2
    tap_valid = tap_mask(segment_ids)
    inputs = low(tokens)
    projected = low_back(jnp.einsum('rsd,de->rse', inputs, low(w_proj), precision=precise))
    queries = low(projected[..., :ATT] + proj_bias[0])
    key_heads = low(projected[..., ATT:2 * ATT])
    value_heads = low(projected[..., 2 * ATT:3 * ATT] + proj_bias[1])
    conv_input = projected[..., 3 * ATT:] + proj_bias[2]
    depth_out = jnp.zeros_like(tokens)
    for tap_index in range(KERNEL):
        depth_out = depth_out + conv_depth[tap_index] * tap_valid[..., tap_index:tap_index + 1] * shifted(inputs, tap_index - half_width)
    key_conv = low_back(jnp.einsum('rsd,de->rse', low(depth_out), low(w_point), precision=precise)) + proj_bias[3]
    conv_attn = key_conv * queries
    kernel_logits = jnp.einsum('rse,ek->rsk', conv_attn, kernel_weight, precision=precise) + kernel_bias
    kernel_soft = jax.nn.softmax(kernel_logits.reshape(row_count, seq_length, HEADS, KERNEL), axis=-1)
    kernel_soft = kernel_soft * tap_valid[:, :, None, :]
    conv_heads = conv_input.reshape(row_count, seq_length, HEADS, HEAD_DIM)
    conv_out = jnp.zeros_like(conv_heads)
    for tap_index in range(KERNEL):
        conv_out = conv_out + kernel_soft[..., tap_index:tap_index + 1] * shifted(conv_heads, tap_index - half_width)
    head_shape = (row_count, seq_length, HEADS, HEAD_DIM)
    scores = low_back(HEAD_DIM ** (-0.5) * jnp.einsum('rthd,ruhd->rhtu', queries.reshape(head_shape), key_heads.reshape(head_shape), precision=precise))
    same_doc = segment_ids[:, None, :, None] == segment_ids[:, None, None, :]
    probs = jax.nn.softmax(jnp.where(same_doc, scores, masked_score), axis=-1)
    context = jnp.einsum('rhtu,ruhd->rthd', low(probs), value_heads.reshape(head_shape), precision=precise)
    mixed = low(low_back(jnp.concatenate([context.reshape(row_count, seq_length, ATT), conv_out.reshape(row_count, seq_length, ATT)], axis=-1)))
    attended = low_back(jnp.einsum('rse,ed->rsd', mixed, low(w_out), precision=precise)) + hidden_bias[0]
    first_norm = layer_norm(attended + tokens, norm_gain[0], hidden_bias[1])
    grouped_in = low(first_norm).reshape(row_count, seq_length, GROUPS, D // GROUPS)
    raised = low_back(jnp.einsum('rsgi,gij->rsgj', grouped_in, low(w_up), precision=precise)).reshape(row_count, seq_length, FF) + up_bias
    activated = low(jax.nn.gelu(raised, approximate=False)).reshape(row_count, seq_length, GROUPS, FF // GROUPS)
    lowered = low_back(jnp.einsum('rsgj,gji->rsgi', activated, low(w_down), precision=precise)).reshape(row_count, seq_length, D) + hidden_bias[2]
    return layer_norm(lowered + first_norm, norm_gain[1], hidden_bias[3])

def add_pair(first_total, second_total):
    return first_total + second_total

def reference(tokens, segment_ids, cotangent, w_proj, w_point, w_out, w_up, w_down, proj_bias, conv_depth, kernel_weight, kernel_bias, hidden_bias, up_bias, norm_gain):
    weights = (w_proj, w_point, w_out, w_up, w_down, proj_bias, conv_depth, kernel_weight, kernel_bias, hidden_bias, up_bias, norm_gain)
    group_rows = 8 if ROWS % 8 == 0 else 1
    group_count = ROWS // group_rows
    token_groups = tokens.astype(jnp.float32).reshape(group_count, group_rows, SEQ, D)
    id_groups = segment_ids.reshape(group_count, group_rows, SEQ)
    cot_groups = cotangent.astype(jnp.float32).reshape(group_count, group_rows, SEQ, D)

    def one_group(totals, group_inputs):
        group_tokens, group_ids, group_cot = group_inputs

        def apply_layer(values, params):
            return forward(values, group_ids, params)
        outputs, pullback = jax.vjp(apply_layer, group_tokens, weights)
        token_grad, weight_grads = pullback(group_cot)
        totals = jax.tree.map(add_pair, totals, weight_grads)
        return (totals, (outputs.astype(jnp.bfloat16), token_grad))
    grad_zeros = jax.tree.map(jnp.zeros_like, weights)
    totals, (layer_rows, token_grads) = lax.scan(one_group, grad_zeros, (token_groups, id_groups, cot_groups))
    return (layer_rows.reshape(ROWS, SEQ, D), token_grads.reshape(ROWS, SEQ, D), totals[0], totals[1], totals[2], totals[3], totals[4], totals[5], totals[6], totals[7], totals[8], totals[9], totals[10], totals[11])
```

```python
import functools
import jax
import jax.numpy as jnp
from jax import lax
from jax.sharding import PartitionSpec as P

D = 768
FF = 3072
HEADS = 6
HEAD_DIM = 64
KERNEL = 9
GROUPS = 2
ATT = 384

def digits(size):
    out, bit = [], 1
    while bit < size:
        ways = 4 if size // bit % 4 == 0 else 2
        out.append((bit, ways))
        bit *= ways
    return out

def send_xor(x, axis, size, step):
    return lax.ppermute(x, axis, [(i, i ^ step) for i in range(size)])

def gather_axis(x, axis, size):
    x = x[None]
    me = lax.axis_index(axis)
    for bit, ways in reversed(digits(size)):
        mine = (me // bit) % ways
        got = [x] + [send_xor(x, axis, size, d * bit) for d in range(1, ways)]
        parts = []
        for place in range(ways):
            rel = mine ^ place
            part = got[0]
            for d in range(1, ways):
                part = jnp.where(rel == d, got[d], part)
            parts.append(part)
        x = jnp.stack(parts, axis=1).reshape((x.shape[0] * ways,) + x.shape[1:])
    return x

def gather_all(x, sizes):
    nd, nf = sizes
    g = gather_axis(x, "dp", nd)
    g = gather_axis(g, "fsdp", nf)
    return jnp.swapaxes(g, 0, 1)

def scatter_axis(g, axis, size):
    me = lax.axis_index(axis)
    for bit, ways in digits(size):
        high = g.shape[0] // ways
        mine = (me // bit) % ways
        h = g.reshape((high, ways) + g.shape[1:])
        pick = lambda d: lax.dynamic_index_in_dim(h, mine ^ d, 1, keepdims=False)
        got = [send_xor(pick(d), axis, size, d * bit) for d in range(1, ways)]
        total = pick(0).astype(jnp.float32)
        for r in got:
            total = total + r.astype(jnp.float32)
        g = total.astype(jnp.bfloat16)
    return g[0]

def scatter_all(g, sizes):
    nd, nf = sizes
    g = scatter_axis(jnp.swapaxes(g, 0, 1), "fsdp", nf)
    return scatter_axis(g, "dp", nd)

def sum_axis(x, axis, size):
    for bit, ways in digits(size):
        got = [send_xor(x, axis, size, d * bit) for d in range(1, ways)]
        for r in got:
            x = x + r
    return x


precise = lax.Precision.HIGHEST
masked_score = -1000000000.0
norm_eps = 1e-12


def shifted(values, offset):
    half_width = KERNEL // 2
    widths = [(0, 0), (half_width, half_width)] + [(0, 0)] * (values.ndim - 2)
    padded = jnp.pad(values, widths)
    return lax.slice_in_dim(
        padded, half_width + offset, half_width + offset + values.shape[1], axis=1
    )


def tap_mask(segment_ids):
    half_width = KERNEL // 2
    padded = jnp.pad(segment_ids, ((0, 0), (half_width, half_width)), constant_values=-1)
    columns = [
        lax.slice_in_dim(padded, tap_index, tap_index + segment_ids.shape[1], axis=1) == segment_ids
        for tap_index in range(KERNEL)
    ]
    return jnp.stack(columns, axis=-1).astype(jnp.float32)


def norm_forward(values, gain_vec, bias_vec):
    row_mean = jnp.mean(values, axis=-1, keepdims=True)
    centered = values - row_mean
    variance = jnp.mean(centered * centered, axis=-1, keepdims=True)
    inv_std = lax.rsqrt(variance + norm_eps)
    normed = centered * inv_std
    return (normed * gain_vec + bias_vec, normed, inv_std)


def norm_backward(grad_out, normed, inv_std, gain_vec):
    grad_normed = grad_out * gain_vec
    grad_in = inv_std * (
        grad_normed
        - jnp.mean(grad_normed, axis=-1, keepdims=True)
        - normed * jnp.mean(grad_normed * normed, axis=-1, keepdims=True)
    )
    return (grad_in, jnp.sum(grad_out * normed, axis=(0, 1)), jnp.sum(grad_out, axis=(0, 1)))


def gelu_exact(values):
    return jax.nn.gelu(values, approximate=False)


def masked_scores(query_row, key_row, ids_row):
    scores = query_row.shape[-1] ** (-0.5) * jnp.einsum(
        "thd,uhd->htu", query_row, key_row, preferred_element_type=jnp.float32
    )
    same_doc = ids_row[:, None] == ids_row[None, :]
    return jnp.where(same_doc[None], scores, masked_score)


def attend_row(row_inputs):
    query_row, key_row, value_row, ids_row = row_inputs
    scores = masked_scores(query_row, key_row, ids_row)
    top_score = jnp.max(scores, axis=-1, keepdims=True)
    expo = jnp.exp(scores - top_score)
    total = jnp.sum(expo, axis=-1, keepdims=True)
    probs = expo / total
    context = jnp.einsum(
        "htu,uhd->thd", probs.astype(jnp.bfloat16), value_row, preferred_element_type=jnp.float32
    )
    return (context, (top_score + jnp.log(total))[..., 0])


def attend_back(row_inputs):
    query_row, key_row, value_row, ids_row, log_total, grad_context = row_inputs
    score_scale = query_row.shape[-1] ** (-0.5)
    probs = jnp.exp(masked_scores(query_row, key_row, ids_row) - log_total[..., None])
    grad_probs = jnp.einsum(
        "thd,uhd->htu", grad_context, value_row, preferred_element_type=jnp.float32
    )
    value_grad = jnp.einsum(
        "htu,thd->uhd", probs.astype(jnp.bfloat16), grad_context, preferred_element_type=jnp.float32
    )
    row_delta = jnp.sum(grad_probs * probs, axis=-1, keepdims=True)
    grad_scores = (probs * (grad_probs - row_delta)).astype(jnp.bfloat16)
    query_grad = score_scale * jnp.einsum(
        "htu,uhd->thd", grad_scores, key_row, preferred_element_type=jnp.float32
    )
    key_grad = score_scale * jnp.einsum(
        "htu,thd->uhd", grad_scores, query_row, preferred_element_type=jnp.float32
    )
    return (query_grad, key_grad, value_grad)


def body(
    tokens,
    segment_ids,
    cotangent,
    w_proj,
    w_point,
    w_out,
    w_up,
    w_down,
    proj_bias,
    conv_depth,
    kernel_weight,
    kernel_bias,
    hidden_bias,
    up_bias,
    norm_gain,
    *,
    sizes,
):
    row_count, seq_length = segment_ids.shape
    half_width = KERNEL // 2
    head_shape = (row_count, seq_length, HEADS, HEAD_DIM)
    group_in = (row_count, seq_length, GROUPS, D // GROUPS)
    group_mid = (row_count, seq_length, GROUPS, FF // GROUPS)
    bf16 = jnp.bfloat16
    first_shard = jnp.concatenate([w_proj, w_point], axis=1).astype(bf16)
    first_full = gather_all(first_shard, sizes).reshape(D, 5 * ATT)
    proj_full, point_full = first_full[:, : 4 * ATT], first_full[:, 4 * ATT :]
    out_full = gather_all(w_out.astype(bf16), sizes).reshape(D, D)
    ff_shard = jnp.concatenate([jnp.swapaxes(w_up, 1, 2), w_down], axis=2).astype(bf16)
    ff_full = gather_all(ff_shard, sizes)
    ff_full = ff_full.transpose(2, 0, 1, 3, 4).reshape(GROUPS, FF // GROUPS, D)
    up_full = jnp.swapaxes(ff_full[..., : D // GROUPS], 1, 2)
    down_full = ff_full[..., D // GROUPS :]
    tap_valid = tap_mask(segment_ids)
    inputs = tokens.astype(jnp.float32)
    projected = jnp.einsum("rsd,de->rse", tokens, proj_full, preferred_element_type=jnp.float32)
    queries = (projected[..., :ATT] + proj_bias[0]).astype(jnp.bfloat16)
    key_heads = projected[..., ATT : 2 * ATT].astype(jnp.bfloat16)
    value_heads = (projected[..., 2 * ATT : 3 * ATT] + proj_bias[1]).astype(jnp.bfloat16)
    conv_input = projected[..., 3 * ATT :] + proj_bias[2]
    depth_out = jnp.zeros_like(inputs)
    for tap_index in range(KERNEL):
        depth_out = depth_out + conv_depth[tap_index] * tap_valid[
            ..., tap_index : tap_index + 1
        ] * shifted(inputs, tap_index - half_width)
    depth_low = depth_out.astype(jnp.bfloat16)
    key_conv = (
        jnp.einsum("rsd,de->rse", depth_low, point_full, preferred_element_type=jnp.float32)
        + proj_bias[3]
    )
    query_float = queries.astype(jnp.float32)
    conv_attn = key_conv * query_float
    kernel_logits = (
        jnp.einsum("rse,ek->rsk", conv_attn, kernel_weight, precision=precise) + kernel_bias
    )
    kernel_soft = jax.nn.softmax(
        kernel_logits.reshape(row_count, seq_length, HEADS, KERNEL), axis=-1
    )
    kernel_masked = kernel_soft * tap_valid[:, :, None, :]
    conv_heads = conv_input.reshape(head_shape)
    conv_out = jnp.zeros_like(conv_heads)
    for tap_index in range(KERNEL):
        conv_out = conv_out + kernel_masked[..., tap_index : tap_index + 1] * shifted(
            conv_heads, tap_index - half_width
        )
    query_heads = queries.reshape(head_shape)
    key_split = key_heads.reshape(head_shape)
    value_split = value_heads.reshape(head_shape)
    context, log_totals = lax.map(attend_row, (query_heads, key_split, value_split, segment_ids))
    mixed = jnp.concatenate(
        [context.reshape(row_count, seq_length, ATT), conv_out.reshape(row_count, seq_length, ATT)],
        axis=-1,
    ).astype(jnp.bfloat16)
    attended = (
        jnp.einsum("rse,ed->rsd", mixed, out_full, preferred_element_type=jnp.float32)
        + hidden_bias[0]
    )
    first_norm, normed_one, inv_one = norm_forward(attended + inputs, norm_gain[0], hidden_bias[1])
    first_low = first_norm.astype(jnp.bfloat16).reshape(group_in)
    raised = (
        jnp.einsum(
            "rsgi,gij->rsgj", first_low, up_full, preferred_element_type=jnp.float32
        ).reshape(row_count, seq_length, FF)
        + up_bias
    )
    activated, gelu_pull = jax.vjp(gelu_exact, raised)
    act_low = activated.astype(jnp.bfloat16).reshape(group_mid)
    lowered = (
        jnp.einsum(
            "rsgj,gji->rsgi", act_low, down_full, preferred_element_type=jnp.float32
        ).reshape(row_count, seq_length, D)
        + hidden_bias[2]
    )
    layer_out, normed_two, inv_two = norm_forward(
        lowered + first_norm, norm_gain[1], hidden_bias[3]
    )
    proj_back, point_back, out_back, up_back, down_back = (
        proj_full, point_full, out_full, up_full, down_full
    )
    grad_two, gain_two, shift_two = norm_backward(
        cotangent.astype(jnp.float32), normed_two, inv_two, norm_gain[1]
    )
    grad_lowered = grad_two.astype(jnp.bfloat16).reshape(group_in)
    down_grad = jnp.einsum(
        "rsgj,rsgi->gji", act_low, grad_lowered, preferred_element_type=jnp.float32
    )
    grad_act = jnp.einsum(
        "rsgi,gji->rsgj", grad_lowered, down_back, preferred_element_type=jnp.float32
    ).reshape(row_count, seq_length, FF)
    grad_raised = gelu_pull(grad_act)[0]
    raised_low = grad_raised.astype(jnp.bfloat16).reshape(group_mid)
    up_grad = jnp.einsum(
        "rsgi,rsgj->gij", first_low, raised_low, preferred_element_type=jnp.float32
    )
    grad_first = (
        jnp.einsum(
            "rsgj,gij->rsgi", raised_low, up_back, preferred_element_type=jnp.float32
        ).reshape(row_count, seq_length, D)
        + grad_two
    )
    grad_one, gain_one, shift_one = norm_backward(grad_first, normed_one, inv_one, norm_gain[0])
    attended_low = grad_one.astype(jnp.bfloat16)
    out_grad = jnp.einsum("rse,rsd->ed", mixed, attended_low, preferred_element_type=jnp.float32)
    grad_mixed = jnp.einsum(
        "rsd,ed->rse", attended_low, out_back, preferred_element_type=jnp.float32
    ).astype(jnp.bfloat16)
    grad_context = grad_mixed[..., :ATT].reshape(head_shape)
    grad_conv = grad_mixed[..., ATT:].astype(jnp.float32).reshape(head_shape)
    kernel_columns = []
    grad_conv_input = jnp.zeros_like(conv_heads)
    for tap_index in range(KERNEL):
        offset = tap_index - half_width
        kernel_columns.append(jnp.sum(grad_conv * shifted(conv_heads, offset), axis=-1))
        grad_conv_input = grad_conv_input + shifted(
            kernel_masked[..., tap_index : tap_index + 1] * grad_conv, -offset
        )
    grad_kernel = jnp.stack(kernel_columns, axis=-1) * tap_valid[:, :, None, :]
    grad_logits = kernel_soft * (
        grad_kernel - jnp.sum(grad_kernel * kernel_soft, axis=-1, keepdims=True)
    )
    grad_logits = grad_logits.reshape(row_count, seq_length, HEADS * KERNEL)
    kernel_bias_grad = jnp.sum(grad_logits, axis=(0, 1))
    kernel_weight_grad = jnp.einsum("rse,rsk->ek", conv_attn, grad_logits, precision=precise)
    grad_attn = jnp.einsum("rsk,ek->rse", grad_logits, kernel_weight, precision=precise)
    grad_key_conv = grad_attn * query_float
    query_from_conv = grad_attn * key_conv
    key_conv_low = grad_key_conv.astype(jnp.bfloat16)
    point_grad = jnp.einsum(
        "rsd,rse->de", depth_low, key_conv_low, preferred_element_type=jnp.float32
    )
    grad_depth = jnp.einsum(
        "rse,de->rsd", key_conv_low, point_back, preferred_element_type=jnp.float32
    )
    depth_rows = []
    tokens_grad = grad_one
    for tap_index in range(KERNEL):
        offset = tap_index - half_width
        tap_column = tap_valid[..., tap_index : tap_index + 1]
        depth_rows.append(jnp.sum(tap_column * shifted(inputs, offset) * grad_depth, axis=(0, 1)))
        tokens_grad = tokens_grad + shifted(
            conv_depth[tap_index] * tap_column * grad_depth, -offset
        )
    conv_depth_grad = jnp.stack(depth_rows, axis=0)
    query_att, key_att, value_att = lax.map(
        attend_back, (query_heads, key_split, value_split, segment_ids, log_totals, grad_context)
    )
    grad_queries = query_att.reshape(row_count, seq_length, ATT) + query_from_conv
    value_flat = value_att.reshape(row_count, seq_length, ATT)
    conv_input_flat = grad_conv_input.reshape(row_count, seq_length, ATT)
    grad_proj = jnp.concatenate(
        [grad_queries, key_att.reshape(row_count, seq_length, ATT), value_flat, conv_input_flat],
        axis=-1,
    )
    proj_bias_grad = jnp.stack(
        [
            jnp.sum(grad_queries, axis=(0, 1)),
            jnp.sum(value_flat, axis=(0, 1)),
            jnp.sum(conv_input_flat, axis=(0, 1)),
            jnp.sum(grad_key_conv, axis=(0, 1)),
        ],
        axis=0,
    )
    proj_low = grad_proj.astype(jnp.bfloat16)
    proj_grad = jnp.einsum("rsd,rse->de", tokens, proj_low, preferred_element_type=jnp.float32)
    tokens_grad = tokens_grad + jnp.einsum(
        "rse,de->rsd", proj_low, proj_back, preferred_element_type=jnp.float32
    )
    hidden_bias_grad = jnp.stack(
        [jnp.sum(grad_one, axis=(0, 1)), shift_one, jnp.sum(grad_two, axis=(0, 1)), shift_two],
        axis=0,
    )
    up_bias_grad = jnp.sum(grad_raised, axis=(0, 1))
    norm_gain_grad = jnp.stack([gain_one, gain_two], axis=0)
    nd, nf = sizes
    shard_rows, ff_rows = D // (nd * nf), FF // GROUPS // (nd * nf)
    ff_grad = jnp.concatenate([jnp.swapaxes(up_grad, 1, 2), down_grad], axis=2).astype(bf16)
    ff_grad = ff_grad.reshape(GROUPS, nd, nf, ff_rows, D).transpose(1, 2, 0, 3, 4)
    ff_share = scatter_all(ff_grad, sizes).astype(jnp.float32)
    out_share = scatter_all(out_grad.astype(bf16).reshape(nd, nf, shard_rows, D), sizes)
    first_grad = jnp.concatenate([proj_grad, point_grad], axis=1).astype(bf16)
    first_share = scatter_all(first_grad.reshape(nd, nf, shard_rows, 5 * ATT), sizes)
    first_share = first_share.astype(jnp.float32)
    matrix_shares = (
        first_share[:, : 4 * ATT],
        first_share[:, 4 * ATT :],
        out_share.astype(jnp.float32),
        jnp.swapaxes(ff_share[..., : D // GROUPS], 1, 2),
        ff_share[..., D // GROUPS :],
    )
    smalls = (
        proj_bias_grad,
        conv_depth_grad,
        kernel_weight_grad,
        kernel_bias_grad,
        hidden_bias_grad,
        up_bias_grad,
        norm_gain_grad,
    )
    flat = jnp.concatenate([small.reshape(-1) for small in smalls])
    padded = -flat.size % 1024
    flat = jnp.pad(flat, (0, padded)).reshape(-1, 128)
    flat = sum_axis(sum_axis(flat, "fsdp", nf), "dp", nd).reshape(-1)
    small_sums, at = [], 0
    for small in smalls:
        small_sums.append(flat[at : at + small.size].reshape(small.shape))
        at += small.size
    return (
        layer_out.astype(jnp.bfloat16),
        tokens_grad,
        matrix_shares[0],
        matrix_shares[1],
        matrix_shares[2],
        matrix_shares[3],
        matrix_shares[4],
        small_sums[0],
        small_sums[1],
        small_sums[2],
        small_sums[3],
        small_sums[4],
        small_sums[5],
        small_sums[6],
    )


def solution(mesh):
    placed = (
        P(("dp", "fsdp"), None, None),
        P(("dp", "fsdp"), None),
        P(("dp", "fsdp"), None, None),
        P(("dp", "fsdp"), None),
        P(("dp", "fsdp"), None),
        P(("dp", "fsdp"), None),
        P(None, None, ("dp", "fsdp")),
        P(None, ("dp", "fsdp"), None),
        P(),
        P(),
        P(),
        P(),
        P(),
        P(),
        P(),
    )
    return jax.shard_map(
        functools.partial(body, sizes=(mesh.shape["dp"], mesh.shape["fsdp"])),
        mesh=mesh,
        in_specs=placed,
        out_specs=(
            P(("dp", "fsdp"), None, None),
            P(("dp", "fsdp"), None, None),
            P(("dp", "fsdp"), None),
            P(("dp", "fsdp"), None),
            P(("dp", "fsdp"), None),
            P(None, None, ("dp", "fsdp")),
            P(None, ("dp", "fsdp"), None),
            P(),
            P(),
            P(),
            P(),
            P(),
            P(),
            P(),
        ),
        check_vma=False,
    )
```

```python
import functools

import jax
import jax.numpy as jnp
from jax import lax
from jax.experimental import pallas as pl
from jax.experimental.pallas import tpu as pltpu
from jax.sharding import PartitionSpec as P

f32=jnp.float32
bf16=jnp.bfloat16
D=768; FF=3072; HEADS=6; HEAD_DIM=64; KERNEL=9; GROUPS=2; ATT=384
norm_eps=1e-12
def dot(a,b): return lax.dot_general(a,b,(((1,),(0,)),((),())),preferred_element_type=f32)
def dot_t(a,b): return lax.dot_general(a,b,(((1,),(1,)),((),())),preferred_element_type=f32)
def dot_l(a,b): return lax.dot_general(a,b,(((0,),(0,)),((),())),preferred_element_type=f32)
def fold8(x):
    return jnp.sum(x.reshape(x.shape[0]//8,8,x.shape[1]),axis=0)
def row_mean(x): return jnp.sum(x,axis=-1,keepdims=True)*(1.0/x.shape[-1])

def ordered(kernel,lead,after):
    extra=len(after)
    return lambda *refs: kernel(*refs[:lead],*refs[lead+extra:])
def waits(after):
    return [pl.BlockSpec(memory_space=pl.ANY) for _ in after]

def gelu_parts(x):
    e=jnp.exp(x*x*-0.5)
    t=1.0/(1.0+jnp.abs(x)*0.231641888)
    poly=t*(0.127414796+t*(-0.142248368+t*(0.7107068705+t*(-0.7265760135+t*0.5307027145))))
    tail=poly*e
    phi=jnp.where(x>=0,1.0-tail,tail)
    return x*phi, phi+x*(e*0.3989422804014327)

CH=256
COPY=384
def hidden(w_ref,rows,g,c,lanes):
    if rows>=COPY:
        return w_ref[c//rows,g*rows+c%rows:g*rows+c%rows+COPY,lanes]
    return w_ref[c//rows:(c+COPY)//rows,g*rows:(g+1)*rows,lanes].reshape(COPY,D//GROUPS)

def ff_kernel(rows,mixed_ref,tok_ref,cot_ref,wout_ref,wff_ref,hb_ref,ub_ref,gain_ref,
              out_ref,gone_ref,gmix_ref,act_ref,gr_ref,xlow_ref,g2low_ref,g1low_ref,sums_ref,ups_ref,dg_ref,wup_ref,wdn_ref):
    half=D//GROUPS; mid=FF//GROUPS
    @pl.when(pl.program_id(0)==0)
    def _():
        sums_ref[...]=jnp.zeros_like(sums_ref); ups_ref[...]=jnp.zeros_like(ups_ref)
        for g in range(GROUPS):
            for c in range(0,mid,COPY):
                wup_ref[g,c:c+COPY,:]=hidden(wff_ref,rows,g,c,slice(0,half))
                wdn_ref[g,c:c+COPY,:]=hidden(wff_ref,rows,g,c,slice(half,D))
    res=dot(mixed_ref[...],wout_ref[...])+hb_ref[0:1,:]+tok_ref[...].astype(f32)
    mean=row_mean(res); cen=res-mean
    inv1=lax.rsqrt(row_mean(cen*cen)+norm_eps)
    n1=cen*inv1
    first=n1*gain_ref[0:1,:]+hb_ref[1:2,:]
    xlow=first.astype(bf16)
    xlow_ref[...]=xlow
    lows=[]
    spans=[(g,c,slice(g*mid+c,g*mid+c+CH)) for g in range(GROUPS) for c in range(0,mid,CH)]
    def raise_(g,c,cs):
        return dot_t(xlow_ref[:,g*half:(g+1)*half],wup_ref[g,c:c+CH,:])+ub_ref[0:1,cs]
    ahead=raise_(*spans[0])
    for i,(g,c,cs) in enumerate(spans):
        raised=ahead
        if i+1<len(spans): ahead=raise_(*spans[i+1])
        a,dg=gelu_parts(raised)
        act_ref[:,cs]=a.astype(bf16)
        dg_ref[:,cs]=dg
        if c+CH==mid:
            lows.append(dot(act_ref[:,g*mid:(g+1)*mid],wdn_ref[g]))
    res=jnp.concatenate(lows,axis=1)+hb_ref[2:3,:]+first
    mean=row_mean(res); cen=res-mean
    inv2=lax.rsqrt(row_mean(cen*cen)+norm_eps)
    n2=cen*inv2
    gain2=gain_ref[1:2,:]
    out_ref[...]=(n2*gain2+hb_ref[3:4,:]).astype(bf16)
    e=cot_ref[...].astype(f32)
    eg=e*gain2
    g2=inv2*(eg-row_mean(eg)-n2*row_mean(eg*n2))
    sums_ref[3]+=fold8(e); sums_ref[5]+=fold8(e*n2); sums_ref[2]+=fold8(g2)
    g2low_ref[...]=g2.astype(bf16)
    parts=[]
    def lower_(g,c,cs):
        return dot_t(g2low_ref[:,g*half:(g+1)*half],wdn_ref[g,c:c+CH,:])
    ahead=lower_(*spans[0])
    for i,(g,c,cs) in enumerate(spans):
        ga=ahead
        if i+1<len(spans): ahead=lower_(*spans[i+1])
        gr=ga*dg_ref[:,cs]
        ups_ref[:,cs]+=fold8(gr)
        gr_ref[:,cs]=gr.astype(bf16)
        if c+CH==mid:
            parts.append(dot(gr_ref[:,g*mid:(g+1)*mid],wup_ref[g]))
    gf=jnp.concatenate(parts,axis=1)+g2
    sums_ref[1]+=fold8(gf); sums_ref[4]+=fold8(gf*n1)
    eg=gf*gain_ref[0:1,:]
    g1=inv1*(eg-row_mean(eg)-n1*row_mean(eg*n1))
    sums_ref[0]+=fold8(g1)
    gone_ref[...]=g1
    g1low_ref[...]=g1.astype(bf16)
    gmix_ref[...]=dot_t(g1low_ref[...],wout_ref[...]).astype(bf16)

def ff_call(mixed,tok,cot,wout,wff,hb,ub,gain,T=256,after=()):
    n=tok.shape[0]
    rows=FF//GROUPS//wff.shape[0]
    row=lambda w,:pl.BlockSpec((T,w),lambda i:(i,0))
    full=lambda s:pl.BlockSpec(s,lambda i:(0,)*len(s),pipeline_mode=pl.Buffered(1))
    S=lambda s,d:jax.ShapeDtypeStruct(s,d)
    W=(GROUPS,FF//GROUPS,D//GROUPS)
    return pl.pallas_call(ordered(functools.partial(ff_kernel,rows),8,after),grid=(n//T,),
        in_specs=[row(D),row(D),row(D),full((D,D)),full(wff.shape),full((4,D)),full((1,FF)),full((2,D))]+waits(after),
        out_specs=[row(D),row(D),row(D),row(FF),row(FF),row(D),row(D),row(D),full((6,8,D)),full((8,FF))],
        out_shape=[S((n,D),bf16),S((n,D),f32),S((n,D),bf16),S((n,FF),bf16),S((n,FF),bf16),S((n,D),bf16),S((n,D),bf16),S((n,D),bf16),S((6,8,D),f32),S((8,FF),f32)],
        scratch_shapes=[pltpu.VMEM((T,FF),f32),pltpu.VMEM(W,bf16),pltpu.VMEM(W,bf16)],
        compiler_params=pltpu.CompilerParams(vmem_limit_bytes=60<<20),
        cost_estimate=pl.CostEstimate(flops=2*n*(2*D*D+4*FF*D//GROUPS),bytes_accessed=n*FF*4+n*D*20,transcendentals=n*FF*2),
        name="feed_forward",
    )(mixed,tok,cot,wout,wff,hb,ub,gain,*after)

def ffw_kernel(act_ref,gr_ref,xlow_ref,g2low_ref,out_ref):
    half=D//GROUPS
    blocks,rows=out_ref.shape[0:2]
    out_ref[:,:,0:half]=dot_l(xlow_ref[...],gr_ref[...]).T.astype(bf16).reshape(blocks,rows,half)
    out_ref[:,:,half:]=dot_l(g2low_ref[...],act_ref[...]).T.astype(bf16).reshape(blocks,rows,half)
def ffw_call(act,gr,xlow,g2low,blocks,C=768,after=()):
    n=act.shape[0]; half=D//GROUPS; mid=FF//GROUPS; per=mid//C
    rows=mid//blocks
    if rows>=C:
        out=pl.BlockSpec((1,C,D),lambda g,c:(0,g*per+c,0))
    else:
        out=pl.BlockSpec((C//rows,rows,D),lambda g,c:(c,g,0))
    return pl.pallas_call(ordered(ffw_kernel,4,after),grid=(GROUPS,per),
        in_specs=[pl.BlockSpec((n,C),lambda g,c:(0,g*per+c))]*2+[pl.BlockSpec((n,half),lambda g,c:(0,g))]*2+waits(after),
        out_specs=out,
        out_shape=jax.ShapeDtypeStruct((blocks,GROUPS*rows,D),bf16),
        compiler_params=pltpu.CompilerParams(vmem_limit_bytes=60<<20),
        cost_estimate=pl.CostEstimate(flops=2*n*2*FF*half,bytes_accessed=n*FF*4+n*D*4+FF*D*2,transcendentals=0),
        name="feed_forward_weights",
    )(act,gr,xlow,g2low,*after)
def wg_kernel(a_ref,b_ref,out_ref):
    out_ref[...]=dot_l(a_ref[...],b_ref[...]).astype(bf16)
def wg_call(a,b,C=384,after=()):
    n,k=a.shape; m=b.shape[1]
    return pl.pallas_call(ordered(wg_kernel,2,after),grid=(m//C,),
        in_specs=[pl.BlockSpec((n,k),lambda c:(0,0)),pl.BlockSpec((n,C),lambda c:(0,c))]+waits(after),
        out_specs=pl.BlockSpec((k,C),lambda c:(0,c)),
        out_shape=jax.ShapeDtypeStruct((k,m),bf16),
        compiler_params=pltpu.CompilerParams(vmem_limit_bytes=60<<20),
        cost_estimate=pl.CostEstimate(flops=2*n*k*m,bytes_accessed=2*(n*k+n*m+k*m),transcendentals=0),
        name="weight_grad",
    )(a,b,*after)


TAPS=16
LANES=HEADS*TAPS
BT=64
LEAD=16
SLOT=4
HALF=256
SEQ=512
NEG=-1000000000.0

def doc_of(pos,b_ref):
    row=pl.program_id(0)
    return ((pos>=b_ref[row,0]).astype(jnp.int32)+(pos>=b_ref[row,1]).astype(jnp.int32)+(pos>=b_ref[row,2]).astype(jnp.int32))
def tap_valid_t(b_ref):
    tap=lax.broadcasted_iota(jnp.int32,(TAPS,SEQ),0); t=lax.broadcasted_iota(jnp.int32,(TAPS,SEQ),1)
    u=t+tap-KERNEL//2-SLOT
    ok=(u>=0)&(u<SEQ)&(doc_of(u,b_ref)==doc_of(t,b_ref))&(tap>=SLOT)&(tap<SLOT+KERNEL)
    return ok.astype(f32)
def roll_matrix(b_ref,back):
    start=b_ref[pl.program_id(0),3]
    a=lax.broadcasted_iota(jnp.int32,(SEQ,SEQ),1 if back else 0); t=lax.broadcasted_iota(jnp.int32,(SEQ,SEQ),0 if back else 1)
    d=a+start-t
    return jnp.where((d==0)|(d==SEQ),1.0,0.0).astype(bf16)
def head_lanes(shape,h):
    lane=lax.broadcasted_iota(jnp.int32,shape,len(shape)-1)
    return (lane<HEAD_DIM) if h==0 else (lane>=HEAD_DIM)
def keep_head(x,h):
    return jnp.where(head_lanes(x.shape,h),x,jnp.zeros_like(x))

BAND=128
def tap_bands(b_ref,r):
    lo=min(max(r-BAND//2,0),SEQ-2*BAND)
    row=lax.broadcasted_iota(jnp.int32,(BAND,2*BAND),0)+r; col=lax.broadcasted_iota(jnp.int32,(BAND,2*BAND),1)+lo
    step=jnp.where(doc_of(row,b_ref)==doc_of(col,b_ref),col-row,SEQ)
    return lo,[jnp.where(step==j-KERNEL//2,1.0,0.0).astype(bf16) for j in range(KERNEL)]

def depth_kernel(b_ref,tok_ref,cd_ref,out_ref):
    for r in range(0,SEQ,BAND):
        lo,bands=tap_bands(b_ref,r)
        x=tok_ref[lo:lo+2*BAND,:]
        acc=None
        for j in range(KERNEL):
            v=dot(bands[j],x)*cd_ref[j:j+1,:]
            acc=v if acc is None else acc+v
        out_ref[r:r+BAND,:]=acc.astype(bf16)

def depth_call(bounds,tok,cd,after=()):
    n=tok.shape[0]
    return pl.pallas_call(ordered(depth_kernel,3,after),
        grid_spec=pltpu.PrefetchScalarGridSpec(num_scalar_prefetch=1,grid=(n//SEQ,),
        in_specs=[pl.BlockSpec((SEQ,D),lambda i,b:(i,0)),pl.BlockSpec((KERNEL,D),lambda i,b:(0,0))]+waits(after),
        out_specs=pl.BlockSpec((SEQ,D),lambda i,b:(i,0)),
        ),
        out_shape=jax.ShapeDtypeStruct((n,D),bf16),
        compiler_params=pltpu.CompilerParams(vmem_limit_bytes=60<<20),
        cost_estimate=pl.CostEstimate(flops=2*n*D*9*256,bytes_accessed=n*D*4,transcendentals=0),
        name="depth_taps")(bounds,tok,cd,*after)


def mix_kernel(b_ref,tok_ref,dep_ref,w_ref,pb_ref,kw_ref,kb_ref,
               mixed_ref,qkv_ref,e_ref,r_ref,ctx_ref,q_ref,kc_ref,ks_ref,band_ref,cin_ref):
    tok=tok_ref[...]
    p=dot(tok,w_ref[:,0:4*ATT])
    q=(p[:,0:ATT]+pb_ref[0:1,:]).astype(bf16)
    k=p[:,ATT:2*ATT].astype(bf16)
    v=(p[:,2*ATT:3*ATT]+pb_ref[1:2,:]).astype(bf16)
    cin=(p[:,3*ATT:]+pb_ref[2:3,:]).astype(bf16)
    q_ref[...]=q
    rolled=dot(roll_matrix(b_ref,False),jnp.concatenate([q*jnp.bfloat16(0.125),k,v],axis=1)).astype(bf16)
    qkv_ref[...]=rolled
    key_conv=dot(dep_ref[...],w_ref[:,4*ATT:])+pb_ref[3:4,:]
    kc_ref[...]=key_conv
    attn=key_conv*q.astype(f32)
    hi=attn.astype(bf16); lo=(attn-hi.astype(f32)).astype(bf16)
    both=dot_t(kw_ref[...],hi)
    logits=both[:LANES]+both[LANES:]+dot_t(kw_ref[0:LANES,:],lo)+kb_ref[...]
    logits=logits.reshape(HEADS,TAPS,SEQ)
    tap=lax.broadcasted_iota(jnp.int32,(HEADS,TAPS,SEQ),1)
    logits=jnp.where((tap>=SLOT)&(tap<SLOT+KERNEL),logits,-1e30)
    ex=jnp.exp(logits-jnp.max(logits,axis=1,keepdims=True))
    ks=ex/jnp.sum(ex,axis=1,keepdims=True)
    ks_ref[...]=ks.reshape(LANES,SEQ)
    km=(ks*tap_valid_t(b_ref)[None]).reshape(LANES,SEQ)
    km=jnp.concatenate([km,jnp.zeros((128-LANES,SEQ),f32)],axis=0).T
    cin_ref[0:LEAD,:]=jnp.zeros((LEAD,ATT),bf16); cin_ref[LEAD+SEQ:,:]=jnp.zeros((128-LEAD-BT,ATT),bf16)
    cin_ref[LEAD:LEAD+SEQ,:]=cin
    row=lax.broadcasted_iota(jnp.int32,(BT,128),0); lane=lax.broadcasted_iota(jnp.int32,(BT,128),1)
    off=lane-row-(LEAD-KERNEL//2)
    on_band=(off>=0)&(off<KERNEL)
    for i in range(SEQ//BT):
        kmi=km[i*BT:(i+1)*BT,:]
        bands=[]
        for h in range(HEADS):
            x=pltpu.roll(kmi,(LEAD-KERNEL//2-SLOT-h*TAPS)%128,1,stride=1,stride_axis=0)
            x=jnp.where(on_band,x,0.0).astype(bf16)
            band_ref[i,h]=x
            bands.append(x)
        for pr in range(HEADS//2):
            win=cin_ref[i*BT:i*BT+128,pr*128:(pr+1)*128]
            o=dot(jnp.concatenate(bands[2*pr:2*pr+2],axis=1),jnp.concatenate([keep_head(win,0),keep_head(win,1)],axis=0))
            mixed_ref[i*BT:(i+1)*BT,ATT+pr*128:ATT+(pr+1)*128]=o.astype(bf16)
    start=b_ref[pl.program_id(0),3]
    def rolled_doc(axis):
        t=lax.broadcasted_iota(jnp.int32,(HALF,HALF),axis)+start+HALF
        return doc_of(jnp.where(t>=SEQ,t-SEQ,t),b_ref)
    same=rolled_doc(0)==rolled_doc(1)
    ones=jnp.ones((HALF,128),bf16)
    for a in range(2):
        rs=slice(a*HALF,(a+1)*HALF)
        for pr in range(HEADS//2):
            Q=rolled[rs,pr*128:(pr+1)*128]; K=rolled[rs,ATT+pr*128:ATT+(pr+1)*128]; V=rolled[rs,2*ATT+pr*128:2*ATT+(pr+1)*128]
            es=[];vs=[]
            for h in range(2):
                s=dot_t(Q,keep_head(K,h))
                if a==1: s=jnp.where(same,s,NEG)
                e=jnp.exp(s-jnp.max(s,axis=-1,keepdims=True)).astype(bf16)
                e_ref[a,2*pr+h]=e
                es.append(e); vs.append(jnp.concatenate([keep_head(V,h),keep_head(ones,h)],axis=1))
            o=dot(jnp.concatenate(es,axis=1),jnp.concatenate(vs,axis=0))
            r=1.0/o[:,128:]
            r_ref[rs,pr*128:(pr+1)*128]=r
            ctx_ref[rs,pr*128:(pr+1)*128]=(o[:,:128]*r).astype(bf16)
    mixed_ref[:,0:ATT]=dot(roll_matrix(b_ref,True),ctx_ref[...]).astype(bf16)

CPAD=SEQ+128-BT
def mix_call(bounds,tok,dep,w,pb,kw,kb,after=()):
    n=tok.shape[0]; R=n//SEQ
    row=lambda w_:pl.BlockSpec((SEQ,w_),lambda i,b:(i,0))
    full=lambda s:pl.BlockSpec(s,lambda i,b:(0,)*len(s))
    lead=lambda s:pl.BlockSpec((None,)+s,lambda i,b:(i,)+(0,)*len(s))
    S=lambda s,d:jax.ShapeDtypeStruct(s,d)
    NT=SEQ//BT
    return pl.pallas_call(ordered(mix_kernel,7,after),
        grid_spec=pltpu.PrefetchScalarGridSpec(num_scalar_prefetch=1,grid=(R,),
        in_specs=[row(D),row(D),full((D,5*ATT)),full((4,ATT)),full((2*LANES,ATT)),full((LANES,1))]+waits(after),
        out_specs=[row(D),row(3*ATT),lead((2,HEADS,HALF,HALF)),row(ATT),row(ATT),row(ATT),row(ATT),lead((LANES,SEQ)),lead((NT,HEADS,BT,128)),lead((CPAD,ATT))]),
        out_shape=[S((n,D),bf16),S((n,3*ATT),bf16),S((R,2,HEADS,HALF,HALF),bf16),S((n,ATT),f32),S((n,ATT),bf16),S((n,ATT),bf16),S((n,ATT),f32),S((R,LANES,SEQ),f32),S((R,NT,HEADS,BT,128),bf16),S((R,CPAD,ATT),bf16)],
        compiler_params=pltpu.CompilerParams(vmem_limit_bytes=60<<20),
        cost_estimate=pl.CostEstimate(flops=2*n*(D*5*ATT+SEQ*4*ATT+HEADS*HALF*256),bytes_accessed=n*20000,transcendentals=n*HEADS*HALF),
        name="attend_and_span")(bounds,tok,dep,w,pb,kw,kb,*after)


def pack_kernel_weight(kw,kb):
    k=kw.T.reshape(HEADS,KERNEL,ATT)
    k=jnp.pad(k,((0,0),(SLOT,TAPS-KERNEL-SLOT),(0,0))).reshape(LANES,ATT)
    hi=lax.reduce_precision(k,8,7); lo=(k-hi).astype(bf16); hi=hi.astype(bf16)
    b=jnp.pad(kb.reshape(HEADS,KERNEL),((0,0),(SLOT,TAPS-KERNEL-SLOT))).reshape(LANES,1)
    return jnp.concatenate([hi,lo],axis=0),b

def find_bounds(seg):
    counts=jnp.stack([jnp.sum(seg==i,axis=1) for i in range(4)],axis=1)
    begin=jnp.cumsum(counts,axis=1)-counts
    which=jnp.argmax(counts==HALF,axis=1)
    start=jnp.take_along_axis(begin,which[:,None],axis=1)
    return jnp.concatenate([begin[:,1:],start],axis=1).astype(jnp.int32)

def back_kernel(b_ref,gm_ref,qkv_ref,e_ref,r_ref,ctx_ref,q_ref,kc_ref,ks_ref,band_ref,cin_ref,kwt_ref,
                gp_ref,gk_ref,kwg_ref,kbg_ref,pbg_ref,gcin_ref,dr_ref):
    @pl.when(pl.program_id(0)==0)
    def _():
        kwg_ref[...]=jnp.zeros_like(kwg_ref); kbg_ref[...]=jnp.zeros_like(kbg_ref); pbg_ref[...]=jnp.zeros_like(pbg_ref)
    gcin_ref[...]=jnp.zeros_like(gcin_ref)
    lane=lax.broadcasted_iota(jnp.int32,(BT,128),1)
    anti=lax.broadcasted_iota(jnp.int32,(SEQ,SEQ),0)+lax.broadcasted_iota(jnp.int32,(SEQ,SEQ),1)
    anti=jnp.where(anti==SEQ-1,1.0,0.0).astype(bf16)
    falling=dot(anti,gm_ref[:,ATT:]).astype(bf16)
    logits=[]
    for i in range(SEQ//BT):
        acc=None
        f=SEQ//BT-1-i
        for pr in range(HEADS//2):
            g=gm_ref[i*BT:(i+1)*BT,ATT+pr*128:ATT+(pr+1)*128]
            gf=falling[i*BT:(i+1)*BT,pr*128:(pr+1)*128]
            win=cin_ref[f*BT:f*BT+128,pr*128:(pr+1)*128]
            back=None
            for h in range(2):
                head=2*pr+h
                d=dot_t(keep_head(gf,h),win)
                d=pltpu.roll(d,(head*TAPS+SLOT-LEAD+KERNEL//2-BT+1)%128,1,stride=1,stride_axis=0)
                d=jnp.where((lane>=head*TAPS+SLOT)&(lane<head*TAPS+SLOT+KERNEL),d,0.0)
                acc=d if acc is None else acc+d
                p=dot_l(band_ref[i,head],keep_head(g,h))
                back=p if back is None else back+p
            gcin_ref[i*BT:i*BT+128,pr*128:(pr+1)*128]+=back
        logits.append(acc)
    gk=jnp.concatenate(logits,axis=0)
    gh=gk.astype(bf16); glo=(gk-gh.astype(f32)).astype(bf16)
    gk=(dot_l(gh,anti)+dot_l(glo,anti))[0:LANES,:].reshape(HEADS,TAPS,SEQ)*tap_valid_t(b_ref)[None]
    ks=ks_ref[...].reshape(HEADS,TAPS,SEQ)
    gl=(ks*(gk-jnp.sum(gk*ks,axis=1,keepdims=True))).reshape(LANES,SEQ)
    kbg_ref[...]+=gl[:,0:128]+gl[:,128:256]+gl[:,256:384]+gl[:,384:512]
    q=q_ref[...].astype(f32); kc=kc_ref[...]
    attn=kc*q
    hi=attn.astype(bf16)
    glb=gl.astype(bf16)
    kwg_ref[...]+=dot(glb,hi)
    gattn=dot_l(glb,kwt_ref[...])
    gkc=gattn*q
    gk_ref[...]=gkc.astype(bf16)
    pbg_ref[3]+=fold8(gkc)
    gci=gcin_ref[LEAD:LEAD+SEQ,:]
    pbg_ref[2]+=fold8(gci)
    gp_ref[:,3*ATT:]=gci.astype(bf16)
    dor=(dot(roll_matrix(b_ref,False),gm_ref[:,0:ATT])*r_ref[...])
    dol=dor.astype(bf16)
    prod=dol.astype(f32)*ctx_ref[...].astype(f32)
    ph=prod.astype(bf16); plo=(prod-ph.astype(f32)).astype(bf16)
    si=lax.broadcasted_iota(jnp.int32,(128,256),0)//HEAD_DIM; sj=lax.broadcasted_iota(jnp.int32,(128,256),1)//128
    pick=jnp.where(si==sj,1.0,0.0).astype(bf16)
    for a in range(2):
        rs=slice(a*HALF,(a+1)*HALF)
        for pr in range(HEADS//2):
            cs=slice(pr*128,(pr+1)*128)
            Q=qkv_ref[rs,pr*128:(pr+1)*128]; K=qkv_ref[rs,ATT+pr*128:ATT+(pr+1)*128]; V=qkv_ref[rs,2*ATT+pr*128:2*ATT+(pr+1)*128]
            delta=dot(ph[rs,cs],pick)+dot(plo[rs,cs],pick)
            G=dol[rs,cs]
            es=[e_ref[a,2*pr+h] for h in range(2)]
            ds=[]
            for h in range(2):
                dp=dot_t(G,keep_head(V,h))
                dl=delta[:,h*128:(h+1)*128]
                ds.append((es[h].astype(f32)*(dp-jnp.concatenate([dl,dl],axis=1))).astype(bf16))
            st=lambda x:jnp.concatenate([keep_head(x,0),keep_head(x,1)],axis=0)
            dq=dot(jnp.concatenate(ds,axis=1),st(K))*0.125
            dk=dot_l(jnp.concatenate(ds,axis=0),st(Q))
            dv=dot_l(jnp.concatenate(es,axis=0),st(G))
            dr_ref[rs,cs]=dq.astype(bf16)
            dr_ref[rs,ATT+pr*128:ATT+(pr+1)*128]=dk.astype(bf16)
            dr_ref[rs,2*ATT+pr*128:2*ATT+(pr+1)*128]=dv.astype(bf16)
    un=dot(roll_matrix(b_ref,True),dr_ref[...])
    gq=un[:,0:ATT]+gattn*kc
    pbg_ref[0]+=fold8(gq); pbg_ref[1]+=fold8(un[:,2*ATT:])
    gp_ref[:,0:ATT]=gq.astype(bf16)
    gp_ref[:,ATT:3*ATT]=un[:,ATT:].astype(bf16)

def back_call(bounds,gm,qkv,E,r,ctx,q,kc,ks,band,cin,kwt,after=()):
    n=gm.shape[0]; R=n//SEQ; NT=SEQ//BT
    row=lambda w_:pl.BlockSpec((SEQ,w_),lambda i,b:(i,0))
    full=lambda s:pl.BlockSpec(s,lambda i,b:(0,)*len(s))
    lead=lambda s:pl.BlockSpec((None,)+s,lambda i,b:(i,)+(0,)*len(s))
    S=lambda s,d:jax.ShapeDtypeStruct(s,d)
    return pl.pallas_call(ordered(back_kernel,12,after),
        grid_spec=pltpu.PrefetchScalarGridSpec(num_scalar_prefetch=1,grid=(R,),
        in_specs=[row(D),row(3*ATT),lead((2,HEADS,HALF,HALF)),row(ATT),row(ATT),row(ATT),row(ATT),lead((LANES,SEQ)),lead((NT,HEADS,BT,128)),lead((CPAD,ATT)),full((LANES,ATT))]+waits(after),
        out_specs=[row(4*ATT),row(ATT),full((LANES,ATT)),full((LANES,128)),full((4,8,ATT))],
        scratch_shapes=[pltpu.VMEM((CPAD,ATT),f32),pltpu.VMEM((SEQ,3*ATT),bf16)]),
        out_shape=[S((n,4*ATT),bf16),S((n,ATT),bf16),S((LANES,ATT),f32),S((LANES,128),f32),S((4,8,ATT),f32)],
        compiler_params=pltpu.CompilerParams(vmem_limit_bytes=60<<20),
        cost_estimate=pl.CostEstimate(flops=2*n*(SEQ*4*ATT+HEADS*HALF*1000),bytes_accessed=n*20000,transcendentals=0),
        name="attend_and_span_back")(bounds,gm,qkv,E,r,ctx,q,kc,ks,band,cin,kwt,*after)


def depth_back_kernel(b_ref,tok_ref,gk_ref,gone_ref,w_ref,cd_ref,out_ref,cdg_ref,gd_ref):
    @pl.when(pl.program_id(0)==0)
    def _(): cdg_ref[...]=jnp.zeros_like(cdg_ref)
    gd_ref[...]=dot_t(gk_ref[...],w_ref[...]).astype(bf16)
    for r in range(0,SEQ,BAND):
        lo,bands=tap_bands(b_ref,r)
        for c in range(0,D,256):
            cs=slice(c,c+256)
            x=tok_ref[r:r+BAND,cs].astype(f32)
            g=gd_ref[lo:lo+2*BAND,cs]
            acc=gone_ref[r:r+BAND,cs]
            for j in range(KERNEL):
                m=KERNEL-1-j
                v=dot(bands[j],g)
                acc=acc+v*cd_ref[m:m+1,cs]
                cdg_ref[m,:,cs]+=fold8(v*x)
            out_ref[r:r+BAND,cs]=acc
def depth_back_call(bounds,tok,gk,gone,w,cd,after=()):
    n=tok.shape[0]; R=n//SEQ
    row=lambda w_:pl.BlockSpec((SEQ,w_),lambda i,b:(i,0))
    full=lambda s:pl.BlockSpec(s,lambda i,b:(0,)*len(s))
    S=lambda s,d:jax.ShapeDtypeStruct(s,d)
    return pl.pallas_call(ordered(depth_back_kernel,6,after),
        grid_spec=pltpu.PrefetchScalarGridSpec(num_scalar_prefetch=1,grid=(R,),
        in_specs=[row(D),row(ATT),row(D),pl.BlockSpec((D,ATT),lambda i,b:(0,4)),full((KERNEL,D))]+waits(after),
        out_specs=[row(D),full((KERNEL,8,D))],
        scratch_shapes=[pltpu.VMEM((SEQ,D),bf16)]),
        out_shape=[S((n,D),f32),S((KERNEL,8,D),f32)],
        compiler_params=pltpu.CompilerParams(vmem_limit_bytes=60<<20),
        cost_estimate=pl.CostEstimate(flops=2*n*D*(ATT+9*256),bytes_accessed=n*11000,transcendentals=0),
        name="depth_taps_back")(bounds,tok,gk,gone,w,cd,*after)

def input_kernel(gp_ref,part_ref,w_ref,out_ref):
    out_ref[...]=part_ref[...]+dot_t(gp_ref[...],w_ref[...])
def input_call(gp,part,w,after=()):
    n=gp.shape[0]
    return pl.pallas_call(ordered(input_kernel,3,after),grid=(n//SEQ,),
        in_specs=[pl.BlockSpec((SEQ,4*ATT),lambda i:(i,0)),pl.BlockSpec((SEQ,D),lambda i:(i,0)),pl.BlockSpec((D,4*ATT),lambda i:(0,0))]+waits(after),
        out_specs=pl.BlockSpec((SEQ,D),lambda i:(i,0)),
        out_shape=jax.ShapeDtypeStruct((n,D),f32),
        compiler_params=pltpu.CompilerParams(vmem_limit_bytes=60<<20),
        cost_estimate=pl.CostEstimate(flops=2*n*D*4*ATT,bytes_accessed=n*9200,transcendentals=0),
        name="input_grad")(gp,part,w,*after)


def digits(axis, size):
    out, bit = [], 1
    while bit < size:
        ways = 4 if size // bit % 4 == 0 else 2
        out.append((axis, size, bit, ways))
        bit *= ways
    return out

def send_xor(x, stage, d):
    axis, size, bit, _ = stage
    return lax.ppermute(x, axis, [(i, i ^ (d * bit)) for i in range(size)])

def my_digit(stage):
    axis, _, bit, ways = stage
    return (lax.axis_index(axis) // bit) % ways

def gather_send(x, stage):
    return [x] + [send_xor(x, stage, d) for d in range(1, stage[3])]

def gather_order(got, stage):
    ways = stage[3]
    mine = my_digit(stage)
    x = got[0]
    parts = []
    for place in range(ways):
        rel = mine ^ place
        part = got[0]
        for d in range(1, ways):
            part = jnp.where(rel == d, got[d], part)
        parts.append(part)
    return jnp.stack(parts, axis=1).reshape((x.shape[0] * ways,) + x.shape[1:])

def gather_near(got):
    return jnp.concatenate(got, axis=0)

def gather_stages(sizes):
    return digits("dp", sizes[0])[::-1] + digits("fsdp", sizes[1])[::-1]

def scatter_stages(sizes):
    return digits("fsdp", sizes[1]) + digits("dp", sizes[0])

def near_owners(sizes):
    nd, nf = sizes
    table = [0]
    for axis, _, bit, ways in gather_stages(sizes):
        step = bit * (nf if axis == "dp" else 1)
        table = [d * step + t for d in range(ways) for t in table]
    place = [0] * len(table)
    for i, t in enumerate(table):
        place[t] = i
    me = lax.axis_index("dp") * nf + lax.axis_index("fsdp")
    owners = jnp.asarray(table, jnp.int32) ^ me
    places = jnp.asarray(place, jnp.int32)[jnp.arange(nd * nf) ^ me]
    return owners, places

def scatter_send(g, stage):
    parts = jnp.split(g, stage[3], axis=0)
    return [parts[0]] + [send_xor(parts[d], stage, d) for d in range(1, stage[3])]

def scatter_add(got):
    total = got[0].astype(jnp.float32)
    for r in got[1:]:
        total = total + r.astype(jnp.float32)
    return total.astype(jnp.bfloat16)

def sum_send(x, stage):
    return [x] + [send_xor(x, stage, d) for d in range(1, stage[3])]

def together(*arrays):
    return lax.optimization_barrier(arrays)


def body(
    tokens,
    segment_ids,
    cotangent,
    w_proj,
    w_point,
    w_out,
    w_up,
    w_down,
    proj_bias,
    conv_depth,
    kernel_weight,
    kernel_bias,
    hidden_bias,
    up_bias,
    norm_gain,
    *,
    sizes,
):
    rows, seq = segment_ids.shape
    nd, nf = sizes
    mid = FF // GROUPS
    shard_rows, ff_rows = D // (nd * nf), mid // (nd * nf)
    tok = tokens.reshape(rows * seq, D)
    cot = cotangent.reshape(rows * seq, D)

    ahead = gather_stages(sizes)
    owners, places = near_owners(sizes)
    first = jnp.concatenate([w_proj, w_point], axis=1).astype(bf16)[None]
    second = jnp.concatenate([jnp.swapaxes(w_up, 1, 2), w_down], axis=2).reshape(GROUPS * ff_rows, D)
    second = jnp.concatenate([second, w_out], axis=0).astype(bf16)[None]
    bounds = find_bounds(segment_ids)
    kernel_rows, kernel_shift = pack_kernel_weight(kernel_weight, kernel_bias)
    up_near = jnp.take(up_bias.reshape(GROUPS, nd * nf, ff_rows), owners, axis=1).reshape(1, FF)
    first = gather_order(gather_send(first, ahead[0]), ahead[0])
    first, second = together(first, second)
    got_first = gather_send(first, ahead[1])
    got_second = gather_send(second, ahead[0])
    depth = depth_call(bounds, tok, conv_depth)
    *got_first, depth = together(*got_first, depth)
    first = gather_order(got_first, ahead[1])
    for stage in ahead[2:]:
        first = gather_order(gather_send(first, stage), stage)
    second = gather_near(got_second)
    first, second = together(first, second)
    got_second = gather_send(second, ahead[1])
    first = first.reshape(D, 5 * ATT)
    mixed, qkv, expo, recip, context, queries, key_conv, soft, bands, conv_in = mix_call(
        bounds, tok, depth, first, proj_bias, kernel_rows, kernel_shift
    )
    *got_second, mixed = together(*got_second, mixed)
    second = gather_near(got_second)
    for stage in ahead[2:]:
        second = gather_near(gather_send(second, stage))
    out_full = jnp.take(second[:, GROUPS * ff_rows :], places, axis=0).reshape(D, D)
    if ff_rows % 16:
        ff_full = second[:, : GROUPS * ff_rows].reshape(nd * nf, GROUPS, ff_rows, D)
        ff_full = jnp.swapaxes(ff_full, 0, 1).reshape(1, GROUPS * mid, D)
    else:
        ff_full = second
    layer_out, grad_one, grad_mixed, act, raised_low, first_low, two_low, one_low, norm_sums, up_sums = ff_call(
        mixed, tok, cot, out_full, ff_full, hidden_bias, up_near, norm_gain
    )

    away = scatter_stages(sizes)
    if ff_rows % 16:
        share = ffw_call(act, raised_low, first_low, two_low, 1)
        share = jnp.swapaxes(share.reshape(GROUPS, nd * nf, ff_rows, D), 0, 1).reshape(nd * nf, GROUPS * ff_rows, D)
    else:
        share = ffw_call(act, raised_low, first_low, two_low, nd * nf)
    share, one_low = together(share, one_low)
    got = scatter_send(share, away[0])
    out_grad = wg_call(mixed, one_low)
    *got, out_grad, grad_mixed = together(*got, out_grad, grad_mixed)
    share = scatter_add(got)
    share, grad_mixed = together(share, grad_mixed)
    got = scatter_send(share, away[1])
    grad_proj, grad_key, kw_sums, kb_sums, proj_sums = back_call(
        bounds, grad_mixed, qkv, expo, recip, context, queries, key_conv, soft, bands, conv_in, kernel_rows[:LANES]
    )
    *got, grad_proj, grad_key, proj_sums = together(*got, grad_proj, grad_key, proj_sums)
    share = scatter_add(got)
    for stage in away[2:-1]:
        share = scatter_add(scatter_send(share, stage))

    def taps_of(x):
        return x.reshape(HEADS, TAPS, -1)[:, SLOT : SLOT + KERNEL].reshape(HEADS * KERNEL, -1)

    norm_sums = jnp.sum(norm_sums, axis=1)
    up_sums = jnp.take(jnp.sum(up_sums, axis=0).reshape(GROUPS, nd * nf, ff_rows), places, axis=1)
    early = (
        jnp.sum(proj_sums, axis=1),
        taps_of(kw_sums).T,
        jnp.sum(taps_of(kb_sums), axis=1),
        norm_sums[:4],
        up_sums.reshape(FF),
        norm_sums[4:],
    )
    flat = flatten_small(early)
    share, flat, grad_proj = together(share, flat, grad_proj)
    got = scatter_send(share, away[-1])
    flat_got = sum_send(flat, away[0])
    proj_grad = wg_call(tok, grad_proj)
    point_grad = wg_call(depth, grad_key)
    *got, proj_grad, point_grad = together(*got, proj_grad, point_grad)
    *flat_got, grad_key = together(*flat_got, grad_key)
    flat = sum(flat_got)
    share = scatter_add(got)[0].astype(f32)
    ff_share = share.reshape(GROUPS, ff_rows, D)

    late = jnp.concatenate([proj_grad, point_grad, out_grad], axis=1).reshape(nd * nf, shard_rows, 5 * ATT + D)
    late = jnp.take(late, owners, axis=0)
    late, grad_key, flat = together(late, grad_key, flat)
    got = scatter_send(late, away[0])
    flat_got = sum_send(flat, away[1])
    partial, depth_sums = depth_back_call(bounds, tok, grad_key, grad_one, first, conv_depth)
    *got, partial, depth_sums = together(*got, partial, depth_sums)
    *flat_got, depth_sums = together(*flat_got, depth_sums)
    late = scatter_add(got)
    flat = sum(flat_got)
    small = flatten_small((jnp.sum(depth_sums, axis=1),))
    late, small, flat, partial = together(late, small, flat, partial)
    got = scatter_send(late, away[1])
    small_got = sum_send(small, away[0])
    tokens_grad = input_call(grad_proj, partial, first)
    *small_got, tokens_grad = together(*small_got, tokens_grad)
    *got, tokens_grad = together(*got, tokens_grad)
    small = sum(small_got)
    late = scatter_add(got)
    for stage in away[2:]:
        late = scatter_add(scatter_send(late, stage))
        flat = sum(sum_send(flat, stage))
    for stage in away[1:]:
        small = sum(sum_send(small, stage))
    late = late[0].astype(f32)
    early = split_small(flat, early)
    (depth_grad,) = split_small(small, (conv_depth,))
    return (
        layer_out.reshape(rows, seq, D),
        tokens_grad.reshape(rows, seq, D),
        late[:, : 4 * ATT],
        late[:, 4 * ATT : 5 * ATT],
        late[:, 5 * ATT :],
        jnp.swapaxes(ff_share[..., : D // GROUPS], 1, 2),
        ff_share[..., D // GROUPS :],
        early[0],
        depth_grad,
        early[1],
        early[2],
        early[3],
        early[4],
        early[5],
    )


def flatten_small(smalls):
    flat = jnp.concatenate([small.reshape(-1) for small in smalls])
    return jnp.pad(flat, (0, -flat.size % 1024)).reshape(-1, 128)


def split_small(flat, smalls):
    flat = flat.reshape(-1)
    out, at = [], 0
    for small in smalls:
        out.append(flat[at : at + small.size].reshape(small.shape))
        at += small.size
    return out


def solution(mesh):
    whole, split = P(), ("dp", "fsdp")
    rows3, rows2 = P(split, None, None), P(split, None)
    up, down = P(None, None, split), P(None, split, None)
    return jax.shard_map(
        functools.partial(body, sizes=(mesh.shape["dp"], mesh.shape["fsdp"])),
        mesh=mesh,
        in_specs=(rows3, rows2, rows3, rows2, rows2, rows2, up, down) + (whole,) * 7,
        out_specs=(rows3, rows3, rows2, rows2, rows2, up, down) + (whole,) * 7,
        check_vma=False,
    )
```

```python
import functools

import jax
import jax.numpy as jnp
from jax import lax
from jax.experimental import pallas as pl
from jax.experimental.pallas import tpu as pltpu
from jax.sharding import PartitionSpec as P

f32=jnp.float32
bf16=jnp.bfloat16
D=768; FF=3072; HEADS=6; HEAD_DIM=64; KERNEL=9; GROUPS=2; ATT=384
norm_eps=1e-12
LIGHT=pl.CostEstimate(flops=1,bytes_accessed=1,transcendentals=0)
def dot(a,b): return lax.dot_general(a,b,(((1,),(0,)),((),())),preferred_element_type=f32)
def dot_t(a,b): return lax.dot_general(a,b,(((1,),(1,)),((),())),preferred_element_type=f32)
def dot_l(a,b): return lax.dot_general(a,b,(((0,),(0,)),((),())),preferred_element_type=f32)
def fold8(x):
    return jnp.sum(x.reshape(x.shape[0]//8,8,x.shape[1]),axis=0)
def row_mean(x): return jnp.sum(x,axis=-1,keepdims=True)*(1.0/x.shape[-1])

def ordered(kernel,lead,after):
    extra=len(after)
    return lambda *refs: kernel(*refs[:lead],*refs[lead+extra:])
def waits(after):
    return [pl.BlockSpec(memory_space=pl.ANY) for _ in after]

def gelu_parts(x):
    phi=0.5+0.5*lax.erf(x*0.7071067811865476)
    return x*phi, phi+x*(jnp.exp(x*x*-0.5)*0.3989422804014327)

CH=256
PARTS=2
LAG=0
def ff_kernel(pieces,own_ref,*refs):
    w_refs=refs[:pieces]
    (mixed_ref,tok_ref,cot_ref,hb_ref,ub_ref,gain_ref,
     out_ref,gone_ref,gmix_ref,act_ref,gr_ref,xlow_ref,g2low_ref,g1low_ref,sums_ref,ups_ref,
     dg_ref,wup_ref,wdn_ref,wide_ref,wout_ref,keep_ref)=refs[pieces:]
    half=D//GROUPS; mid=FF//GROUPS
    @pl.when(pl.program_id(0)==0)
    def _():
        sums_ref[...]=jnp.zeros_like(sums_ref); ups_ref[...]=jnp.zeros_like(ups_ref)
        at=0
        total=sum(w.shape[0] for w in w_refs)
        rows,share=mid//total,D//total
        for w_ref in w_refs:
            n=w_ref.shape[0]
            for g in range(GROUPS):
                span=slice(at*rows,(at+n)*rows); part=slice(g*rows,(g+1)*rows)
                wup_ref[g,span,:]=w_ref[:,part,0:half].reshape(n*rows,half)
                wdn_ref[g,span,:]=w_ref[:,part,half:].reshape(n*rows,half)
            for i in range(n):
                place=pl.multiple_of(own_ref[at+i]*share,8)
                wide_ref[pl.ds(place,share),:]=w_ref[i,GROUPS*rows:GROUPS*rows+share,:].astype(f32)
            at+=n
        wout_ref[...]=wide_ref[...].astype(bf16)
    spans=[(g,c,slice(g*mid+c,g*mid+c+CH)) for g in range(GROUPS) for c in range(0,mid,CH)]
    gain1,gain2=gain_ref[0:1,:],gain_ref[1:2,:]

    def tokens_part(rs):
        res=dot(mixed_ref[rs,:],wout_ref[...])
        yield
        res=res+hb_ref[0:1,:]+tok_ref[rs,:].astype(f32)
        mean=row_mean(res); cen=res-mean
        inv1=lax.rsqrt(row_mean(cen*cen)+norm_eps)
        n1=cen*inv1
        first=n1*gain1+hb_ref[1:2,:]
        xlow_ref[rs,:]=first.astype(bf16)
        gone_ref[rs,:]=n1
        yield
        def raise_(g,c,cs):
            return dot_t(xlow_ref[rs,g*half:(g+1)*half],wup_ref[g,c:c+CH,:])+ub_ref[0:1,cs]
        lows=[]
        ahead=raise_(*spans[0])
        for i,(g,c,cs) in enumerate(spans):
            raised=ahead
            if i+1<len(spans): ahead=raise_(*spans[i+1])
            yield
            a,dg=gelu_parts(raised)
            act_ref[rs,cs]=a.astype(bf16)
            dg_ref[rs,cs]=dg
            yield
            if c+CH==mid:
                lows.append(dot(act_ref[rs,g*mid:(g+1)*mid],wdn_ref[g]))
                yield
        n1=gone_ref[rs,:]
        res=jnp.concatenate(lows,axis=1)+hb_ref[2:3,:]+(n1*gain1+hb_ref[1:2,:])
        mean=row_mean(res); cen=res-mean
        inv2=lax.rsqrt(row_mean(cen*cen)+norm_eps)
        n2=cen*inv2
        out_ref[rs,:]=(n2*gain2+hb_ref[3:4,:]).astype(bf16)
        yield
        e=cot_ref[rs,:].astype(f32)
        eg=e*gain2
        g2=inv2*(eg-row_mean(eg)-n2*row_mean(eg*n2))
        sums_ref[3]+=fold8(e); sums_ref[5]+=fold8(e*n2); sums_ref[2]+=fold8(g2)
        g2low_ref[rs,:]=g2.astype(bf16)
        keep_ref[rs,:]=g2
        yield
        def fall(g,c,cs):
            return dot_t(g2low_ref[rs,g*half:(g+1)*half],wdn_ref[g,c:c+CH,:])
        parts=[]
        ahead=fall(*spans[0])
        for i,(g,c,cs) in enumerate(spans):
            ga=ahead
            if i+1<len(spans): ahead=fall(*spans[i+1])
            yield
            gr=ga*dg_ref[rs,cs]
            ups_ref[:,cs]+=fold8(gr)
            gr_ref[rs,cs]=gr.astype(bf16)
            yield
            if c+CH==mid:
                parts.append(dot(gr_ref[rs,g*mid:(g+1)*mid],wup_ref[g]))
                yield
        gf=jnp.concatenate(parts,axis=1)+keep_ref[rs,:]
        n1=gone_ref[rs,:]
        sums_ref[1]+=fold8(gf); sums_ref[4]+=fold8(gf*n1)
        yield
        eg=gf*gain1
        g1=inv1*(eg-row_mean(eg)-n1*row_mean(eg*n1))
        sums_ref[0]+=fold8(g1)
        gone_ref[rs,:]=g1
        g1low_ref[rs,:]=g1.astype(bf16)
        yield
        gmix_ref[rs,:]=dot_t(g1low_ref[rs,:],wout_ref[...]).astype(bf16)
    total=mixed_ref.shape[0]; piece=total//PARTS
    running=[tokens_part(slice(i*piece,(i+1)*piece)) for i in range(PARTS)]
    waiting=[i*LAG for i in range(PARTS)]
    while any(part is not None for part in running):
        for i,part in enumerate(running):
            if waiting[i]>0:
                waiting[i]-=1
            elif part is not None and next(part,StopIteration) is StopIteration:
                running[i]=None

def ff_call(owners,weights,mixed,tok,cot,hb,ub,gain,T=512,after=()):
    n=tok.shape[0]
    row=lambda w,:pl.BlockSpec((T,w),lambda i,o:(i,0))
    full=lambda s:pl.BlockSpec(s,lambda i,o:(0,)*len(s),pipeline_mode=pl.Buffered(1))
    S=lambda s,d:jax.ShapeDtypeStruct(s,d)
    W=(GROUPS,FF//GROUPS,D//GROUPS)
    return pl.pallas_call(ordered(functools.partial(ff_kernel,len(weights)),7+len(weights),after),
        grid_spec=pltpu.PrefetchScalarGridSpec(num_scalar_prefetch=1,grid=(n//T,),
        in_specs=[full(w.shape) for w in weights]+[row(D),row(D),row(D),full((4,D)),full((1,FF)),full((2,D))]+waits(after),
        out_specs=[row(D),row(D),row(D),row(FF),row(FF),row(D),row(D),row(D),full((6,8,D)),full((8,FF))],
        scratch_shapes=[pltpu.VMEM((T,FF),f32),pltpu.VMEM(W,bf16),pltpu.VMEM(W,bf16),pltpu.VMEM((D,D),f32),pltpu.VMEM((D,D),bf16),pltpu.VMEM((T,D),f32)]),
        out_shape=[S((n,D),bf16),S((n,D),f32),S((n,D),bf16),S((n,FF),bf16),S((n,FF),bf16),S((n,D),bf16),S((n,D),bf16),S((n,D),bf16),S((6,8,D),f32),S((8,FF),f32)],
        compiler_params=pltpu.CompilerParams(vmem_limit_bytes=60<<20),
        cost_estimate=LIGHT,
        name="feed_forward",
    )(owners,*weights,mixed,tok,cot,hb,ub,gain,*after)

def fetch(pairs,sems):
    copies=[pltpu.make_async_copy(src,dst,sems.at[i]) for i,(src,dst) in enumerate(pairs)]
    for copy in copies: copy.start()
    return copies
def by_owner(own_ref,wide_ref,width,outs,rows,columns):
    per=outs[0].shape[0]; share=rows.stop-rows.start
    for p,out in enumerate(outs):
        for i in range(per):
            place=pl.multiple_of(own_ref[p*per+i]*share,8)
            out[i,rows,columns]=wide_ref[pl.ds(place,share),0:width].astype(bf16)

def ffw_kernel(parts,share,own_ref,act_ref,gr_ref,xlow_ref,g2low_ref,mix_ref,g1_ref,*refs):
    outs=refs[:parts]
    act,gr,xlow,g2low,mix,g1,wide,sems=refs[parts:parts+8]
    blocks=refs[parts+8:parts+8+parts]
    out_sem=refs[-1]
    half=D//GROUPS; mid=FF//GROUPS; C=mid//parts
    rows=(blocks[0].shape[1]-share)//GROUPS
    jobs=[(p,g) for p in range(parts) for g in range(GROUPS)]
    cols=[slice(g*mid+p*C,g*mid+(p+1)*C) for p,g in jobs]
    pairs=[(xlow_ref,xlow)]+[(gr_ref.at[:,cols[0]],gr.at[0]),(g2low_ref,g2low),(act_ref.at[:,cols[0]],act.at[0])]
    for j in range(1,len(jobs)):
        pairs+=[(gr_ref.at[:,cols[j]],gr.at[j]),(act_ref.at[:,cols[j]],act.at[j])]
    pairs+=[(mix_ref,mix),(g1_ref,g1)]
    copies=fetch(pairs,sems)
    per=blocks[0].shape[0]
    for j,(p,g) in enumerate(jobs):
        gs=slice(g*half,(g+1)*half); rs=slice(g*rows,(g+1)*rows)
        if j==0: copies[0].wait()
        copies[1 if j==0 else 2+2*j].wait()
        blocks[p][:,rs,0:half]=dot_l(xlow[:,gs],gr[j]).T.astype(bf16).reshape(per,rows,half)
        if j==0: copies[2].wait()
        copies[3+2*j].wait()
        blocks[p][:,rs,half:]=dot_l(g2low[:,gs],act[j]).T.astype(bf16).reshape(per,rows,half)
    copies[-2].wait(); copies[-1].wait()
    if share:
        wide[...]=dot_l(mix[...],g1[...])
        by_owner(own_ref,wide,D,blocks,slice(GROUPS*rows,GROUPS*rows+share),slice(0,D))
    done=fetch([(blocks[p],outs[p]) for p in range(parts)],out_sem)
    for copy in done: copy.wait()
def ffw_call(owners,act,gr,xlow,g2low,mixed,g1,parts,share,after=()):
    n=act.shape[0]; blocks=owners.shape[0]; mid=FF//GROUPS; C=mid//parts
    shape=(blocks//parts,FF//blocks+share,D)
    any_=pl.BlockSpec(memory_space=pl.ANY)
    jobs=parts*GROUPS
    return pl.pallas_call(ordered(functools.partial(ffw_kernel,parts,share),7,after),
        grid_spec=pltpu.PrefetchScalarGridSpec(num_scalar_prefetch=1,grid=(1,),
        in_specs=[any_]*6+waits(after),out_specs=[any_]*parts,
        scratch_shapes=[pltpu.VMEM((jobs,n,C),bf16)]*2+[pltpu.VMEM((n,D),bf16)]*4+[pltpu.VMEM((D,D),f32),pltpu.SemaphoreType.DMA((2*jobs+4,))]
            +[pltpu.VMEM(shape,bf16)]*parts+[pltpu.SemaphoreType.DMA((parts,))]),
        out_shape=[jax.ShapeDtypeStruct(shape,bf16)]*parts,
        compiler_params=pltpu.CompilerParams(vmem_limit_bytes=60<<20),
        cost_estimate=LIGHT,
        name="feed_forward_weights",
    )(owners,act,gr,xlow,g2low,mixed,g1,*after)

def feature_weights_kernel(parts,own_ref,tok_ref,gp_ref,dep_ref,gk_ref,*refs):
    outs=refs[:parts]
    tok,gp,dep,gk,wide,sems=refs[parts:parts+6]
    blocks=refs[parts+6:parts+6+parts]
    out_sem=refs[-1]
    copies=fetch([(gk_ref,gk),(dep_ref,dep),(tok_ref,tok),(gp_ref.at[:,0:2*ATT],gp.at[0]),(gp_ref.at[:,2*ATT:],gp.at[1])],sems)
    rows=slice(0,blocks[0].shape[1])
    copies[0].wait(); copies[1].wait()
    wide[:,0:ATT]=dot_l(dep[...],gk[...])
    by_owner(own_ref,wide,ATT,blocks,rows,slice(4*ATT,5*ATT))
    copies[2].wait()
    for j in range(2):
        copies[3+j].wait()
        wide[...]=dot_l(tok[...],gp[j])
        by_owner(own_ref,wide,D,blocks,rows,slice(j*D,(j+1)*D))
    done=fetch([(blocks[p],outs[p]) for p in range(parts)],out_sem)
    for copy in done: copy.wait()
def feature_weights_call(owners,tok,gp,dep,gk,parts,after=()):
    n=tok.shape[0]; blocks=owners.shape[0]
    shape=(blocks//parts,D//blocks,5*ATT)
    any_=pl.BlockSpec(memory_space=pl.ANY)
    return pl.pallas_call(ordered(functools.partial(feature_weights_kernel,parts),5,after),
        grid_spec=pltpu.PrefetchScalarGridSpec(num_scalar_prefetch=1,grid=(1,),
        in_specs=[any_]*4+waits(after),out_specs=[any_]*parts,
        scratch_shapes=[pltpu.VMEM((n,D),bf16),pltpu.VMEM((2,n,2*ATT),bf16),pltpu.VMEM((n,D),bf16),pltpu.VMEM((n,ATT),bf16),pltpu.VMEM((D,D),f32),pltpu.SemaphoreType.DMA((5,))]
            +[pltpu.VMEM(shape,bf16)]*parts+[pltpu.SemaphoreType.DMA((parts,))]),
        out_shape=[jax.ShapeDtypeStruct(shape,bf16)]*parts,
        compiler_params=pltpu.CompilerParams(vmem_limit_bytes=60<<20),
        cost_estimate=LIGHT,
        name="feature_weights",
    )(owners,tok,gp,dep,gk,*after)

TAPS=16
LANES=HEADS*TAPS
BT=64
LEAD=16
SLOT=4
HALF=256
SEQ=512
NEG=-1000000000.0

def doc_of(pos,b_ref,first=0):
    row=pl.program_id(0)+first
    return ((pos>=b_ref[row,0]).astype(jnp.int32)+(pos>=b_ref[row,1]).astype(jnp.int32)+(pos>=b_ref[row,2]).astype(jnp.int32))
def tap_valid_t(b_ref):
    tap=lax.broadcasted_iota(jnp.int32,(TAPS,SEQ),0); t=lax.broadcasted_iota(jnp.int32,(TAPS,SEQ),1)
    u=t+tap-KERNEL//2-SLOT
    ok=(u>=0)&(u<SEQ)&(doc_of(u,b_ref)==doc_of(t,b_ref))&(tap>=SLOT)&(tap<SLOT+KERNEL)
    return ok.astype(f32)
def roll_matrix(b_ref,back):
    start=b_ref[pl.program_id(0),3]
    a=lax.broadcasted_iota(jnp.int32,(SEQ,SEQ),1 if back else 0); t=lax.broadcasted_iota(jnp.int32,(SEQ,SEQ),0 if back else 1)
    d=a+start-t
    return jnp.where((d==0)|(d==SEQ),1.0,0.0).astype(bf16)
def head_lanes(shape,h):
    lane=lax.broadcasted_iota(jnp.int32,shape,len(shape)-1)
    return (lane<HEAD_DIM) if h==0 else (lane>=HEAD_DIM)
def keep_head(x,h):
    return jnp.where(head_lanes(x.shape,h),x,jnp.zeros_like(x))

BAND=128
def tap_bands(b_ref,r,first=0):
    lo=min(max(r-BAND//2,0),SEQ-2*BAND)
    row=lax.broadcasted_iota(jnp.int32,(BAND,2*BAND),0)+r; col=lax.broadcasted_iota(jnp.int32,(BAND,2*BAND),1)+lo
    step=jnp.where(doc_of(row,b_ref,first)==doc_of(col,b_ref,first),col-row,SEQ)
    return lo,[jnp.where(step==j-KERNEL//2,1.0,0.0).astype(bf16) for j in range(KERNEL)]

def depth_kernel(b_ref,tok_ref,cd_ref,out_ref):
    for r in range(0,SEQ,BAND):
        lo,bands=tap_bands(b_ref,r)
        x=tok_ref[lo:lo+2*BAND,:]
        acc=None
        for j in range(KERNEL):
            v=dot(bands[j],x)*cd_ref[j:j+1,:]
            acc=v if acc is None else acc+v
        out_ref[r:r+BAND,:]=acc.astype(bf16)

def depth_call(bounds,tok,cd,after=()):
    n=tok.shape[0]
    return pl.pallas_call(ordered(depth_kernel,3,after),
        grid_spec=pltpu.PrefetchScalarGridSpec(num_scalar_prefetch=1,grid=(n//SEQ,),
        in_specs=[pl.BlockSpec((SEQ,D),lambda i,b:(i,0)),pl.BlockSpec((KERNEL,D),lambda i,b:(0,0))]+waits(after),
        out_specs=pl.BlockSpec((SEQ,D),lambda i,b:(i,0)),
        ),
        out_shape=jax.ShapeDtypeStruct((n,D),bf16),
        compiler_params=pltpu.CompilerParams(vmem_limit_bytes=60<<20),
        cost_estimate=LIGHT,
        name="depth_taps")(bounds,tok,cd,*after)


def mix_kernel(b_ref,tok_ref,dep_ref,w_ref,pb_ref,kw_ref,kb_ref,
               mixed_ref,qkv_ref,e_ref,r_ref,ctx_ref,q_ref,kc_ref,ks_ref,band_ref,cin_ref):
    tok=tok_ref[...]
    p=dot(tok,w_ref[:,0:4*ATT])
    q=(p[:,0:ATT]+pb_ref[0:1,:]).astype(bf16)
    k=p[:,ATT:2*ATT].astype(bf16)
    v=(p[:,2*ATT:3*ATT]+pb_ref[1:2,:]).astype(bf16)
    cin=(p[:,3*ATT:]+pb_ref[2:3,:]).astype(bf16)
    q_ref[...]=q
    rolled=dot(roll_matrix(b_ref,False),jnp.concatenate([q*jnp.bfloat16(0.125),k,v],axis=1)).astype(bf16)
    qkv_ref[...]=rolled
    key_conv=dot(dep_ref[...],w_ref[:,4*ATT:])+pb_ref[3:4,:]
    kc_ref[...]=key_conv
    attn=key_conv*q.astype(f32)
    hi=attn.astype(bf16); lo=(attn-hi.astype(f32)).astype(bf16)
    both=dot_t(kw_ref[...],hi)
    logits=both[:LANES]+both[LANES:]+dot_t(kw_ref[0:LANES,:],lo)+kb_ref[...]
    logits=logits.reshape(HEADS,TAPS,SEQ)
    tap=lax.broadcasted_iota(jnp.int32,(HEADS,TAPS,SEQ),1)
    logits=jnp.where((tap>=SLOT)&(tap<SLOT+KERNEL),logits,-1e30)
    ex=jnp.exp(logits-jnp.max(logits,axis=1,keepdims=True))
    ks=ex/jnp.sum(ex,axis=1,keepdims=True)
    ks_ref[...]=ks.reshape(LANES,SEQ)
    km=(ks*tap_valid_t(b_ref)[None]).reshape(LANES,SEQ)
    km=jnp.concatenate([km,jnp.zeros((128-LANES,SEQ),f32)],axis=0).T
    cin_ref[0:LEAD,:]=jnp.zeros((LEAD,ATT),bf16); cin_ref[LEAD+SEQ:,:]=jnp.zeros((128-LEAD-BT,ATT),bf16)
    cin_ref[LEAD:LEAD+SEQ,:]=cin
    row=lax.broadcasted_iota(jnp.int32,(BT,128),0); lane=lax.broadcasted_iota(jnp.int32,(BT,128),1)
    off=lane-row-(LEAD-KERNEL//2)
    on_band=(off>=0)&(off<KERNEL)
    for i in range(SEQ//BT):
        kmi=km[i*BT:(i+1)*BT,:]
        bands=[]
        for h in range(HEADS):
            x=pltpu.roll(kmi,(LEAD-KERNEL//2-SLOT-h*TAPS)%128,1,stride=1,stride_axis=0)
            x=jnp.where(on_band,x,0.0).astype(bf16)
            band_ref[i,h]=x
            bands.append(x)
        for pr in range(HEADS//2):
            win=cin_ref[i*BT:i*BT+128,pr*128:(pr+1)*128]
            o=dot(jnp.concatenate(bands[2*pr:2*pr+2],axis=1),jnp.concatenate([keep_head(win,0),keep_head(win,1)],axis=0))
            mixed_ref[i*BT:(i+1)*BT,ATT+pr*128:ATT+(pr+1)*128]=o.astype(bf16)
    start=b_ref[pl.program_id(0),3]
    def rolled_doc(axis):
        t=lax.broadcasted_iota(jnp.int32,(HALF,HALF),axis)+start+HALF
        return doc_of(jnp.where(t>=SEQ,t-SEQ,t),b_ref)
    same=rolled_doc(0)==rolled_doc(1)
    ones=jnp.ones((HALF,128),bf16)
    for a in range(2):
        rs=slice(a*HALF,(a+1)*HALF)
        for pr in range(HEADS//2):
            Q=rolled[rs,pr*128:(pr+1)*128]; K=rolled[rs,ATT+pr*128:ATT+(pr+1)*128]; V=rolled[rs,2*ATT+pr*128:2*ATT+(pr+1)*128]
            es=[];vs=[]
            for h in range(2):
                s=dot_t(Q,keep_head(K,h))
                if a==1: s=jnp.where(same,s,NEG)
                e=jnp.exp(s-jnp.max(s,axis=-1,keepdims=True)).astype(bf16)
                e_ref[a,2*pr+h]=e
                es.append(e); vs.append(jnp.concatenate([keep_head(V,h),keep_head(ones,h)],axis=1))
            o=dot(jnp.concatenate(es,axis=1),jnp.concatenate(vs,axis=0))
            r=1.0/o[:,128:]
            r_ref[rs,pr*128:(pr+1)*128]=r
            ctx_ref[rs,pr*128:(pr+1)*128]=(o[:,:128]*r).astype(bf16)
    mixed_ref[:,0:ATT]=dot(roll_matrix(b_ref,True),ctx_ref[...]).astype(bf16)

CPAD=SEQ+128-BT
def mix_call(bounds,tok,dep,w,pb,kw,kb,after=()):
    n=tok.shape[0]; R=n//SEQ
    row=lambda w_:pl.BlockSpec((SEQ,w_),lambda i,b:(i,0))
    full=lambda s:pl.BlockSpec(s,lambda i,b:(0,)*len(s))
    lead=lambda s:pl.BlockSpec((None,)+s,lambda i,b:(i,)+(0,)*len(s))
    S=lambda s,d:jax.ShapeDtypeStruct(s,d)
    NT=SEQ//BT
    return pl.pallas_call(ordered(mix_kernel,7,after),
        grid_spec=pltpu.PrefetchScalarGridSpec(num_scalar_prefetch=1,grid=(R,),
        in_specs=[row(D),row(D),full((D,5*ATT)),full((4,ATT)),full((2*LANES,ATT)),full((LANES,1))]+waits(after),
        out_specs=[row(D),row(3*ATT),lead((2,HEADS,HALF,HALF)),row(ATT),row(ATT),row(ATT),row(ATT),lead((LANES,SEQ)),lead((NT,HEADS,BT,128)),lead((CPAD,ATT))]),
        out_shape=[S((n,D),bf16),S((n,3*ATT),bf16),S((R,2,HEADS,HALF,HALF),bf16),S((n,ATT),f32),S((n,ATT),bf16),S((n,ATT),bf16),S((n,ATT),f32),S((R,LANES,SEQ),f32),S((R,NT,HEADS,BT,128),bf16),S((R,CPAD,ATT),bf16)],
        compiler_params=pltpu.CompilerParams(vmem_limit_bytes=60<<20),
        cost_estimate=LIGHT,
        name="attend_and_span")(bounds,tok,dep,w,pb,kw,kb,*after)


def pack_kernel_weight(kw,kb):
    k=kw.T.reshape(HEADS,KERNEL,ATT)
    k=jnp.pad(k,((0,0),(SLOT,TAPS-KERNEL-SLOT),(0,0))).reshape(LANES,ATT)
    hi=lax.reduce_precision(k,8,7); lo=(k-hi).astype(bf16); hi=hi.astype(bf16)
    b=jnp.pad(kb.reshape(HEADS,KERNEL),((0,0),(SLOT,TAPS-KERNEL-SLOT))).reshape(LANES,1)
    return jnp.concatenate([hi,lo],axis=0),b

def find_bounds(seg):
    counts=jnp.stack([jnp.sum(seg==i,axis=1) for i in range(4)],axis=1)
    begin=jnp.cumsum(counts,axis=1)-counts
    which=jnp.argmax(counts==HALF,axis=1)
    start=jnp.take_along_axis(begin,which[:,None],axis=1)
    return jnp.concatenate([begin[:,1:],start],axis=1).astype(jnp.int32)

def span_back_kernel(b_ref,gm_ref,q_ref,kc_ref,ks_ref,band_ref,cin_ref,kwt_ref,
                gk_ref,gqc_ref,gci_ref,kwg_ref,kbg_ref,pbg_ref,gcin_ref):
    @pl.when(pl.program_id(0)==0)
    def _():
        kwg_ref[...]=jnp.zeros_like(kwg_ref); kbg_ref[...]=jnp.zeros_like(kbg_ref); pbg_ref[...]=jnp.zeros_like(pbg_ref)
    gcin_ref[...]=jnp.zeros_like(gcin_ref)
    lane=lax.broadcasted_iota(jnp.int32,(BT,128),1)
    anti=lax.broadcasted_iota(jnp.int32,(SEQ,SEQ),0)+lax.broadcasted_iota(jnp.int32,(SEQ,SEQ),1)
    anti=jnp.where(anti==SEQ-1,1.0,0.0).astype(bf16)
    falling=dot(anti,gm_ref[:,ATT:]).astype(bf16)
    logits=[]
    for i in range(SEQ//BT):
        acc=None
        f=SEQ//BT-1-i
        for pr in range(HEADS//2):
            g=gm_ref[i*BT:(i+1)*BT,ATT+pr*128:ATT+(pr+1)*128]
            gf=falling[i*BT:(i+1)*BT,pr*128:(pr+1)*128]
            win=cin_ref[f*BT:f*BT+128,pr*128:(pr+1)*128]
            back=None
            for h in range(2):
                head=2*pr+h
                d=dot_t(keep_head(gf,h),win)
                d=pltpu.roll(d,(head*TAPS+SLOT-LEAD+KERNEL//2-BT+1)%128,1,stride=1,stride_axis=0)
                d=jnp.where((lane>=head*TAPS+SLOT)&(lane<head*TAPS+SLOT+KERNEL),d,0.0)
                acc=d if acc is None else acc+d
                p=dot_l(band_ref[i,head],keep_head(g,h))
                back=p if back is None else back+p
            gcin_ref[i*BT:i*BT+128,pr*128:(pr+1)*128]+=back
        logits.append(acc)
    gk=jnp.concatenate(logits,axis=0)
    gh=gk.astype(bf16); glo=(gk-gh.astype(f32)).astype(bf16)
    gk=(dot_l(gh,anti)+dot_l(glo,anti))[0:LANES,:].reshape(HEADS,TAPS,SEQ)*tap_valid_t(b_ref)[None]
    ks=ks_ref[...].reshape(HEADS,TAPS,SEQ)
    gl=(ks*(gk-jnp.sum(gk*ks,axis=1,keepdims=True))).reshape(LANES,SEQ)
    kbg_ref[...]+=gl[:,0:128]+gl[:,128:256]+gl[:,256:384]+gl[:,384:512]
    q=q_ref[...].astype(f32); kc=kc_ref[...]
    attn=kc*q
    hi=attn.astype(bf16)
    glb=gl.astype(bf16)
    kwg_ref[...]+=dot(glb,hi)
    gattn=dot_l(glb,kwt_ref[...])
    gkc=gattn*q
    gk_ref[...]=gkc.astype(bf16)
    pbg_ref[1]+=fold8(gkc)
    gqc_ref[...]=gattn*kc
    gci=gcin_ref[LEAD:LEAD+SEQ,:]
    pbg_ref[0]+=fold8(gci)
    gci_ref[...]=gci.astype(bf16)

def attend_back_kernel(b_ref,gm_ref,qkv_ref,e_ref,r_ref,ctx_ref,gqc_ref,gci_ref,gp_ref,pbg_ref,dr_ref):
    @pl.when(pl.program_id(0)==0)
    def _(): pbg_ref[...]=jnp.zeros_like(pbg_ref)
    dor=(dot(roll_matrix(b_ref,False),gm_ref[:,0:ATT])*r_ref[...])
    dol=dor.astype(bf16)
    prod=dol.astype(f32)*ctx_ref[...].astype(f32)
    ph=prod.astype(bf16); plo=(prod-ph.astype(f32)).astype(bf16)
    si=lax.broadcasted_iota(jnp.int32,(128,256),0)//HEAD_DIM; sj=lax.broadcasted_iota(jnp.int32,(128,256),1)//128
    pick=jnp.where(si==sj,1.0,0.0).astype(bf16)
    for a in range(2):
        rs=slice(a*HALF,(a+1)*HALF)
        for pr in range(HEADS//2):
            cs=slice(pr*128,(pr+1)*128)
            Q=qkv_ref[rs,pr*128:(pr+1)*128]; K=qkv_ref[rs,ATT+pr*128:ATT+(pr+1)*128]; V=qkv_ref[rs,2*ATT+pr*128:2*ATT+(pr+1)*128]
            delta=dot(ph[rs,cs],pick)+dot(plo[rs,cs],pick)
            G=dol[rs,cs]
            es=[e_ref[a,2*pr+h] for h in range(2)]
            ds=[]
            for h in range(2):
                dp=dot_t(G,keep_head(V,h))
                dl=delta[:,h*128:(h+1)*128]
                ds.append((es[h].astype(f32)*(dp-jnp.concatenate([dl,dl],axis=1))).astype(bf16))
            st=lambda x:jnp.concatenate([keep_head(x,0),keep_head(x,1)],axis=0)
            dq=dot(jnp.concatenate(ds,axis=1),st(K))*0.125
            dk=dot_l(jnp.concatenate(ds,axis=0),st(Q))
            dv=dot_l(jnp.concatenate(es,axis=0),st(G))
            dr_ref[rs,cs]=dq.astype(bf16)
            dr_ref[rs,ATT+pr*128:ATT+(pr+1)*128]=dk.astype(bf16)
            dr_ref[rs,2*ATT+pr*128:2*ATT+(pr+1)*128]=dv.astype(bf16)
    un=dot(roll_matrix(b_ref,True),dr_ref[...])
    gq=un[:,0:ATT]+gqc_ref[...]
    pbg_ref[0]+=fold8(gq); pbg_ref[1]+=fold8(un[:,2*ATT:])
    gp_ref[:,0:ATT]=gq.astype(bf16)
    gp_ref[:,ATT:3*ATT]=un[:,ATT:].astype(bf16)
    gp_ref[:,3*ATT:]=gci_ref[...]

def span_back_call(bounds,gm,q,kc,ks,band,cin,kwt,after=()):
    n=gm.shape[0]; R=n//SEQ; NT=SEQ//BT
    row=lambda w_:pl.BlockSpec((SEQ,w_),lambda i,b:(i,0))
    full=lambda s:pl.BlockSpec(s,lambda i,b:(0,)*len(s))
    lead=lambda s:pl.BlockSpec((None,)+s,lambda i,b:(i,)+(0,)*len(s))
    S=lambda s,d:jax.ShapeDtypeStruct(s,d)
    return pl.pallas_call(ordered(span_back_kernel,8,after),
        grid_spec=pltpu.PrefetchScalarGridSpec(num_scalar_prefetch=1,grid=(R,),
        in_specs=[row(D),row(ATT),row(ATT),lead((LANES,SEQ)),lead((NT,HEADS,BT,128)),lead((CPAD,ATT)),full((LANES,ATT))]+waits(after),
        out_specs=[row(ATT),row(ATT),row(ATT),full((LANES,ATT)),full((LANES,128)),full((2,8,ATT))],
        scratch_shapes=[pltpu.VMEM((CPAD,ATT),f32)]),
        out_shape=[S((n,ATT),bf16),S((n,ATT),f32),S((n,ATT),bf16),S((LANES,ATT),f32),S((LANES,128),f32),S((2,8,ATT),f32)],
        compiler_params=pltpu.CompilerParams(vmem_limit_bytes=60<<20),
        cost_estimate=LIGHT,
        name="span_back")(bounds,gm,q,kc,ks,band,cin,kwt,*after)
def attend_back_call(bounds,gm,qkv,E,r,ctx,gqc,gci,after=()):
    n=gm.shape[0]; R=n//SEQ
    row=lambda w_:pl.BlockSpec((SEQ,w_),lambda i,b:(i,0))
    full=lambda s:pl.BlockSpec(s,lambda i,b:(0,)*len(s))
    lead=lambda s:pl.BlockSpec((None,)+s,lambda i,b:(i,)+(0,)*len(s))
    S=lambda s,d:jax.ShapeDtypeStruct(s,d)
    return pl.pallas_call(ordered(attend_back_kernel,8,after),
        grid_spec=pltpu.PrefetchScalarGridSpec(num_scalar_prefetch=1,grid=(R,),
        in_specs=[row(D),row(3*ATT),lead((2,HEADS,HALF,HALF)),row(ATT),row(ATT),row(ATT),row(ATT)]+waits(after),
        out_specs=[row(4*ATT),full((2,8,ATT))],
        scratch_shapes=[pltpu.VMEM((SEQ,3*ATT),bf16)]),
        out_shape=[S((n,4*ATT),bf16),S((2,8,ATT),f32)],
        compiler_params=pltpu.CompilerParams(vmem_limit_bytes=60<<20),
        cost_estimate=LIGHT,
        name="attend_back")(bounds,gm,qkv,E,r,ctx,gqc,gci,*after)

def depth_back_kernel(first,b_ref,tok_ref,gk_ref,gone_ref,w_ref,cd_ref,out_ref,cdg_ref,gd_ref):
    @pl.when(pl.program_id(0)==0)
    def _(): cdg_ref[...]=jnp.zeros_like(cdg_ref)
    gd_ref[...]=dot_t(gk_ref[...],w_ref[...]).astype(bf16)
    for r in range(0,SEQ,BAND):
        lo,bands=tap_bands(b_ref,r,first)
        for c in range(0,D,256):
            cs=slice(c,c+256)
            x=tok_ref[r:r+BAND,cs].astype(f32)
            g=gd_ref[lo:lo+2*BAND,cs]
            acc=gone_ref[r:r+BAND,cs]
            for j in range(KERNEL):
                m=KERNEL-1-j
                v=dot(bands[j],g)
                acc=acc+v*cd_ref[m:m+1,cs]
                cdg_ref[m,:,cs]+=fold8(v*x)
            out_ref[r:r+BAND,cs]=acc
def depth_back_call(bounds,tok,gk,gone,w,cd,first,rows,after=()):
    row=lambda w_:pl.BlockSpec((SEQ,w_),lambda i,b:(i+first,0))
    full=lambda s:pl.BlockSpec(s,lambda i,b:(0,)*len(s))
    S=lambda s,d:jax.ShapeDtypeStruct(s,d)
    return pl.pallas_call(ordered(functools.partial(depth_back_kernel,first),6,after),
        grid_spec=pltpu.PrefetchScalarGridSpec(num_scalar_prefetch=1,grid=(rows,),
        in_specs=[row(D),row(ATT),row(D),pl.BlockSpec((D,ATT),lambda i,b:(0,4)),full((KERNEL,D))]+waits(after),
        out_specs=[pl.BlockSpec((SEQ,D),lambda i,b:(i,0)),full((KERNEL,8,D))],
        scratch_shapes=[pltpu.VMEM((SEQ,D),bf16)]),
        out_shape=[S((rows*SEQ,D),f32),S((KERNEL,8,D),f32)],
        compiler_params=pltpu.CompilerParams(vmem_limit_bytes=60<<20),
        cost_estimate=LIGHT,
        name="depth_taps_back")(bounds,tok,gk,gone,w,cd,*after)
def input_kernel(cut,gp_ref,low_ref,high_ref,w_ref,out_ref):
    x=dot_t(gp_ref[...],w_ref[...])
    @pl.when(pl.program_id(0)<cut)
    def _(): out_ref[...]=low_ref[...]+x
    @pl.when(pl.program_id(0)>=cut)
    def _(): out_ref[...]=high_ref[...]+x
def input_call(gp,low,high,w,after=()):
    n=gp.shape[0]; cut=low.shape[0]//SEQ
    return pl.pallas_call(ordered(functools.partial(input_kernel,cut),4,after),grid=(n//SEQ,),
        in_specs=[pl.BlockSpec((SEQ,4*ATT),lambda i:(i,0)),pl.BlockSpec((SEQ,D),lambda i:(jnp.minimum(i,cut-1),0)),pl.BlockSpec((SEQ,D),lambda i:(jnp.maximum(i-cut,0),0)),pl.BlockSpec((D,4*ATT),lambda i:(0,0))]+waits(after),
        out_specs=pl.BlockSpec((SEQ,D),lambda i:(i,0)),
        out_shape=jax.ShapeDtypeStruct((n,D),f32),
        compiler_params=pltpu.CompilerParams(vmem_limit_bytes=60<<20),
        cost_estimate=LIGHT,
        name="input_grad")(gp,low,high,w,*after)

SMALL=112
def pack_kernel(att_ref,span_ref,low_ref,high_ref,kw_ref,kb_ref,norm_ref,up_ref,out_ref,wide_ref):
    wide_ref[...]=jnp.zeros_like(wide_ref)
    wide_ref[0:2,:]=jnp.sum(att_ref[...],axis=1)
    wide_ref[2:4,:]=jnp.sum(span_ref[...],axis=1)
    taps=jnp.sum(low_ref[...]+high_ref[...],axis=1)
    wide_ref[4:13,:]=taps[:,0:ATT]
    wide_ref[13:22,:]=taps[:,ATT:]
    for h in range(HEADS):
        wide_ref[22+h*KERNEL:22+(h+1)*KERNEL,:]=kw_ref[h*TAPS+SLOT:h*TAPS+SLOT+KERNEL,:]
    norms=jnp.sum(norm_ref[...],axis=1)
    wide_ref[76:82,:]=norms[:,0:ATT]
    wide_ref[82:88,:]=norms[:,ATT:]
    wide_ref[88:96,:]=up_ref[...]
    kb=jnp.concatenate([kb_ref[...],jnp.zeros((128-LANES,128),f32)],axis=0).T
    wide_ref[96:97,0:128]=jnp.sum(kb,axis=0,keepdims=True)
    out_ref[...]=wide_ref[...].astype(bf16)
def pack_call(att,span,low,high,kw,kb,norm,up):
    return pl.pallas_call(pack_kernel,
        out_shape=jax.ShapeDtypeStruct((SMALL,ATT),bf16),
        scratch_shapes=[pltpu.VMEM((SMALL,ATT),f32)],
        cost_estimate=LIGHT,
        name="pack_small")(att,span,low,high,kw,kb,norm,up)
def unpack_kernel(count,*refs):
    got=refs[:count]
    proj_ref,depth_ref,kw_ref,kb_ref,hid_ref,up_ref,gain_ref,wide_ref=refs[count:]
    x=got[0][...].astype(f32)
    for g in got[1:]: x=x+g[...].astype(f32)
    wide_ref[...]=x
    proj_ref[...]=wide_ref[0:4,:]
    depth_ref[:,0:ATT]=wide_ref[4:13,:]
    depth_ref[:,ATT:]=wide_ref[13:22,:]
    kw_ref[...]=wide_ref[22:86,:].T[:,0:HEADS*KERNEL]
    hid_ref[:,0:ATT]=wide_ref[76:80,:]
    hid_ref[:,ATT:]=wide_ref[82:86,:]
    gain_ref[:,0:ATT]=wide_ref[80:82,:]
    gain_ref[:,ATT:]=wide_ref[86:88,:]
    for i in range(FF//ATT): up_ref[0:1,i*ATT:(i+1)*ATT]=wide_ref[88+i:89+i,:]
    for h in range(HEADS): kb_ref[0:1,h*KERNEL:(h+1)*KERNEL]=wide_ref[96:97,h*TAPS+SLOT:h*TAPS+SLOT+KERNEL]
def unpack_call(got):
    S=lambda *s:jax.ShapeDtypeStruct(s,f32)
    out=pl.pallas_call(functools.partial(unpack_kernel,len(got)),
        out_shape=[S(4,ATT),S(KERNEL,D),S(ATT,HEADS*KERNEL),S(1,HEADS*KERNEL),S(4,D),S(1,FF),S(2,D)],
        scratch_shapes=[pltpu.VMEM((SMALL,ATT),f32)],
        cost_estimate=LIGHT,
        name="unpack_small")(*got)
    return [out[0],out[1],out[2],out[3].reshape(-1),out[4],out[5].reshape(-1),out[6]]


def digits(axis, size):
    out, bit = [], 1
    while bit < size:
        ways = 4 if size // bit % 4 == 0 else 2
        out.append((axis, size, [d * bit for d in range(ways)]))
        bit *= ways
    return out

def send_xor(x, stage, d):
    axis, size, xors = stage
    return lax.ppermute(x, axis, [(i, i ^ xors[d]) for i in range(size)])

def gather_send(x, stage, less=0):
    return [x] + [send_xor(x, stage, d) for d in range(1, len(stage[2]) - less)]

def gather_order(got, stage):
    axis, _, xors = stage
    ways = len(xors)
    mine = (lax.axis_index(axis) // xors[1]) % ways
    x = got[0]
    parts = []
    for place in range(ways):
        rel = mine ^ place
        part = got[0]
        for d in range(1, ways):
            part = jnp.where(rel == d, got[d], part)
        parts.append(part)
    return jnp.stack(parts, axis=1).reshape((x.shape[0] * ways,) + x.shape[1:])

def gather_near(got):
    return jnp.concatenate(got, axis=0)

def gather_stages(sizes):
    return digits("dp", sizes[0])[::-1] + digits("fsdp", sizes[1])[::-1]

def near_stages(sizes):
    ahead = gather_stages(sizes)
    return ahead, ahead[::-1]

def near_owners(sizes):
    nd, nf = sizes
    table = [0]
    for axis, _, xors in near_stages(sizes)[0]:
        step = nf if axis == "dp" else 1
        table = [x * step + t for x in xors for t in table]
    place = [0] * len(table)
    for i, t in enumerate(table):
        place[t] = i
    me = lax.axis_index("dp") * nf + lax.axis_index("fsdp")
    owners = jnp.asarray(table, jnp.int32) ^ me
    places = jnp.asarray(place, jnp.int32)[jnp.arange(nd * nf) ^ me]
    return owners, places

def scatter_send(g, stage):
    ways = len(stage[2])
    parts = g if isinstance(g, (list, tuple)) else jnp.split(g, ways, axis=0)
    return [parts[0]] + [send_xor(parts[d], stage, d) for d in range(1, ways)]

def scatter_total(got):
    total = got[0].astype(jnp.float32)
    for r in got[1:]:
        total = total + r.astype(jnp.float32)
    return total

def scatter_add(got):
    return scatter_total(got).astype(jnp.bfloat16)

def sum_send(x, stage):
    return [x] + [send_xor(x, stage, d) for d in range(1, len(stage[2]))]

def together(*arrays):
    return lax.optimization_barrier(arrays)


def body(
    tokens,
    segment_ids,
    cotangent,
    w_proj,
    w_point,
    w_out,
    w_up,
    w_down,
    proj_bias,
    conv_depth,
    kernel_weight,
    kernel_bias,
    hidden_bias,
    up_bias,
    norm_gain,
    *,
    sizes,
):
    rows, seq = segment_ids.shape
    nd, nf = sizes
    mid = FF // GROUPS
    shard_rows, ff_rows = D // (nd * nf), mid // (nd * nf)
    tok = tokens.reshape(rows * seq, D)
    cot = cotangent.reshape(rows * seq, D)

    ahead = gather_stages(sizes)
    owners, places = near_owners(sizes)
    first = jnp.concatenate([w_proj, w_point], axis=1).astype(bf16)[None]
    second = jnp.concatenate([jnp.swapaxes(w_up, 1, 2), w_down], axis=2).reshape(GROUPS * ff_rows, D)
    second = jnp.concatenate([second, w_out], axis=0).astype(bf16)[None]
    bounds = find_bounds(segment_ids)
    kernel_rows, kernel_shift = pack_kernel_weight(kernel_weight, kernel_bias)
    up_near = jnp.take(up_bias.reshape(GROUPS, nd * nf, ff_rows), owners, axis=1).reshape(1, FF)
    near, away = near_stages(sizes)
    direct = ff_rows % 16 == 0 and shard_rows % 8 == 0 and len(near) == 3 and sizes[1] == 2
    first = gather_order(gather_send(first, ahead[0]), ahead[0])
    first, second = together(first, second)
    got_first = gather_send(first, ahead[1])
    got_second = gather_send(second, near[0], 1)
    depth = depth_call(bounds, tok, conv_depth)
    *got_second, depth = together(*got_second, depth)
    got_second += gather_send(got_second[0], near[0])[len(got_second) :]
    *got_first, depth = together(*got_first, depth)
    first = gather_order(got_first, ahead[1])
    second = gather_near(got_second)
    got_second = gather_send(second, near[1])
    for stage in ahead[2:]:
        first = gather_order(gather_send(first, stage), stage)
    first = first.reshape(D, 5 * ATT)
    mixed, qkv, expo, recip, context, queries, key_conv, soft, bands, conv_in = mix_call(
        bounds, tok, depth, first, proj_bias, kernel_rows, kernel_shift
    )
    *got_second, mixed = together(*got_second, mixed)
    if direct:
        weights = got_second + [send_xor(piece, near[2], 1) for piece in got_second]
        weight_owners = owners
    else:
        second = gather_near(got_second)
        for stage in near[2:]:
            second = gather_near(gather_send(second, stage))
        ff_full = second[:, : GROUPS * ff_rows].reshape(nd * nf, GROUPS, ff_rows, D)
        ff_full = jnp.swapaxes(ff_full, 0, 1).reshape(GROUPS * mid, D)
        out_full = jnp.take(second[:, GROUPS * ff_rows :], places, axis=0).reshape(D, D)
        weights = [jnp.concatenate([ff_full, out_full], axis=0)[None]]
        weight_owners = jnp.zeros((1,), jnp.int32)
    layer_out, grad_one, grad_mixed, act, raised_low, first_low, two_low, one_low, norm_sums, up_sums = ff_call(
        weight_owners, weights, mixed, tok, cot, hidden_bias, up_near, norm_gain
    )

    if direct:
        parts = ffw_call(owners, act, raised_low, first_low, two_low, mixed, one_low, 2, shard_rows)
    else:
        halves = ffw_call(jnp.arange(2), act, raised_low, first_low, two_low, mixed, one_low, 2, D // 2)
        share = jnp.stack(halves)[:, 0]
        out_share = share[:, FF // 2 :].reshape(nd * nf, shard_rows, D)
        share = share[:, : FF // 2].reshape(2, GROUPS, nd * nf // 2, ff_rows, D).swapaxes(1, 2)
        share = share.reshape(nd * nf, GROUPS * ff_rows, D)
        share = jnp.concatenate([share, jnp.take(out_share, owners, axis=0)], axis=1)
        parts = jnp.split(share, len(away[0][2]), axis=0)
    *parts, grad_mixed = together(*parts, grad_mixed)
    got = scatter_send(parts, away[0])
    grad_key, query_part, conv_part, kw_sums, kb_sums, span_sums = span_back_call(
        bounds, grad_mixed, queries, key_conv, soft, bands, conv_in, kernel_rows[:LANES]
    )
    *got, query_part = together(*got, query_part)
    share = scatter_add(got)
    share, query_part = together(share, query_part)
    got = scatter_send(share, away[1])
    grad_proj, proj_sums = attend_back_call(bounds, grad_mixed, qkv, expo, recip, context, query_part, conv_part)
    few = max(rows // 4, 1)
    grad_key, grad_proj = together(grad_key, grad_proj)
    part_low, sums_low = depth_back_call(bounds, tok, grad_key, grad_one, first, conv_depth, 0, rows - few)
    *got, part_low, grad_proj = together(*got, part_low, grad_proj)
    share = scatter_add(got)
    for stage in away[2:-1]:
        share = scatter_add(scatter_send(share, stage))
    share, grad_proj = together(share, grad_proj)
    got_share = scatter_send(share, away[-1])
    if direct:
        parts = feature_weights_call(owners, tok, grad_proj, depth, grad_key, 2)
    else:
        halves = feature_weights_call(jnp.arange(2), tok, grad_proj, depth, grad_key, 2)
        late = jnp.concatenate(halves, axis=0).reshape(nd * nf, shard_rows, 5 * ATT)
        parts = jnp.split(jnp.take(late, owners, axis=0), len(away[0][2]), axis=0)
    tied = together(*got_share, *parts, grad_key)
    got_share, parts, grad_key = tied[: len(got_share)], tied[len(got_share) : -1], tied[-1]
    got = scatter_send(parts, away[0])
    part_high, sums_high = depth_back_call(
        bounds, tok, grad_key, grad_one, first, conv_depth, rows - few, few
    )
    *got, part_high, sums_high = together(*got, part_high, sums_high)
    share = scatter_add(got_share)[0].astype(f32)
    ff_share = share[: GROUPS * ff_rows].reshape(GROUPS, ff_rows, D)
    out_share = share[GROUPS * ff_rows :]
    late = scatter_add(got)

    up_sums = jnp.take(jnp.sum(up_sums, axis=0).reshape(GROUPS, nd * nf, ff_rows), places, axis=1)
    small = pack_call(
        proj_sums, span_sums, sums_low, sums_high, kw_sums, kb_sums, norm_sums, up_sums.reshape(FF // ATT, ATT)
    )
    late, small, part_high = together(late, small, part_high)
    got = scatter_send(late, away[1])
    small_got = sum_send(small, away[0])
    tokens_grad = input_call(grad_proj, part_low, part_high, first)
    *got, tokens_grad = together(*got, tokens_grad)
    *small_got, tokens_grad = together(*small_got, tokens_grad)
    late = scatter_add(got)
    small = scatter_add(small_got)
    for stage in away[2:-1]:
        late = scatter_add(scatter_send(late, stage))
    late, small = together(late, small)
    got = scatter_send(late, away[-1])
    for stage in away[1:-1]:
        small = scatter_add(sum_send(small, stage))
    smalls = unpack_call(sum_send(small, away[-1]))
    late = scatter_add(got)
    late = late[0].astype(f32)
    return (
        layer_out.reshape(rows, seq, D),
        tokens_grad.reshape(rows, seq, D),
        late[:, : 4 * ATT],
        late[:, 4 * ATT :],
        out_share,
        jnp.swapaxes(ff_share[..., : D // GROUPS], 1, 2),
        ff_share[..., D // GROUPS :],
        *smalls,
    )


def solution(mesh):
    whole, split = P(), ("dp", "fsdp")
    rows3, rows2 = P(split, None, None), P(split, None)
    up, down = P(None, None, split), P(None, split, None)
    return jax.shard_map(
        functools.partial(body, sizes=(mesh.shape["dp"], mesh.shape["fsdp"])),
        mesh=mesh,
        in_specs=(rows3, rows2, rows3, rows2, rows2, rows2, up, down) + (whole,) * 7,
        out_specs=(rows3, rows3, rows2, rows2, rows2, up, down) + (whole,) * 7,
        check_vma=False,
    )
```

```python
import functools

import jax
import jax.numpy as jnp
from jax import lax
from jax.experimental import pallas as pl
from jax.experimental.pallas import tpu as pltpu
from jax.sharding import PartitionSpec as P

f32=jnp.float32
bf16=jnp.bfloat16
D=768; FF=3072; HEADS=6; HEAD_DIM=64; KERNEL=9; GROUPS=2; ATT=384
norm_eps=1e-12
LIGHT=pl.CostEstimate(flops=1,bytes_accessed=1,transcendentals=0)
def dot(a,b): return lax.dot_general(a,b,(((1,),(0,)),((),())),preferred_element_type=f32)
def dot_t(a,b): return lax.dot_general(a,b,(((1,),(1,)),((),())),preferred_element_type=f32)
def dot_l(a,b): return lax.dot_general(a,b,(((0,),(0,)),((),())),preferred_element_type=f32)
def fold8(x):
    return jnp.sum(x.reshape(x.shape[0]//8,8,x.shape[1]),axis=0)
def row_mean(x): return jnp.sum(x,axis=-1,keepdims=True)*(1.0/x.shape[-1])

def ordered(kernel,lead,after):
    extra=len(after)
    return lambda *refs: kernel(*refs[:lead],*refs[lead+extra:])
def waits(after):
    return [pl.BlockSpec(memory_space=pl.ANY) for _ in after]

def gelu_parts(x):
    phi=0.5+0.5*lax.erf(x*0.7071067811865476)
    return x*phi, phi+x*(jnp.exp(x*x*-0.5)*0.3989422804014327)

CH=256
PARTS=2
LAG=0
def ff_kernel(pieces,own_ref,*refs):
    w_refs=refs[:pieces]
    (mixed_ref,tok_ref,cot_ref,hb_ref,ub_ref,gain_ref,
     out_ref,gone_ref,gmix_ref,act_ref,gr_ref,xlow_ref,g2low_ref,g1low_ref,sums_ref,ups_ref,
     dg_ref,wup_ref,wdn_ref,wide_ref,wout_ref,keep_ref)=refs[pieces:]
    half=D//GROUPS; mid=FF//GROUPS
    @pl.when(pl.program_id(0)==0)
    def _():
        sums_ref[...]=jnp.zeros_like(sums_ref); ups_ref[...]=jnp.zeros_like(ups_ref)
        at=0
        total=sum(w.shape[0] for w in w_refs)
        rows,share=mid//total,D//total
        for w_ref in w_refs:
            n=w_ref.shape[0]
            for g in range(GROUPS):
                span=slice(at*rows,(at+n)*rows); part=slice(g*rows,(g+1)*rows)
                wup_ref[g,span,:]=w_ref[:,part,0:half].reshape(n*rows,half)
                wdn_ref[g,span,:]=w_ref[:,part,half:].reshape(n*rows,half)
            for i in range(n):
                place=pl.multiple_of(own_ref[at+i]*share,8)
                wide_ref[pl.ds(place,share),:]=w_ref[i,GROUPS*rows:GROUPS*rows+share,:].astype(f32)
            at+=n
        wout_ref[...]=wide_ref[...].astype(bf16)
    spans=[(g,c,slice(g*mid+c,g*mid+c+CH)) for g in range(GROUPS) for c in range(0,mid,CH)]
    gain1,gain2=gain_ref[0:1,:],gain_ref[1:2,:]

    def tokens_part(rs):
        res=dot(mixed_ref[rs,:],wout_ref[...])
        yield
        res=res+hb_ref[0:1,:]+tok_ref[rs,:].astype(f32)
        mean=row_mean(res); cen=res-mean
        inv1=lax.rsqrt(row_mean(cen*cen)+norm_eps)
        n1=cen*inv1
        first=n1*gain1+hb_ref[1:2,:]
        xlow_ref[rs,:]=first.astype(bf16)
        gone_ref[rs,:]=n1
        yield
        def raise_(g,c,cs):
            return dot_t(xlow_ref[rs,g*half:(g+1)*half],wup_ref[g,c:c+CH,:])+ub_ref[0:1,cs]
        lows=[]
        ahead=raise_(*spans[0])
        for i,(g,c,cs) in enumerate(spans):
            raised=ahead
            if i+1<len(spans): ahead=raise_(*spans[i+1])
            yield
            a,dg=gelu_parts(raised)
            act_ref[rs,cs]=a.astype(bf16)
            dg_ref[rs,cs]=dg
            yield
            if c+CH==mid:
                lows.append(dot(act_ref[rs,g*mid:(g+1)*mid],wdn_ref[g]))
                yield
        n1=gone_ref[rs,:]
        res=jnp.concatenate(lows,axis=1)+hb_ref[2:3,:]+(n1*gain1+hb_ref[1:2,:])
        mean=row_mean(res); cen=res-mean
        inv2=lax.rsqrt(row_mean(cen*cen)+norm_eps)
        n2=cen*inv2
        out_ref[rs,:]=(n2*gain2+hb_ref[3:4,:]).astype(bf16)
        yield
        e=cot_ref[rs,:].astype(f32)
        eg=e*gain2
        g2=inv2*(eg-row_mean(eg)-n2*row_mean(eg*n2))
        sums_ref[3]+=fold8(e); sums_ref[5]+=fold8(e*n2); sums_ref[2]+=fold8(g2)
        g2low_ref[rs,:]=g2.astype(bf16)
        keep_ref[rs,:]=g2
        yield
        def fall(g,c,cs):
            return dot_t(g2low_ref[rs,g*half:(g+1)*half],wdn_ref[g,c:c+CH,:])
        parts=[]
        ahead=fall(*spans[0])
        for i,(g,c,cs) in enumerate(spans):
            ga=ahead
            if i+1<len(spans): ahead=fall(*spans[i+1])
            yield
            gr=ga*dg_ref[rs,cs]
            ups_ref[:,cs]+=fold8(gr)
            gr_ref[rs,cs]=gr.astype(bf16)
            yield
            if c+CH==mid:
                parts.append(dot(gr_ref[rs,g*mid:(g+1)*mid],wup_ref[g]))
                yield
        gf=jnp.concatenate(parts,axis=1)+keep_ref[rs,:]
        n1=gone_ref[rs,:]
        sums_ref[1]+=fold8(gf); sums_ref[4]+=fold8(gf*n1)
        yield
        eg=gf*gain1
        g1=inv1*(eg-row_mean(eg)-n1*row_mean(eg*n1))
        sums_ref[0]+=fold8(g1)
        gone_ref[rs,:]=g1
        g1low_ref[rs,:]=g1.astype(bf16)
        yield
        gmix_ref[rs,:]=dot_t(g1low_ref[rs,:],wout_ref[...]).astype(bf16)
    total=mixed_ref.shape[0]; piece=total//PARTS
    running=[tokens_part(slice(i*piece,(i+1)*piece)) for i in range(PARTS)]
    waiting=[i*LAG for i in range(PARTS)]
    while any(part is not None for part in running):
        for i,part in enumerate(running):
            if waiting[i]>0:
                waiting[i]-=1
            elif part is not None and next(part,StopIteration) is StopIteration:
                running[i]=None

def ff_call(owners,weights,mixed,tok,cot,hb,ub,gain,T=512,after=()):
    n=tok.shape[0]
    row=lambda w,:pl.BlockSpec((T,w),lambda i,o:(i,0))
    full=lambda s:pl.BlockSpec(s,lambda i,o:(0,)*len(s),pipeline_mode=pl.Buffered(1))
    S=lambda s,d:jax.ShapeDtypeStruct(s,d)
    W=(GROUPS,FF//GROUPS,D//GROUPS)
    return pl.pallas_call(ordered(functools.partial(ff_kernel,len(weights)),7+len(weights),after),
        grid_spec=pltpu.PrefetchScalarGridSpec(num_scalar_prefetch=1,grid=(n//T,),
        in_specs=[full(w.shape) for w in weights]+[row(D),row(D),row(D),full((4,D)),full((1,FF)),full((2,D))]+waits(after),
        out_specs=[row(D),row(D),row(D),row(FF),row(FF),row(D),row(D),row(D),full((6,8,D)),full((8,FF))],
        scratch_shapes=[pltpu.VMEM((T,FF),f32),pltpu.VMEM(W,bf16),pltpu.VMEM(W,bf16),pltpu.VMEM((D,D),f32),pltpu.VMEM((D,D),bf16),pltpu.VMEM((T,D),f32)]),
        out_shape=[S((n,D),bf16),S((n,D),f32),S((n,D),bf16),S((n,FF),bf16),S((n,FF),bf16),S((n,D),bf16),S((n,D),bf16),S((n,D),bf16),S((6,8,D),f32),S((8,FF),f32)],
        compiler_params=pltpu.CompilerParams(vmem_limit_bytes=60<<20),
        cost_estimate=LIGHT,
        name="feed_forward",
    )(owners,*weights,mixed,tok,cot,hb,ub,gain,*after)

def fetch(pairs,sems):
    copies=[pltpu.make_async_copy(src,dst,sems.at[i]) for i,(src,dst) in enumerate(pairs)]
    for copy in copies: copy.start()
    return copies
def by_owner(own_ref,wide_ref,width,outs,rows,columns):
    per=outs[0].shape[0]; share=rows.stop-rows.start
    for p,out in enumerate(outs):
        for i in range(per):
            place=pl.multiple_of(own_ref[p*per+i]*share,8)
            out[i,rows,columns]=wide_ref[pl.ds(place,share),0:width].astype(bf16)

def ffw_kernel(parts,share,own_ref,act_ref,gr_ref,xlow_ref,g2low_ref,mix_ref,g1_ref,*refs):
    outs=refs[:parts]
    act,gr,xlow,g2low,mix,g1,wide,sems=refs[parts:parts+8]
    blocks=refs[parts+8:parts+8+parts]
    out_sem=refs[-1]
    half=D//GROUPS; mid=FF//GROUPS; C=mid//parts
    rows=(blocks[0].shape[1]-share)//GROUPS
    jobs=[(p,g) for p in range(parts) for g in range(GROUPS)]
    cols=[slice(g*mid+p*C,g*mid+(p+1)*C) for p,g in jobs]
    pairs=[(xlow_ref,xlow)]+[(gr_ref.at[:,cols[0]],gr.at[0]),(g2low_ref,g2low),(act_ref.at[:,cols[0]],act.at[0])]
    for j in range(1,len(jobs)):
        pairs+=[(gr_ref.at[:,cols[j]],gr.at[j]),(act_ref.at[:,cols[j]],act.at[j])]
    pairs+=[(mix_ref,mix),(g1_ref,g1)]
    copies=fetch(pairs,sems)
    per=blocks[0].shape[0]
    for j,(p,g) in enumerate(jobs):
        gs=slice(g*half,(g+1)*half); rs=slice(g*rows,(g+1)*rows)
        if j==0: copies[0].wait()
        copies[1 if j==0 else 2+2*j].wait()
        blocks[p][:,rs,0:half]=dot_l(xlow[:,gs],gr[j]).T.astype(bf16).reshape(per,rows,half)
        if j==0: copies[2].wait()
        copies[3+2*j].wait()
        blocks[p][:,rs,half:]=dot_l(g2low[:,gs],act[j]).T.astype(bf16).reshape(per,rows,half)
    copies[-2].wait(); copies[-1].wait()
    wide[...]=dot_l(mix[...],g1[...])
    by_owner(own_ref,wide,D,blocks,slice(GROUPS*rows,GROUPS*rows+share),slice(0,D))
    done=fetch([(blocks[p],outs[p]) for p in range(parts)],out_sem)
    for copy in done: copy.wait()
def ffw_call(owners,act,gr,xlow,g2low,mixed,g1,parts,share,after=()):
    n=act.shape[0]; blocks=owners.shape[0]; mid=FF//GROUPS; C=mid//parts
    shape=(blocks//parts,FF//blocks+share,D)
    any_=pl.BlockSpec(memory_space=pl.ANY)
    jobs=parts*GROUPS
    return pl.pallas_call(ordered(functools.partial(ffw_kernel,parts,share),7,after),
        grid_spec=pltpu.PrefetchScalarGridSpec(num_scalar_prefetch=1,grid=(1,),
        in_specs=[any_]*6+waits(after),out_specs=[any_]*parts,
        scratch_shapes=[pltpu.VMEM((jobs,n,C),bf16)]*2+[pltpu.VMEM((n,D),bf16)]*4+[pltpu.VMEM((D,D),f32),pltpu.SemaphoreType.DMA((2*jobs+4,))]
            +[pltpu.VMEM(shape,bf16)]*parts+[pltpu.SemaphoreType.DMA((parts,))]),
        out_shape=[jax.ShapeDtypeStruct(shape,bf16)]*parts,
        compiler_params=pltpu.CompilerParams(vmem_limit_bytes=60<<20),
        cost_estimate=LIGHT,
        name="feed_forward_weights",
    )(owners,act,gr,xlow,g2low,mixed,g1,*after)

def feature_weights_kernel(parts,own_ref,tok_ref,gp_ref,dep_ref,gk_ref,*refs):
    outs=refs[:parts]
    tok,gp,dep,gk,wide,sems=refs[parts:parts+6]
    blocks=refs[parts+6:parts+6+parts]
    out_sem=refs[-1]
    copies=fetch([(gk_ref,gk),(dep_ref,dep),(tok_ref,tok),(gp_ref.at[:,0:2*ATT],gp.at[0]),(gp_ref.at[:,2*ATT:],gp.at[1])],sems)
    rows=slice(0,blocks[0].shape[1])
    copies[0].wait(); copies[1].wait()
    wide[:,0:ATT]=dot_l(dep[...],gk[...])
    by_owner(own_ref,wide,ATT,blocks,rows,slice(4*ATT,5*ATT))
    copies[2].wait()
    for j in range(2):
        copies[3+j].wait()
        wide[...]=dot_l(tok[...],gp[j])
        by_owner(own_ref,wide,D,blocks,rows,slice(j*D,(j+1)*D))
    done=fetch([(blocks[p],outs[p]) for p in range(parts)],out_sem)
    for copy in done: copy.wait()
def feature_weights_call(owners,tok,gp,dep,gk,parts,after=()):
    n=tok.shape[0]; blocks=owners.shape[0]
    shape=(blocks//parts,D//blocks,5*ATT)
    any_=pl.BlockSpec(memory_space=pl.ANY)
    return pl.pallas_call(ordered(functools.partial(feature_weights_kernel,parts),5,after),
        grid_spec=pltpu.PrefetchScalarGridSpec(num_scalar_prefetch=1,grid=(1,),
        in_specs=[any_]*4+waits(after),out_specs=[any_]*parts,
        scratch_shapes=[pltpu.VMEM((n,D),bf16),pltpu.VMEM((2,n,2*ATT),bf16),pltpu.VMEM((n,D),bf16),pltpu.VMEM((n,ATT),bf16),pltpu.VMEM((D,D),f32),pltpu.SemaphoreType.DMA((5,))]
            +[pltpu.VMEM(shape,bf16)]*parts+[pltpu.SemaphoreType.DMA((parts,))]),
        out_shape=[jax.ShapeDtypeStruct(shape,bf16)]*parts,
        compiler_params=pltpu.CompilerParams(vmem_limit_bytes=60<<20),
        cost_estimate=LIGHT,
        name="feature_weights",
    )(owners,tok,gp,dep,gk,*after)

TAPS=16
LANES=HEADS*TAPS
BT=64
LEAD=16
SLOT=4
HALF=256
SEQ=512
NEG=-1000000000.0

def doc_of(pos,b_ref,first=0):
    row=pl.program_id(0)+first
    return ((pos>=b_ref[row,0]).astype(jnp.int32)+(pos>=b_ref[row,1]).astype(jnp.int32)+(pos>=b_ref[row,2]).astype(jnp.int32))
def tap_valid_t(b_ref):
    tap=lax.broadcasted_iota(jnp.int32,(TAPS,SEQ),0); t=lax.broadcasted_iota(jnp.int32,(TAPS,SEQ),1)
    u=t+tap-KERNEL//2-SLOT
    ok=(u>=0)&(u<SEQ)&(doc_of(u,b_ref)==doc_of(t,b_ref))&(tap>=SLOT)&(tap<SLOT+KERNEL)
    return ok.astype(f32)
def roll_matrix(b_ref,back):
    start=b_ref[pl.program_id(0),3]
    a=lax.broadcasted_iota(jnp.int32,(SEQ,SEQ),1 if back else 0); t=lax.broadcasted_iota(jnp.int32,(SEQ,SEQ),0 if back else 1)
    d=a+start-t
    return jnp.where((d==0)|(d==SEQ),1.0,0.0).astype(bf16)
def head_lanes(shape,h):
    lane=lax.broadcasted_iota(jnp.int32,shape,len(shape)-1)
    return (lane<HEAD_DIM) if h==0 else (lane>=HEAD_DIM)
def keep_head(x,h):
    return jnp.where(head_lanes(x.shape,h),x,jnp.zeros_like(x))

BAND=128
def tap_bands(b_ref,r,first=0):
    lo=min(max(r-BAND//2,0),SEQ-2*BAND)
    row=lax.broadcasted_iota(jnp.int32,(BAND,2*BAND),0)+r; col=lax.broadcasted_iota(jnp.int32,(BAND,2*BAND),1)+lo
    step=jnp.where(doc_of(row,b_ref,first)==doc_of(col,b_ref,first),col-row,SEQ)
    return lo,[jnp.where(step==j-KERNEL//2,1.0,0.0).astype(bf16) for j in range(KERNEL)]

def depth_kernel(b_ref,tok_ref,cd_ref,out_ref):
    side=[j for j in range(KERNEL) if j!=KERNEL//2]
    for r in range(0,SEQ,BAND):
        lo,bands=tap_bands(b_ref,r)
        stack=jnp.concatenate([bands[j] for j in side],axis=0)
        for c in range(0,D,256):
            cs=slice(c,c+256)
            moved=dot(stack,tok_ref[lo:lo+2*BAND,cs])
            acc=tok_ref[r:r+BAND,cs].astype(f32)*cd_ref[KERNEL//2:KERNEL//2+1,cs]
            for i,j in enumerate(side):
                acc=acc+moved[i*BAND:(i+1)*BAND]*cd_ref[j:j+1,cs]
            out_ref[r:r+BAND,cs]=acc.astype(bf16)
def depth_call(bounds,tok,cd):
    n=tok.shape[0]
    row=pl.BlockSpec((SEQ,D),lambda i,b:(i,0))
    return pl.pallas_call(depth_kernel,
        grid_spec=pltpu.PrefetchScalarGridSpec(num_scalar_prefetch=1,grid=(n//SEQ,),
        in_specs=[row,pl.BlockSpec((KERNEL,D),lambda i,b:(0,0))],
        out_specs=row),
        out_shape=jax.ShapeDtypeStruct((n,D),bf16),
        compiler_params=pltpu.CompilerParams(vmem_limit_bytes=60<<20),
        cost_estimate=LIGHT,
        name="depth_taps")(bounds,tok,cd)

def mix_kernel(b_ref,tok_ref,dep_ref,w_ref,pb_ref,kw_ref,kb_ref,
               mixed_ref,qkv_ref,e_ref,r_ref,ctx_ref,q_ref,kc_ref,ks_ref,band_ref,cin_ref):
    tok=tok_ref[...]
    p=dot(tok,w_ref[:,0:4*ATT])
    q=(p[:,0:ATT]+pb_ref[0:1,:]).astype(bf16)
    k=p[:,ATT:2*ATT].astype(bf16)
    v=(p[:,2*ATT:3*ATT]+pb_ref[1:2,:]).astype(bf16)
    cin=(p[:,3*ATT:]+pb_ref[2:3,:]).astype(bf16)
    q_ref[...]=q
    rolled=dot(roll_matrix(b_ref,False),jnp.concatenate([q*jnp.bfloat16(0.125),k,v],axis=1)).astype(bf16)
    qkv_ref[...]=rolled
    key_conv=dot(dep_ref[...],w_ref[:,4*ATT:])+pb_ref[3:4,:]
    kc_ref[...]=key_conv
    attn=key_conv*q.astype(f32)
    hi=attn.astype(bf16); lo=(attn-hi.astype(f32)).astype(bf16)
    both=dot_t(kw_ref[...],hi)
    logits=both[:LANES]+both[LANES:]+dot_t(kw_ref[0:LANES,:],lo)+kb_ref[...]
    logits=logits.reshape(HEADS,TAPS,SEQ)
    tap=lax.broadcasted_iota(jnp.int32,(HEADS,TAPS,SEQ),1)
    logits=jnp.where((tap>=SLOT)&(tap<SLOT+KERNEL),logits,-1e30)
    ex=jnp.exp(logits-jnp.max(logits,axis=1,keepdims=True))
    ks=ex/jnp.sum(ex,axis=1,keepdims=True)
    ks_ref[...]=ks.reshape(LANES,SEQ)
    km=(ks*tap_valid_t(b_ref)[None]).reshape(LANES,SEQ)
    km=jnp.concatenate([km,jnp.zeros((128-LANES,SEQ),f32)],axis=0).T
    cin_ref[0:LEAD,:]=jnp.zeros((LEAD,ATT),bf16); cin_ref[LEAD+SEQ:,:]=jnp.zeros((128-LEAD-BT,ATT),bf16)
    cin_ref[LEAD:LEAD+SEQ,:]=cin
    row=lax.broadcasted_iota(jnp.int32,(BT,128),0); lane=lax.broadcasted_iota(jnp.int32,(BT,128),1)
    off=lane-row-(LEAD-KERNEL//2)
    on_band=(off>=0)&(off<KERNEL)
    for i in range(SEQ//BT):
        kmi=km[i*BT:(i+1)*BT,:]
        bands=[]
        for h in range(HEADS):
            x=pltpu.roll(kmi,(LEAD-KERNEL//2-SLOT-h*TAPS)%128,1,stride=1,stride_axis=0)
            x=jnp.where(on_band,x,0.0).astype(bf16)
            band_ref[i,h]=x
            bands.append(x)
        for pr in range(HEADS//2):
            win=cin_ref[i*BT:i*BT+128,pr*128:(pr+1)*128]
            o=dot(jnp.concatenate(bands[2*pr:2*pr+2],axis=1),jnp.concatenate([keep_head(win,0),keep_head(win,1)],axis=0))
            mixed_ref[i*BT:(i+1)*BT,ATT+pr*128:ATT+(pr+1)*128]=o.astype(bf16)
    start=b_ref[pl.program_id(0),3]
    def rolled_doc(axis):
        t=lax.broadcasted_iota(jnp.int32,(HALF,HALF),axis)+start+HALF
        return doc_of(jnp.where(t>=SEQ,t-SEQ,t),b_ref)
    same=rolled_doc(0)==rolled_doc(1)
    ones=jnp.ones((HALF,128),bf16)
    for a in range(2):
        rs=slice(a*HALF,(a+1)*HALF)
        for pr in range(HEADS//2):
            Q=rolled[rs,pr*128:(pr+1)*128]; K=rolled[rs,ATT+pr*128:ATT+(pr+1)*128]; V=rolled[rs,2*ATT+pr*128:2*ATT+(pr+1)*128]
            es=[];vs=[]
            both=dot_t(Q,jnp.concatenate([keep_head(K,0),keep_head(K,1)],axis=0))
            for h in range(2):
                s=both[:,h*HALF:(h+1)*HALF]
                if a==1: s=jnp.where(same,s,NEG)
                e=jnp.exp(s-jnp.max(s,axis=-1,keepdims=True)).astype(bf16)
                e_ref[a,2*pr+h]=e
                es.append(e); vs.append(jnp.concatenate([keep_head(V,h),keep_head(ones,h)],axis=1))
            o=dot(jnp.concatenate(es,axis=1),jnp.concatenate(vs,axis=0))
            r=1.0/o[:,128:]
            r_ref[rs,pr*128:(pr+1)*128]=r
            ctx_ref[rs,pr*128:(pr+1)*128]=(o[:,:128]*r).astype(bf16)
    mixed_ref[:,0:ATT]=dot(roll_matrix(b_ref,True),ctx_ref[...]).astype(bf16)

CPAD=SEQ+128-BT
def mix_call(bounds,tok,dep,w,pb,kw,kb,after=()):
    n=tok.shape[0]; R=n//SEQ
    row=lambda w_:pl.BlockSpec((SEQ,w_),lambda i,b:(i,0))
    full=lambda s:pl.BlockSpec(s,lambda i,b:(0,)*len(s))
    lead=lambda s:pl.BlockSpec((None,)+s,lambda i,b:(i,)+(0,)*len(s))
    S=lambda s,d:jax.ShapeDtypeStruct(s,d)
    NT=SEQ//BT
    return pl.pallas_call(ordered(mix_kernel,7,after),
        grid_spec=pltpu.PrefetchScalarGridSpec(num_scalar_prefetch=1,grid=(R,),
        in_specs=[row(D),row(D),full((D,5*ATT)),full((4,ATT)),full((2*LANES,ATT)),full((LANES,1))]+waits(after),
        out_specs=[row(D),row(3*ATT),lead((2,HEADS,HALF,HALF)),row(ATT),row(ATT),row(ATT),row(ATT),lead((LANES,SEQ)),lead((NT,HEADS,BT,128)),lead((CPAD,ATT))]),
        out_shape=[S((n,D),bf16),S((n,3*ATT),bf16),S((R,2,HEADS,HALF,HALF),bf16),S((n,ATT),f32),S((n,ATT),bf16),S((n,ATT),bf16),S((n,ATT),f32),S((R,LANES,SEQ),f32),S((R,NT,HEADS,BT,128),bf16),S((R,CPAD,ATT),bf16)],
        compiler_params=pltpu.CompilerParams(vmem_limit_bytes=60<<20),
        cost_estimate=LIGHT,
        name="attend_and_span")(bounds,tok,dep,w,pb,kw,kb,*after)


def pack_kernel_weight(kw,kb):
    k=kw.T.reshape(HEADS,KERNEL,ATT)
    k=jnp.pad(k,((0,0),(SLOT,TAPS-KERNEL-SLOT),(0,0))).reshape(LANES,ATT)
    hi=lax.reduce_precision(k,8,7); lo=(k-hi).astype(bf16); hi=hi.astype(bf16)
    b=jnp.pad(kb.reshape(HEADS,KERNEL),((0,0),(SLOT,TAPS-KERNEL-SLOT))).reshape(LANES,1)
    return jnp.concatenate([hi,lo],axis=0),b

def find_bounds(seg):
    counts=jnp.stack([jnp.sum(seg==i,axis=1) for i in range(4)],axis=1)
    begin=jnp.cumsum(counts,axis=1)-counts
    which=jnp.argmax(counts==HALF,axis=1)
    start=jnp.take_along_axis(begin,which[:,None],axis=1)
    return jnp.concatenate([begin[:,1:],start],axis=1).astype(jnp.int32)

def span_back_kernel(b_ref,gm_ref,q_ref,kc_ref,ks_ref,band_ref,cin_ref,kwt_ref,
                gk_ref,gqc_ref,gci_ref,kwg_ref,kbg_ref,pbg_ref,gcin_ref,anti_ref):
    @pl.when(pl.program_id(0)==0)
    def _():
        anti=lax.broadcasted_iota(jnp.int32,(SEQ,SEQ),0)+lax.broadcasted_iota(jnp.int32,(SEQ,SEQ),1)
        anti_ref[...]=jnp.where(anti==SEQ-1,1.0,0.0).astype(bf16)
        kwg_ref[...]=jnp.zeros_like(kwg_ref); kbg_ref[...]=jnp.zeros_like(kbg_ref); pbg_ref[...]=jnp.zeros_like(pbg_ref)
    gcin_ref[...]=jnp.zeros_like(gcin_ref)
    lane=lax.broadcasted_iota(jnp.int32,(BT,128),1)
    anti=anti_ref[...]
    falling=dot(anti,gm_ref[:,ATT:]).astype(bf16)
    logits=[]
    for i in range(SEQ//BT):
        acc=None
        f=SEQ//BT-1-i
        for pr in range(HEADS//2):
            g=gm_ref[i*BT:(i+1)*BT,ATT+pr*128:ATT+(pr+1)*128]
            gf=falling[i*BT:(i+1)*BT,pr*128:(pr+1)*128]
            win=cin_ref[f*BT:f*BT+128,pr*128:(pr+1)*128]
            both=dot_t(jnp.concatenate([keep_head(gf,0),keep_head(gf,1)],axis=0),win)
            for h in range(2):
                head=2*pr+h
                d=pltpu.roll(both[h*BT:(h+1)*BT],(head*TAPS+SLOT-LEAD+KERNEL//2-BT+1)%128,1,stride=1,stride_axis=0)
                d=jnp.where((lane>=head*TAPS+SLOT)&(lane<head*TAPS+SLOT+KERNEL),d,0.0)
                acc=d if acc is None else acc+d
            bands=jnp.concatenate([band_ref[i,2*pr],band_ref[i,2*pr+1]],axis=0)
            gcin_ref[i*BT:i*BT+128,pr*128:(pr+1)*128]+=dot_l(bands,jnp.concatenate([keep_head(g,0),keep_head(g,1)],axis=0))
        logits.append(acc)
    gk=jnp.concatenate(logits,axis=0)
    gh=gk.astype(bf16); glo=(gk-gh.astype(f32)).astype(bf16)
    gk=(dot_l(gh,anti)+dot_l(glo,anti))[0:LANES,:].reshape(HEADS,TAPS,SEQ)*tap_valid_t(b_ref)[None]
    ks=ks_ref[...].reshape(HEADS,TAPS,SEQ)
    gl=(ks*(gk-jnp.sum(gk*ks,axis=1,keepdims=True))).reshape(LANES,SEQ)
    kbg_ref[...]+=gl[:,0:128]+gl[:,128:256]+gl[:,256:384]+gl[:,384:512]
    q=q_ref[...].astype(f32); kc=kc_ref[...]
    attn=kc*q
    hi=attn.astype(bf16)
    glb=gl.astype(bf16)
    kwg_ref[...]+=dot(glb,hi)
    gattn=dot_l(glb,kwt_ref[...])
    gkc=gattn*q
    gk_ref[...]=gkc.astype(bf16)
    pbg_ref[1]+=fold8(gkc)
    gqc_ref[...]=gattn*kc
    gci=gcin_ref[LEAD:LEAD+SEQ,:]
    pbg_ref[0]+=fold8(gci)
    gci_ref[...]=gci.astype(bf16)

def attend_back_kernel(b_ref,gm_ref,qkv_ref,e_ref,r_ref,ctx_ref,gqc_ref,gci_ref,gp_ref,pbg_ref,dr_ref):
    @pl.when(pl.program_id(0)==0)
    def _(): pbg_ref[...]=jnp.zeros_like(pbg_ref)
    dor=(dot(roll_matrix(b_ref,False),gm_ref[:,0:ATT])*r_ref[...])
    dol=dor.astype(bf16)
    prod=(dol.astype(f32)*ctx_ref[...].astype(f32)).astype(bf16)
    minus=jnp.full((HALF,128),-1.0,bf16)
    minus=jnp.concatenate([keep_head(minus,0),keep_head(minus,1)],axis=0)
    def heads(x): return jnp.concatenate([keep_head(x,0),keep_head(x,1)],axis=0)
    for a in range(2):
        rs=slice(a*HALF,(a+1)*HALF)
        for pr in range(HEADS//2):
            cs=slice(pr*128,(pr+1)*128)
            Q=qkv_ref[rs,pr*128:(pr+1)*128]; K=qkv_ref[rs,ATT+pr*128:ATT+(pr+1)*128]; V=qkv_ref[rs,2*ATT+pr*128:2*ATT+(pr+1)*128]
            G=dol[rs,cs]
            dp=dot_t(jnp.concatenate([G,prod[rs,cs]],axis=1),jnp.concatenate([heads(V),minus],axis=1))
            es=[e_ref[a,2*pr+h] for h in range(2)]
            ds=[(es[h].astype(f32)*dp[:,h*HALF:(h+1)*HALF]).astype(bf16) for h in range(2)]
            dq=dot(jnp.concatenate(ds,axis=1),heads(K))*0.125
            dk=dot_l(jnp.concatenate(ds,axis=0),heads(Q))
            dv=dot_l(jnp.concatenate(es,axis=0),heads(G))
            dr_ref[rs,cs]=dq.astype(bf16)
            dr_ref[rs,ATT+pr*128:ATT+(pr+1)*128]=dk.astype(bf16)
            dr_ref[rs,2*ATT+pr*128:2*ATT+(pr+1)*128]=dv.astype(bf16)
    un=dot(roll_matrix(b_ref,True),dr_ref[...])
    gq=un[:,0:ATT]+gqc_ref[...]
    pbg_ref[0]+=fold8(gq); pbg_ref[1]+=fold8(un[:,2*ATT:])
    gp_ref[:,0:ATT]=gq.astype(bf16)
    gp_ref[:,ATT:3*ATT]=un[:,ATT:].astype(bf16)
    gp_ref[:,3*ATT:]=gci_ref[...]

def span_back_call(bounds,gm,q,kc,ks,band,cin,kwt,after=()):
    n=gm.shape[0]; R=n//SEQ; NT=SEQ//BT
    row=lambda w_:pl.BlockSpec((SEQ,w_),lambda i,b:(i,0))
    full=lambda s:pl.BlockSpec(s,lambda i,b:(0,)*len(s))
    lead=lambda s:pl.BlockSpec((None,)+s,lambda i,b:(i,)+(0,)*len(s))
    S=lambda s,d:jax.ShapeDtypeStruct(s,d)
    return pl.pallas_call(ordered(span_back_kernel,8,after),
        grid_spec=pltpu.PrefetchScalarGridSpec(num_scalar_prefetch=1,grid=(R,),
        in_specs=[row(D),row(ATT),row(ATT),lead((LANES,SEQ)),lead((NT,HEADS,BT,128)),lead((CPAD,ATT)),full((LANES,ATT))]+waits(after),
        out_specs=[row(ATT),row(ATT),row(ATT),full((LANES,ATT)),full((LANES,128)),full((2,8,ATT))],
        scratch_shapes=[pltpu.VMEM((CPAD,ATT),f32),pltpu.VMEM((SEQ,SEQ),bf16)]),
        out_shape=[S((n,ATT),bf16),S((n,ATT),f32),S((n,ATT),bf16),S((LANES,ATT),f32),S((LANES,128),f32),S((2,8,ATT),f32)],
        compiler_params=pltpu.CompilerParams(vmem_limit_bytes=60<<20),
        cost_estimate=LIGHT,
        name="span_back")(bounds,gm,q,kc,ks,band,cin,kwt,*after)
def attend_back_call(bounds,gm,qkv,E,r,ctx,gqc,gci,after=()):
    n=gm.shape[0]; R=n//SEQ
    row=lambda w_:pl.BlockSpec((SEQ,w_),lambda i,b:(i,0))
    full=lambda s:pl.BlockSpec(s,lambda i,b:(0,)*len(s))
    lead=lambda s:pl.BlockSpec((None,)+s,lambda i,b:(i,)+(0,)*len(s))
    S=lambda s,d:jax.ShapeDtypeStruct(s,d)
    return pl.pallas_call(ordered(attend_back_kernel,8,after),
        grid_spec=pltpu.PrefetchScalarGridSpec(num_scalar_prefetch=1,grid=(R,),
        in_specs=[row(D),row(3*ATT),lead((2,HEADS,HALF,HALF)),row(ATT),row(ATT),row(ATT),row(ATT)]+waits(after),
        out_specs=[row(4*ATT),full((2,8,ATT))],
        scratch_shapes=[pltpu.VMEM((SEQ,3*ATT),bf16)]),
        out_shape=[S((n,4*ATT),bf16),S((2,8,ATT),f32)],
        compiler_params=pltpu.CompilerParams(vmem_limit_bytes=60<<20),
        cost_estimate=LIGHT,
        name="attend_back")(bounds,gm,qkv,E,r,ctx,gqc,gci,*after)

def depth_back_kernel(b_ref,tok_ref,gk_ref,gone_ref,w_ref,cd_ref,out_ref,cdg_ref,gd_ref):
    @pl.when(pl.program_id(0)==0)
    def _(): cdg_ref[...]=jnp.zeros_like(cdg_ref)
    gd_ref[...]=dot_t(gk_ref[...],w_ref[...]).astype(bf16)
    side=[j for j in range(KERNEL) if j!=KERNEL//2]
    for r in range(0,SEQ,BAND):
        lo,bands=tap_bands(b_ref,r)
        stack=jnp.concatenate([bands[j] for j in side],axis=0)
        for c in range(0,D,256):
            cs=slice(c,c+256)
            x=tok_ref[r:r+BAND,cs].astype(f32)
            moved=dot(stack,gd_ref[lo:lo+2*BAND,cs])
            acc=gone_ref[r:r+BAND,cs]
            for j in range(KERNEL):
                m=KERNEL-1-j
                if j==KERNEL//2:
                    v=gd_ref[r:r+BAND,cs].astype(f32)
                else:
                    i=side.index(j)
                    v=moved[i*BAND:(i+1)*BAND]
                acc=acc+v*cd_ref[m:m+1,cs]
                cdg_ref[m,:,cs]+=fold8(v*x)
            out_ref[r:r+BAND,cs]=acc
def depth_back_call(bounds,tok,gk,gone,w,cd,after=()):
    n=tok.shape[0]
    row=lambda w_:pl.BlockSpec((SEQ,w_),lambda i,b:(i,0))
    full=lambda s:pl.BlockSpec(s,lambda i,b:(0,)*len(s))
    S=lambda s,d:jax.ShapeDtypeStruct(s,d)
    return pl.pallas_call(ordered(depth_back_kernel,6,after),
        grid_spec=pltpu.PrefetchScalarGridSpec(num_scalar_prefetch=1,grid=(n//SEQ,),
        in_specs=[row(D),row(ATT),row(D),pl.BlockSpec((D,ATT),lambda i,b:(0,4)),full((KERNEL,D))]+waits(after),
        out_specs=[row(D),full((KERNEL,8,D))],
        scratch_shapes=[pltpu.VMEM((SEQ,D),bf16)]),
        out_shape=[S((n,D),f32),S((KERNEL,8,D),f32)],
        compiler_params=pltpu.CompilerParams(vmem_limit_bytes=60<<20),
        cost_estimate=LIGHT,
        name="depth_taps_back")(bounds,tok,gk,gone,w,cd,*after)
def input_kernel(gp_ref,part_ref,w_ref,out_ref):
    out_ref[...]=part_ref[...]+dot_t(gp_ref[...],w_ref[...])
def input_call(gp,part,w,first,rows,into=None):
    n=gp.shape[0]
    row=lambda w_:pl.BlockSpec((SEQ,w_),lambda i:(i+first,0))
    extra=() if into is None else (into,)
    return pl.pallas_call(ordered(input_kernel,3,extra),grid=(rows,),
        in_specs=[row(4*ATT),row(D),pl.BlockSpec((D,4*ATT),lambda i:(0,0))]+waits(extra),
        out_specs=row(D),
        out_shape=jax.ShapeDtypeStruct((n,D),f32),
        input_output_aliases={} if into is None else {3:0},
        compiler_params=pltpu.CompilerParams(vmem_limit_bytes=60<<20),
        cost_estimate=LIGHT,
        name="input_grad")(gp,part,w,*extra)

SMALL=112
def pack_kernel(att_ref,span_ref,low_ref,kw_ref,kb_ref,norm_ref,up_ref,out_ref,wide_ref):
    wide_ref[...]=jnp.zeros_like(wide_ref)
    wide_ref[0:2,:]=jnp.sum(att_ref[...],axis=1)
    wide_ref[2:4,:]=jnp.sum(span_ref[...],axis=1)
    taps=jnp.sum(low_ref[...],axis=1)
    wide_ref[4:13,:]=taps[:,0:ATT]
    wide_ref[13:22,:]=taps[:,ATT:]
    for h in range(HEADS):
        wide_ref[22+h*KERNEL:22+(h+1)*KERNEL,:]=kw_ref[h*TAPS+SLOT:h*TAPS+SLOT+KERNEL,:]
    norms=jnp.sum(norm_ref[...],axis=1)
    wide_ref[76:82,:]=norms[:,0:ATT]
    wide_ref[82:88,:]=norms[:,ATT:]
    wide_ref[88:96,:]=up_ref[...]
    kb=jnp.concatenate([kb_ref[...],jnp.zeros((128-LANES,128),f32)],axis=0).T
    wide_ref[96:97,0:128]=jnp.sum(kb,axis=0,keepdims=True)
    out_ref[...]=wide_ref[...].astype(bf16)
def pack_call(att,span,low,kw,kb,norm,up):
    return pl.pallas_call(pack_kernel,
        out_shape=jax.ShapeDtypeStruct((SMALL,ATT),bf16),
        scratch_shapes=[pltpu.VMEM((SMALL,ATT),f32)],
        cost_estimate=LIGHT,
        name="pack_small")(att,span,low,kw,kb,norm,up)
def unpack_kernel(count,*refs):
    got=refs[:count]
    proj_ref,depth_ref,kw_ref,kb_ref,hid_ref,up_ref,gain_ref,wide_ref=refs[count:]
    x=got[0][...].astype(f32)
    for g in got[1:]: x=x+g[...].astype(f32)
    wide_ref[...]=x
    proj_ref[...]=wide_ref[0:4,:]
    depth_ref[:,0:ATT]=wide_ref[4:13,:]
    depth_ref[:,ATT:]=wide_ref[13:22,:]
    kw_ref[...]=wide_ref[22:76,:]
    hid_ref[:,0:ATT]=wide_ref[76:80,:]
    hid_ref[:,ATT:]=wide_ref[82:86,:]
    gain_ref[:,0:ATT]=wide_ref[80:82,:]
    gain_ref[:,ATT:]=wide_ref[86:88,:]
    for i in range(FF//ATT): up_ref[0:1,i*ATT:(i+1)*ATT]=wide_ref[88+i:89+i,:]
    for h in range(HEADS): kb_ref[0:1,h*KERNEL:(h+1)*KERNEL]=wide_ref[96:97,h*TAPS+SLOT:h*TAPS+SLOT+KERNEL]
def unpack_call(got):
    S=lambda *s:jax.ShapeDtypeStruct(s,f32)
    out=pl.pallas_call(functools.partial(unpack_kernel,len(got)),
        out_shape=[S(4,ATT),S(KERNEL,D),S(HEADS*KERNEL,ATT),S(1,HEADS*KERNEL),S(4,D),S(1,FF),S(2,D)],
        scratch_shapes=[pltpu.VMEM((SMALL,ATT),f32)],
        cost_estimate=LIGHT,
        name="unpack_small")(*got)
    return [out[0],out[1],out[2].T,out[3].reshape(-1),out[4],out[5].reshape(-1),out[6]]


def digits(axis, size):
    out, bit = [], 1
    while bit < size:
        ways = 4 if size // bit % 4 == 0 else 2
        out.append((axis, size, [d * bit for d in range(ways)]))
        bit *= ways
    return out

def send_xor(x, stage, d):
    axis, size, xors = stage
    return lax.ppermute(x, axis, [(i, i ^ xors[d]) for i in range(size)])

def gather_send(x, stage, less=0):
    return [x] + [send_xor(x, stage, d) for d in range(1, len(stage[2]) - less)]

def gather_order(got, stage):
    axis, _, xors = stage
    ways = len(xors)
    mine = (lax.axis_index(axis) // xors[1]) % ways
    x = got[0]
    parts = []
    for place in range(ways):
        rel = mine ^ place
        part = got[0]
        for d in range(1, ways):
            part = jnp.where(rel == d, got[d], part)
        parts.append(part)
    return jnp.stack(parts, axis=1).reshape((x.shape[0] * ways,) + x.shape[1:])

def gather_near(got):
    return jnp.concatenate(got, axis=0)

def gather_stages(sizes):
    return digits("dp", sizes[0])[::-1] + digits("fsdp", sizes[1])[::-1]

def near_stages(sizes):
    ahead = gather_stages(sizes)
    return ahead, ahead[::-1]

def near_owners(sizes):
    nd, nf = sizes
    table = [0]
    for axis, _, xors in near_stages(sizes)[0]:
        step = nf if axis == "dp" else 1
        table = [x * step + t for x in xors for t in table]
    place = [0] * len(table)
    for i, t in enumerate(table):
        place[t] = i
    me = lax.axis_index("dp") * nf + lax.axis_index("fsdp")
    owners = jnp.asarray(table, jnp.int32) ^ me
    places = jnp.asarray(place, jnp.int32)[jnp.arange(nd * nf) ^ me]
    return owners, places

def scatter_send(g, stage):
    ways = len(stage[2])
    parts = g if isinstance(g, (list, tuple)) else jnp.split(g, ways, axis=0)
    return [parts[0]] + [send_xor(parts[d], stage, d) for d in range(1, ways)]

def scatter_total(got):
    total = got[0].astype(jnp.float32)
    for r in got[1:]:
        total = total + r.astype(jnp.float32)
    return total

def scatter_add(got):
    return scatter_total(got).astype(jnp.bfloat16)

def sum_send(x, stage):
    return [x] + [send_xor(x, stage, d) for d in range(1, len(stage[2]))]

def together(*arrays):
    return lax.optimization_barrier(arrays)


def body(
    tokens,
    segment_ids,
    cotangent,
    w_proj,
    w_point,
    w_out,
    w_up,
    w_down,
    proj_bias,
    conv_depth,
    kernel_weight,
    kernel_bias,
    hidden_bias,
    up_bias,
    norm_gain,
    *,
    sizes,
):
    rows, seq = segment_ids.shape
    nd, nf = sizes
    mid = FF // GROUPS
    shard_rows, ff_rows = D // (nd * nf), mid // (nd * nf)
    tok = tokens.reshape(rows * seq, D)
    cot = cotangent.reshape(rows * seq, D)

    ahead = gather_stages(sizes)
    owners, places = near_owners(sizes)
    first = jnp.concatenate([w_proj, w_point], axis=1).astype(bf16)[None]
    second = jnp.concatenate([jnp.swapaxes(w_up, 1, 2), w_down], axis=2).reshape(GROUPS * ff_rows, D)
    second = jnp.concatenate([second, w_out], axis=0).astype(bf16)[None]
    bounds = find_bounds(segment_ids)
    kernel_rows, kernel_shift = pack_kernel_weight(kernel_weight, kernel_bias)
    up_near = jnp.take(up_bias.reshape(GROUPS, nd * nf, ff_rows), owners, axis=1).reshape(1, FF)
    near, away = near_stages(sizes)
    direct = ff_rows % 16 == 0 and shard_rows % 8 == 0 and len(near) == 3 and sizes[1] == 2
    first = gather_order(gather_send(first, ahead[0]), ahead[0])
    first, second = together(first, second)
    got_first = gather_send(first, ahead[1])
    got_second = gather_send(second, near[0], 1)
    depth = depth_call(bounds, tok, conv_depth)
    *got_second, depth = together(*got_second, depth)
    got_second += gather_send(got_second[0], near[0])[len(got_second) :]
    *got_first, depth = together(*got_first, depth)
    first = gather_order(got_first, ahead[1])
    second = gather_near(got_second)
    got_second = gather_send(second, near[1])
    for stage in ahead[2:]:
        first = gather_order(gather_send(first, stage), stage)
    first = first.reshape(D, 5 * ATT)
    mixed, qkv, expo, recip, context, queries, key_conv, soft, bands, conv_in = mix_call(
        bounds, tok, depth, first, proj_bias, kernel_rows, kernel_shift
    )
    *got_second, mixed = together(*got_second, mixed)
    if direct:
        weights = got_second + [send_xor(piece, near[2], 1) for piece in got_second]
        weight_owners = owners
    else:
        second = gather_near(got_second)
        for stage in near[2:]:
            second = gather_near(gather_send(second, stage))
        ff_full = second[:, : GROUPS * ff_rows].reshape(nd * nf, GROUPS, ff_rows, D)
        ff_full = jnp.swapaxes(ff_full, 0, 1).reshape(GROUPS * mid, D)
        out_full = jnp.take(second[:, GROUPS * ff_rows :], places, axis=0).reshape(D, D)
        weights = [jnp.concatenate([ff_full, out_full], axis=0)[None]]
        weight_owners = jnp.zeros((1,), jnp.int32)
    layer_out, grad_one, grad_mixed, act, raised_low, first_low, two_low, one_low, norm_sums, up_sums = ff_call(
        weight_owners, weights, mixed, tok, cot, hidden_bias, up_near, norm_gain
    )

    if direct:
        parts = ffw_call(owners, act, raised_low, first_low, two_low, mixed, one_low, 2, shard_rows)
    else:
        halves = ffw_call(jnp.arange(2), act, raised_low, first_low, two_low, mixed, one_low, 2, D // 2)
        share = jnp.stack(halves)[:, 0]
        out_share = share[:, FF // 2 :].reshape(nd * nf, shard_rows, D)
        share = share[:, : FF // 2].reshape(2, GROUPS, nd * nf // 2, ff_rows, D).swapaxes(1, 2)
        share = share.reshape(nd * nf, GROUPS * ff_rows, D)
        share = jnp.concatenate([share, jnp.take(out_share, owners, axis=0)], axis=1)
        parts = jnp.split(share, len(away[0][2]), axis=0)
    *parts, grad_mixed = together(*parts, grad_mixed)
    got = scatter_send(parts, away[0])
    grad_key, query_part, conv_part, kw_sums, kb_sums, span_sums = span_back_call(
        bounds, grad_mixed, queries, key_conv, soft, bands, conv_in, kernel_rows[:LANES]
    )
    *got, query_part = together(*got, query_part)
    share = scatter_add(got)
    share, query_part = together(share, query_part)
    got = scatter_send(share, away[1])
    grad_proj, proj_sums = attend_back_call(bounds, grad_mixed, qkv, expo, recip, context, query_part, conv_part)
    grad_key, grad_proj = together(grad_key, grad_proj)
    part, depth_sums = depth_back_call(bounds, tok, grad_key, grad_one, first, conv_depth)
    *got, part, grad_proj = together(*got, part, grad_proj)
    for stage in away[2:-1]:
        got = scatter_send(scatter_add(got), stage)
    share = scatter_add(got)
    up_sums = jnp.take(jnp.sum(up_sums, axis=0).reshape(GROUPS, nd * nf, ff_rows), places, axis=1)
    small = pack_call(
        proj_sums, span_sums, depth_sums, kw_sums, kb_sums, norm_sums, up_sums.reshape(FF // ATT, ATT)
    )
    share, small, grad_proj = together(share, small, grad_proj)
    got_share = scatter_send(share, away[-1])
    got_small = sum_send(small, away[0])
    if direct:
        parts = feature_weights_call(owners, tok, grad_proj, depth, grad_key, 2)
    else:
        halves = feature_weights_call(jnp.arange(2), tok, grad_proj, depth, grad_key, 2)
        late = jnp.concatenate(halves, axis=0).reshape(nd * nf, shard_rows, 5 * ATT)
        parts = jnp.split(jnp.take(late, owners, axis=0), len(away[0][2]), axis=0)
    tied = together(*got_share, *got_small, *parts, part)
    n_share, n_small = len(got_share), len(got_share) + len(got_small)
    got_share, got_small, parts, part = tied[:n_share], tied[n_share:n_small], tied[n_small:-1], tied[-1]
    share = scatter_add(got_share)[0].astype(f32)
    ff_share = share[: GROUPS * ff_rows].reshape(GROUPS, ff_rows, D)
    out_share = share[GROUPS * ff_rows :]
    small = scatter_add(got_small)
    small, part = together(small, part)
    got = scatter_send(parts, away[0])
    got_small = sum_send(small, away[1])
    half_rows = rows // 2
    tokens_grad = input_call(grad_proj, part, first, 0, half_rows)
    *got, tokens_grad = together(*got, tokens_grad)
    *got_small, tokens_grad = together(*got_small, tokens_grad)
    late = scatter_add(got)
    small = scatter_add(got_small)
    for stage in away[2:-1]:
        small = scatter_add(sum_send(small, stage))
    late, small, tokens_grad = together(late, small, tokens_grad)
    got = scatter_send(late, away[1])
    axis, size, xors = away[-1]
    bits = [(axis, size, [0, x]) for x in xors[1:] if x & (x - 1) == 0][::-1]
    got_small = sum_send(small, bits[0])
    tokens_grad = input_call(grad_proj, part, first, half_rows, rows - half_rows, tokens_grad)
    up_share = jnp.swapaxes(ff_share[..., : D // GROUPS], 1, 2)
    down_share = ff_share[..., D // GROUPS :]
    *got, tokens_grad, up_share, down_share = together(*got, tokens_grad, up_share, down_share)
    *got_small, tokens_grad, out_share = together(*got_small, tokens_grad, out_share)
    for stage in away[2:-1]:
        got = scatter_send(scatter_add(got), stage)
    late = scatter_add(got)
    if len(bits) > 1:
        small = scatter_add(got_small)
    late, small = together(late, small)
    got = scatter_send(late, away[-1])
    if len(bits) > 1:
        got_small = sum_send(small, bits[1])
    smalls = unpack_call(got_small)
    late = scatter_add(got)
    late = late[0].astype(f32)
    return (
        layer_out.reshape(rows, seq, D),
        tokens_grad.reshape(rows, seq, D),
        late[:, : 4 * ATT],
        late[:, 4 * ATT :],
        out_share,
        up_share,
        down_share,
        *smalls,
    )


def solution(mesh):
    whole, split = P(), ("dp", "fsdp")
    rows3, rows2 = P(split, None, None), P(split, None)
    up, down = P(None, None, split), P(None, split, None)
    return jax.shard_map(
        functools.partial(body, sizes=(mesh.shape["dp"], mesh.shape["fsdp"])),
        mesh=mesh,
        in_specs=(rows3, rows2, rows3, rows2, rows2, rows2, up, down) + (whole,) * 7,
        out_specs=(rows3, rows3, rows2, rows2, rows2, up, down) + (whole,) * 7,
        check_vma=False,
    )
```

```python
import functools

import jax
import jax.numpy as jnp
from jax import lax
from jax.experimental import pallas as pl
from jax.experimental.pallas import tpu as pltpu
from jax.sharding import PartitionSpec as P

f32=jnp.float32
bf16=jnp.bfloat16
D=768; FF=3072; HEADS=6; HEAD_DIM=64; KERNEL=9; GROUPS=2; ATT=384
norm_eps=1e-12
LIGHT=pl.CostEstimate(flops=1,bytes_accessed=1,transcendentals=0)
def dot(a,b): return lax.dot_general(a,b,(((1,),(0,)),((),())),preferred_element_type=f32)
def dot_t(a,b): return lax.dot_general(a,b,(((1,),(1,)),((),())),preferred_element_type=f32)
def dot_l(a,b): return lax.dot_general(a,b,(((0,),(0,)),((),())),preferred_element_type=f32)
def fold8(x):
    return jnp.sum(x.reshape(x.shape[0]//8,8,x.shape[1]),axis=0)
def row_mean(x): return jnp.sum(x,axis=-1,keepdims=True)*(1.0/x.shape[-1])

def ordered(kernel,lead,after):
    extra=len(after)
    return lambda *refs: kernel(*refs[:lead],*refs[lead+extra:])
def waits(after):
    return [pl.BlockSpec(memory_space=pl.ANY) for _ in after]

def gelu_parts(x):
    phi=0.5+0.5*lax.erf(x*0.7071067811865476)
    return x*phi, phi+x*(jnp.exp(x*x*-0.5)*0.3989422804014327)

CH=512
PARTS=2
LAG=0
def ff_kernel(pieces,own_ref,*refs):
    w_refs=refs[:pieces]
    (mixed_ref,tok_ref,cot_ref,hb_ref,ub_ref,gain_ref,
     out_ref,gone_ref,gmix_ref,act_ref,gr_ref,xlow_ref,g2low_ref,g1low_ref,sums_ref,ups_ref,
     dg_ref,wup_ref,wdn_ref,wide_ref,wout_ref,keep_ref)=refs[pieces:]
    half=D//GROUPS; mid=FF//GROUPS
    @pl.when(pl.program_id(0)==0)
    def _():
        sums_ref[...]=jnp.zeros_like(sums_ref); ups_ref[...]=jnp.zeros_like(ups_ref)
        at=0
        total=sum(w.shape[0] for w in w_refs)
        rows,share=mid//total,D//total
        for w_ref in w_refs:
            n=w_ref.shape[0]
            for g in range(GROUPS):
                span=slice(at*rows,(at+n)*rows); part=slice(g*rows,(g+1)*rows)
                wup_ref[g,span,:]=w_ref[:,part,0:half].reshape(n*rows,half)
                wdn_ref[g,span,:]=w_ref[:,part,half:].reshape(n*rows,half)
            for i in range(n):
                place=pl.multiple_of(own_ref[at+i]*share,8)
                wide_ref[pl.ds(place,share),:]=w_ref[i,GROUPS*rows:GROUPS*rows+share,:].astype(f32)
            at+=n
        wout_ref[...]=wide_ref[...].astype(bf16)
    spans=[(g,c,slice(g*mid+c,g*mid+c+CH)) for g in range(GROUPS) for c in range(0,mid,CH)]
    gain1,gain2=gain_ref[0:1,:],gain_ref[1:2,:]

    def tokens_part(rs):
        res=dot(mixed_ref[rs,:],wout_ref[...])
        yield
        res=res+hb_ref[0:1,:]+tok_ref[rs,:].astype(f32)
        mean=row_mean(res); cen=res-mean
        inv1=lax.rsqrt(row_mean(cen*cen)+norm_eps)
        n1=cen*inv1
        first=n1*gain1+hb_ref[1:2,:]
        xlow_ref[rs,:]=first.astype(bf16)
        gone_ref[rs,:]=n1
        yield
        def raise_(g,c,cs):
            return dot_t(xlow_ref[rs,g*half:(g+1)*half],wup_ref[g,c:c+CH,:])+ub_ref[0:1,cs]
        lows=[]
        ahead=raise_(*spans[0])
        for i,(g,c,cs) in enumerate(spans):
            raised=ahead
            if i+1<len(spans): ahead=raise_(*spans[i+1])
            yield
            a,dg=gelu_parts(raised)
            act_ref[rs,cs]=a.astype(bf16)
            dg_ref[rs,cs]=dg
            yield
            if c+CH==mid:
                lows.append(dot(act_ref[rs,g*mid:(g+1)*mid],wdn_ref[g]))
                yield
        n1=gone_ref[rs,:]
        res=jnp.concatenate(lows,axis=1)+hb_ref[2:3,:]+(n1*gain1+hb_ref[1:2,:])
        mean=row_mean(res); cen=res-mean
        inv2=lax.rsqrt(row_mean(cen*cen)+norm_eps)
        n2=cen*inv2
        out_ref[rs,:]=(n2*gain2+hb_ref[3:4,:]).astype(bf16)
        yield
        e=cot_ref[rs,:].astype(f32)
        eg=e*gain2
        g2=inv2*(eg-row_mean(eg)-n2*row_mean(eg*n2))
        sums_ref[3]+=fold8(e); sums_ref[5]+=fold8(e*n2); sums_ref[2]+=fold8(g2)
        g2low_ref[rs,:]=g2.astype(bf16)
        keep_ref[rs,:]=g2
        yield
        def fall(g,c,cs):
            return dot_t(g2low_ref[rs,g*half:(g+1)*half],wdn_ref[g,c:c+CH,:])
        parts=[]
        ahead=fall(*spans[0])
        for i,(g,c,cs) in enumerate(spans):
            ga=ahead
            if i+1<len(spans): ahead=fall(*spans[i+1])
            yield
            gr=ga*dg_ref[rs,cs]
            ups_ref[:,cs]+=fold8(gr)
            gr_ref[rs,cs]=gr.astype(bf16)
            yield
            if c+CH==mid:
                parts.append(dot(gr_ref[rs,g*mid:(g+1)*mid],wup_ref[g]))
                yield
        gf=jnp.concatenate(parts,axis=1)+keep_ref[rs,:]
        n1=gone_ref[rs,:]
        sums_ref[1]+=fold8(gf); sums_ref[4]+=fold8(gf*n1)
        yield
        eg=gf*gain1
        g1=inv1*(eg-row_mean(eg)-n1*row_mean(eg*n1))
        sums_ref[0]+=fold8(g1)
        gone_ref[rs,:]=g1
        g1low_ref[rs,:]=g1.astype(bf16)
        yield
        gmix_ref[rs,:]=dot_t(g1low_ref[rs,:],wout_ref[...]).astype(bf16)
    total=mixed_ref.shape[0]; piece=total//PARTS
    running=[tokens_part(slice(i*piece,(i+1)*piece)) for i in range(PARTS)]
    waiting=[i*LAG for i in range(PARTS)]
    while any(part is not None for part in running):
        for i,part in enumerate(running):
            if waiting[i]>0:
                waiting[i]-=1
            elif part is not None and next(part,StopIteration) is StopIteration:
                running[i]=None

def ff_call(owners,weights,mixed,tok,cot,hb,ub,gain,T=512,after=()):
    n=tok.shape[0]
    row=lambda w,:pl.BlockSpec((T,w),lambda i,o:(i,0))
    full=lambda s:pl.BlockSpec(s,lambda i,o:(0,)*len(s),pipeline_mode=pl.Buffered(1))
    S=lambda s,d:jax.ShapeDtypeStruct(s,d)
    W=(GROUPS,FF//GROUPS,D//GROUPS)
    return pl.pallas_call(ordered(functools.partial(ff_kernel,len(weights)),7+len(weights),after),
        grid_spec=pltpu.PrefetchScalarGridSpec(num_scalar_prefetch=1,grid=(n//T,),
        in_specs=[full(w.shape) for w in weights]+[row(D),row(D),row(D),full((4,D)),full((1,FF)),full((2,D))]+waits(after),
        out_specs=[row(D),row(D),row(D),row(FF),row(FF),row(D),row(D),row(D),full((6,8,D)),full((8,FF))],
        scratch_shapes=[pltpu.VMEM((T,FF),f32),pltpu.VMEM(W,bf16),pltpu.VMEM(W,bf16),pltpu.VMEM((D,D),f32),pltpu.VMEM((D,D),bf16),pltpu.VMEM((T,D),f32)]),
        out_shape=[S((n,D),bf16),S((n,D),f32),S((n,D),bf16),S((n,FF),bf16),S((n,FF),bf16),S((n,D),bf16),S((n,D),bf16),S((n,D),bf16),S((6,8,D),f32),S((8,FF),f32)],
        compiler_params=pltpu.CompilerParams(vmem_limit_bytes=60<<20),
        cost_estimate=LIGHT,
        name="feed_forward",
    )(owners,*weights,mixed,tok,cot,hb,ub,gain,*after)

def fetch(pairs,sems):
    copies=[pltpu.make_async_copy(src,dst,sems.at[i]) for i,(src,dst) in enumerate(pairs)]
    for copy in copies: copy.start()
    return copies
def by_owner(own_ref,wide_ref,width,outs,rows,columns):
    per=outs[0].shape[0]; share=rows.stop-rows.start
    for p,out in enumerate(outs):
        for i in range(per):
            place=pl.multiple_of(own_ref[p*per+i]*share,8)
            out[i,rows,columns]=wide_ref[pl.ds(place,share),0:width].astype(bf16)

def ffw_kernel(parts,share,turned,own_ref,act_ref,gr_ref,xlow_ref,g2low_ref,mix_ref,g1_ref,*refs):
    count=parts if turned else 2*parts
    outs=refs[:count]
    act,gr,xlow,g2low,mix,g1,wide,sems=refs[count:count+8]
    blocks=refs[count+8:2*count+8]
    out_sem=refs[-1]
    half=D//GROUPS; mid=FF//GROUPS; C=mid//parts
    jobs=[(p,g) for p in range(parts) for g in range(GROUPS)]
    cols=[slice(g*mid+p*C,g*mid+(p+1)*C) for p,g in jobs]
    pairs=[(xlow_ref,xlow)]+[(gr_ref.at[:,cols[0]],gr.at[0]),(g2low_ref,g2low),(act_ref.at[:,cols[0]],act.at[0])]
    for j in range(1,len(jobs)):
        pairs+=[(gr_ref.at[:,cols[j]],gr.at[j]),(act_ref.at[:,cols[j]],act.at[j])]
    pairs+=[(mix_ref,mix),(g1_ref,g1)]
    copies=fetch(pairs,sems)
    done=[]
    def put(p,g,down,x):
        if turned:
            per=blocks[p].shape[0]; rows=(blocks[p].shape[1]-share)//GROUPS
            blocks[p][:,g*rows:(g+1)*rows,down*half:(down+1)*half]=x.T.astype(bf16).reshape(per,rows,half)
        else:
            blocks[p][2*g+down]=x.astype(bf16)
    def send(i):
        done.append(pltpu.make_async_copy(blocks[i],outs[i],out_sem.at[i]))
        done[-1].start()
    for j,(p,g) in enumerate(jobs):
        gs=slice(g*half,(g+1)*half)
        if j==0: copies[0].wait()
        copies[1 if j==0 else 2+2*j].wait()
        put(p,g,0,dot_l(xlow[:,gs],gr[j]))
        if j==0: copies[2].wait()
        copies[3+2*j].wait()
        put(p,g,1,dot_l(g2low[:,gs],act[j]))
        if g==GROUPS-1 and not turned: send(p)
    copies[-2].wait(); copies[-1].wait()
    wide[...]=dot_l(mix[...],g1[...])
    if turned:
        rows=blocks[0].shape[1]-share
        by_owner(own_ref,wide,D,blocks,slice(rows,rows+share),slice(0,D))
    else:
        by_owner(own_ref,wide,D,blocks[parts:],slice(0,share),slice(0,D))
    for i in range(0 if turned else parts,count): send(i)
    for copy in done: copy.wait()
def ffw_call(owners,act,gr,xlow,g2low,mixed,g1,parts,share,turned=False,after=()):
    n=act.shape[0]; blocks=owners.shape[0]; mid=FF//GROUPS; C=mid//parts
    if turned:
        shapes=[(blocks//parts,FF//blocks+share,D)]*parts
    else:
        shapes=[(2*GROUPS,D//GROUPS,C)]*parts+[(blocks//parts,share,D)]*parts
    any_=pl.BlockSpec(memory_space=pl.ANY)
    jobs=parts*GROUPS
    return pl.pallas_call(ordered(functools.partial(ffw_kernel,parts,share,turned),7,after),
        grid_spec=pltpu.PrefetchScalarGridSpec(num_scalar_prefetch=1,grid=(1,),
        in_specs=[any_]*6+waits(after),out_specs=[any_]*len(shapes),
        scratch_shapes=[pltpu.VMEM((jobs,n,C),bf16)]*2+[pltpu.VMEM((n,D),bf16)]*4+[pltpu.VMEM((D,D),f32),pltpu.SemaphoreType.DMA((2*jobs+4,))]
            +[pltpu.VMEM(s,bf16) for s in shapes]+[pltpu.SemaphoreType.DMA((len(shapes),))]),
        out_shape=[jax.ShapeDtypeStruct(s,bf16) for s in shapes],
        compiler_params=pltpu.CompilerParams(vmem_limit_bytes=60<<20),
        cost_estimate=LIGHT,
        name="feed_forward_weights",
    )(owners,act,gr,xlow,g2low,mixed,g1,*after)

def turn_kernel(rows,ka_ref,ra_ref,kb_ref,rb_ref,*outs):
    half=D//GROUPS
    per=outs[0].shape[0]
    x=(ka_ref[...].astype(f32)+ra_ref[...].astype(f32)).astype(bf16).T
    for i in range(2*GROUPS):
        g,down=i//2,i%2
        @pl.when(pl.program_id(0)==i)
        def _(g=g,down=down):
            for p,out in enumerate(outs):
                out[:,g*rows:(g+1)*rows,down*half:(down+1)*half]=x[p*per*rows:(p+1)*per*rows].reshape(per,rows,half)
    low=GROUPS*rows
    @pl.when(pl.program_id(0)==0)
    def _():
        for p,out in enumerate(outs):
            s=slice(p*per,(p+1)*per)
            out[:,low:,:]=(kb_ref[s].astype(f32)+rb_ref[s].astype(f32)).astype(bf16)
def turn_call(got,parts,rows):
    ka,ra,kb,rb=got
    shape=(kb.shape[0]//parts,GROUPS*rows+kb.shape[1],D)
    one=pl.BlockSpec((None,)+ka.shape[1:],lambda i:(i,0,0))
    full=lambda s:pl.BlockSpec(s,lambda i:(0,0,0))
    return pl.pallas_call(functools.partial(turn_kernel,rows),grid=(2*GROUPS,),
        in_specs=[one,one,full(kb.shape),full(kb.shape)],out_specs=[full(shape)]*parts,
        out_shape=[jax.ShapeDtypeStruct(shape,bf16)]*parts,
        compiler_params=pltpu.CompilerParams(vmem_limit_bytes=60<<20),
        cost_estimate=LIGHT,
        name="add_and_turn")(ka,ra,kb,rb)

def feature_weights_kernel(parts,own_ref,tok_ref,gp_ref,dep_ref,gk_ref,*refs):
    outs=refs[:parts]
    tok,gp,dep,gk,wide,sems=refs[parts:parts+6]
    blocks=refs[parts+6:parts+6+parts]
    out_sem=refs[-1]
    copies=fetch([(gk_ref,gk),(dep_ref,dep),(tok_ref,tok),(gp_ref.at[:,0:2*ATT],gp.at[0]),(gp_ref.at[:,2*ATT:],gp.at[1])],sems)
    rows=slice(0,blocks[0].shape[1])
    copies[0].wait(); copies[1].wait()
    wide[:,0:ATT]=dot_l(dep[...],gk[...])
    by_owner(own_ref,wide,ATT,blocks,rows,slice(4*ATT,5*ATT))
    copies[2].wait()
    for j in range(2):
        copies[3+j].wait()
        wide[...]=dot_l(tok[...],gp[j])
        by_owner(own_ref,wide,D,blocks,rows,slice(j*D,(j+1)*D))
    done=fetch([(blocks[p],outs[p]) for p in range(parts)],out_sem)
    for copy in done: copy.wait()
def feature_weights_call(owners,tok,gp,dep,gk,parts,after=()):
    n=tok.shape[0]; blocks=owners.shape[0]
    shape=(blocks//parts,D//blocks,5*ATT)
    any_=pl.BlockSpec(memory_space=pl.ANY)
    return pl.pallas_call(ordered(functools.partial(feature_weights_kernel,parts),5,after),
        grid_spec=pltpu.PrefetchScalarGridSpec(num_scalar_prefetch=1,grid=(1,),
        in_specs=[any_]*4+waits(after),out_specs=[any_]*parts,
        scratch_shapes=[pltpu.VMEM((n,D),bf16),pltpu.VMEM((2,n,2*ATT),bf16),pltpu.VMEM((n,D),bf16),pltpu.VMEM((n,ATT),bf16),pltpu.VMEM((D,D),f32),pltpu.SemaphoreType.DMA((5,))]
            +[pltpu.VMEM(shape,bf16)]*parts+[pltpu.SemaphoreType.DMA((parts,))]),
        out_shape=[jax.ShapeDtypeStruct(shape,bf16)]*parts,
        compiler_params=pltpu.CompilerParams(vmem_limit_bytes=60<<20),
        cost_estimate=LIGHT,
        name="feature_weights",
    )(owners,tok,gp,dep,gk,*after)

TAPS=16
LANES=HEADS*TAPS
BT=64
LEAD=16
SLOT=4
HALF=256
SEQ=512
NEG=-1000000000.0

def doc_of(pos,b_ref,first=0):
    row=pl.program_id(0)+first
    return ((pos>=b_ref[row,0]).astype(jnp.int32)+(pos>=b_ref[row,1]).astype(jnp.int32)+(pos>=b_ref[row,2]).astype(jnp.int32))
def tap_valid_t(b_ref):
    tap=lax.broadcasted_iota(jnp.int32,(TAPS,SEQ),0); t=lax.broadcasted_iota(jnp.int32,(TAPS,SEQ),1)
    u=t+tap-KERNEL//2-SLOT
    ok=(u>=0)&(u<SEQ)&(doc_of(u,b_ref)==doc_of(t,b_ref))&(tap>=SLOT)&(tap<SLOT+KERNEL)
    return ok.astype(f32)
def roll_matrix(b_ref,back):
    start=b_ref[pl.program_id(0),3]
    a=lax.broadcasted_iota(jnp.int32,(SEQ,SEQ),1 if back else 0); t=lax.broadcasted_iota(jnp.int32,(SEQ,SEQ),0 if back else 1)
    d=a+start-t
    return jnp.where((d==0)|(d==SEQ),1.0,0.0).astype(bf16)
def head_lanes(shape,h):
    lane=lax.broadcasted_iota(jnp.int32,shape,len(shape)-1)
    return (lane<HEAD_DIM) if h==0 else (lane>=HEAD_DIM)
def keep_head(x,h):
    return jnp.where(head_lanes(x.shape,h),x,jnp.zeros_like(x))

BAND=128
def tap_bands(b_ref,r,first=0):
    lo=min(max(r-BAND//2,0),SEQ-2*BAND)
    row=lax.broadcasted_iota(jnp.int32,(BAND,2*BAND),0)+r; col=lax.broadcasted_iota(jnp.int32,(BAND,2*BAND),1)+lo
    step=jnp.where(doc_of(row,b_ref,first)==doc_of(col,b_ref,first),col-row,SEQ)
    return lo,[jnp.where(step==j-KERNEL//2,1.0,0.0).astype(bf16) for j in range(KERNEL)]

def depth_kernel(b_ref,tok_ref,cd_ref,out_ref):
    side=[j for j in range(KERNEL) if j!=KERNEL//2]
    for r in range(0,SEQ,BAND):
        lo,bands=tap_bands(b_ref,r)
        stack=jnp.concatenate([bands[j] for j in side],axis=0)
        for c in range(0,D,256):
            cs=slice(c,c+256)
            moved=dot(stack,tok_ref[lo:lo+2*BAND,cs])
            acc=tok_ref[r:r+BAND,cs].astype(f32)*cd_ref[KERNEL//2:KERNEL//2+1,cs]
            for i,j in enumerate(side):
                acc=acc+moved[i*BAND:(i+1)*BAND]*cd_ref[j:j+1,cs]
            out_ref[r:r+BAND,cs]=acc.astype(bf16)
def depth_call(bounds,tok,cd):
    n=tok.shape[0]
    row=pl.BlockSpec((SEQ,D),lambda i,b:(i,0))
    return pl.pallas_call(depth_kernel,
        grid_spec=pltpu.PrefetchScalarGridSpec(num_scalar_prefetch=1,grid=(n//SEQ,),
        in_specs=[row,pl.BlockSpec((KERNEL,D),lambda i,b:(0,0))],
        out_specs=row),
        out_shape=jax.ShapeDtypeStruct((n,D),bf16),
        compiler_params=pltpu.CompilerParams(vmem_limit_bytes=60<<20),
        cost_estimate=LIGHT,
        name="depth_taps")(bounds,tok,cd)

def mix_kernel(b_ref,tok_ref,dep_ref,w_ref,pb_ref,kw_ref,kb_ref,
               mixed_ref,qkv_ref,e_ref,r_ref,ctx_ref,q_ref,kc_ref,ks_ref,band_ref,cin_ref):
    tok=tok_ref[...]
    p=dot(tok,w_ref[:,0:4*ATT])
    q=(p[:,0:ATT]+pb_ref[0:1,:]).astype(bf16)
    k=p[:,ATT:2*ATT].astype(bf16)
    v=(p[:,2*ATT:3*ATT]+pb_ref[1:2,:]).astype(bf16)
    cin=(p[:,3*ATT:]+pb_ref[2:3,:]).astype(bf16)
    q_ref[...]=q
    rolled=dot(roll_matrix(b_ref,False),jnp.concatenate([q*jnp.bfloat16(0.125),k,v],axis=1)).astype(bf16)
    qkv_ref[...]=rolled
    key_conv=dot(dep_ref[...],w_ref[:,4*ATT:])+pb_ref[3:4,:]
    kc_ref[...]=key_conv
    attn=key_conv*q.astype(f32)
    hi=attn.astype(bf16); lo=(attn-hi.astype(f32)).astype(bf16)
    both=dot_t(kw_ref[...],hi)
    logits=both[:LANES]+both[LANES:]+dot_t(kw_ref[0:LANES,:],lo)+kb_ref[...]
    logits=logits.reshape(HEADS,TAPS,SEQ)
    tap=lax.broadcasted_iota(jnp.int32,(HEADS,TAPS,SEQ),1)
    logits=jnp.where((tap>=SLOT)&(tap<SLOT+KERNEL),logits,-1e30)
    ex=jnp.exp(logits-jnp.max(logits,axis=1,keepdims=True))
    ks=ex/jnp.sum(ex,axis=1,keepdims=True)
    ks_ref[...]=ks.reshape(LANES,SEQ)
    km=(ks*tap_valid_t(b_ref)[None]).reshape(LANES,SEQ)
    km=jnp.concatenate([km,jnp.zeros((128-LANES,SEQ),f32)],axis=0).T
    cin_ref[0:LEAD,:]=jnp.zeros((LEAD,ATT),bf16); cin_ref[LEAD+SEQ:,:]=jnp.zeros((128-LEAD-BT,ATT),bf16)
    cin_ref[LEAD:LEAD+SEQ,:]=cin
    row=lax.broadcasted_iota(jnp.int32,(BT,128),0); lane=lax.broadcasted_iota(jnp.int32,(BT,128),1)
    off=lane-row-(LEAD-KERNEL//2)
    on_band=(off>=0)&(off<KERNEL)
    for i in range(SEQ//BT):
        kmi=km[i*BT:(i+1)*BT,:]
        bands=[]
        for h in range(HEADS):
            x=pltpu.roll(kmi,(LEAD-KERNEL//2-SLOT-h*TAPS)%128,1,stride=1,stride_axis=0)
            x=jnp.where(on_band,x,0.0).astype(bf16)
            band_ref[i,h]=x
            bands.append(x)
        for pr in range(HEADS//2):
            win=cin_ref[i*BT:i*BT+128,pr*128:(pr+1)*128]
            o=dot(jnp.concatenate(bands[2*pr:2*pr+2],axis=1),jnp.concatenate([keep_head(win,0),keep_head(win,1)],axis=0))
            mixed_ref[i*BT:(i+1)*BT,ATT+pr*128:ATT+(pr+1)*128]=o.astype(bf16)
    start=b_ref[pl.program_id(0),3]
    def rolled_doc(axis):
        t=lax.broadcasted_iota(jnp.int32,(HALF,HALF),axis)+start+HALF
        return doc_of(jnp.where(t>=SEQ,t-SEQ,t),b_ref)
    same=rolled_doc(0)==rolled_doc(1)
    ones=jnp.ones((HALF,128),bf16)
    for a in range(2):
        rs=slice(a*HALF,(a+1)*HALF)
        for pr in range(HEADS//2):
            Q=rolled[rs,pr*128:(pr+1)*128]; K=rolled[rs,ATT+pr*128:ATT+(pr+1)*128]; V=rolled[rs,2*ATT+pr*128:2*ATT+(pr+1)*128]
            es=[];vs=[]
            both=dot_t(Q,jnp.concatenate([keep_head(K,0),keep_head(K,1)],axis=0))
            for h in range(2):
                s=both[:,h*HALF:(h+1)*HALF]
                if a==1: s=jnp.where(same,s,NEG)
                e=jnp.exp(s-jnp.max(s,axis=-1,keepdims=True)).astype(bf16)
                e_ref[a,2*pr+h]=e
                es.append(e); vs.append(jnp.concatenate([keep_head(V,h),keep_head(ones,h)],axis=1))
            o=dot(jnp.concatenate(es,axis=1),jnp.concatenate(vs,axis=0))
            r=1.0/o[:,128:]
            r_ref[rs,pr*128:(pr+1)*128]=r
            ctx_ref[rs,pr*128:(pr+1)*128]=(o[:,:128]*r).astype(bf16)
    mixed_ref[:,0:ATT]=dot(roll_matrix(b_ref,True),ctx_ref[...]).astype(bf16)

CPAD=SEQ+128-BT
def mix_call(bounds,tok,dep,w,pb,kw,kb,after=()):
    n=tok.shape[0]; R=n//SEQ
    row=lambda w_:pl.BlockSpec((SEQ,w_),lambda i,b:(i,0))
    full=lambda s:pl.BlockSpec(s,lambda i,b:(0,)*len(s))
    lead=lambda s:pl.BlockSpec((None,)+s,lambda i,b:(i,)+(0,)*len(s))
    S=lambda s,d:jax.ShapeDtypeStruct(s,d)
    NT=SEQ//BT
    return pl.pallas_call(ordered(mix_kernel,7,after),
        grid_spec=pltpu.PrefetchScalarGridSpec(num_scalar_prefetch=1,grid=(R,),
        in_specs=[row(D),row(D),full((D,5*ATT)),full((4,ATT)),full((2*LANES,ATT)),full((LANES,1))]+waits(after),
        out_specs=[row(D),row(3*ATT),lead((2,HEADS,HALF,HALF)),row(ATT),row(ATT),row(ATT),row(ATT),lead((LANES,SEQ)),lead((NT,HEADS,BT,128)),lead((CPAD,ATT))]),
        out_shape=[S((n,D),bf16),S((n,3*ATT),bf16),S((R,2,HEADS,HALF,HALF),bf16),S((n,ATT),f32),S((n,ATT),bf16),S((n,ATT),bf16),S((n,ATT),f32),S((R,LANES,SEQ),f32),S((R,NT,HEADS,BT,128),bf16),S((R,CPAD,ATT),bf16)],
        compiler_params=pltpu.CompilerParams(vmem_limit_bytes=60<<20),
        cost_estimate=LIGHT,
        name="attend_and_span")(bounds,tok,dep,w,pb,kw,kb,*after)


def pack_kernel_weight(kw,kb):
    k=kw.T.reshape(HEADS,KERNEL,ATT)
    k=jnp.pad(k,((0,0),(SLOT,TAPS-KERNEL-SLOT),(0,0))).reshape(LANES,ATT)
    hi=lax.reduce_precision(k,8,7); lo=(k-hi).astype(bf16); hi=hi.astype(bf16)
    b=jnp.pad(kb.reshape(HEADS,KERNEL),((0,0),(SLOT,TAPS-KERNEL-SLOT))).reshape(LANES,1)
    return jnp.concatenate([hi,lo],axis=0),b

def find_bounds(seg):
    counts=jnp.stack([jnp.sum(seg==i,axis=1) for i in range(4)],axis=1)
    begin=jnp.cumsum(counts,axis=1)-counts
    which=jnp.argmax(counts==HALF,axis=1)
    start=jnp.take_along_axis(begin,which[:,None],axis=1)
    return jnp.concatenate([begin[:,1:],start],axis=1).astype(jnp.int32)

def span_back_kernel(b_ref,gm_ref,q_ref,kc_ref,ks_ref,band_ref,cin_ref,kwt_ref,
                gk_ref,gqc_ref,gci_ref,kwg_ref,kbg_ref,pbg_ref,gcin_ref,anti_ref):
    @pl.when(pl.program_id(0)==0)
    def _():
        anti=lax.broadcasted_iota(jnp.int32,(SEQ,SEQ),0)+lax.broadcasted_iota(jnp.int32,(SEQ,SEQ),1)
        anti_ref[...]=jnp.where(anti==SEQ-1,1.0,0.0).astype(bf16)
        kwg_ref[...]=jnp.zeros_like(kwg_ref); kbg_ref[...]=jnp.zeros_like(kbg_ref); pbg_ref[...]=jnp.zeros_like(pbg_ref)
    gcin_ref[...]=jnp.zeros_like(gcin_ref)
    lane=lax.broadcasted_iota(jnp.int32,(BT,128),1)
    anti=anti_ref[...]
    falling=dot(anti,gm_ref[:,ATT:]).astype(bf16)
    logits=[]
    for i in range(SEQ//BT):
        acc=None
        f=SEQ//BT-1-i
        for pr in range(HEADS//2):
            g=gm_ref[i*BT:(i+1)*BT,ATT+pr*128:ATT+(pr+1)*128]
            gf=falling[i*BT:(i+1)*BT,pr*128:(pr+1)*128]
            win=cin_ref[f*BT:f*BT+128,pr*128:(pr+1)*128]
            both=dot_t(jnp.concatenate([keep_head(gf,0),keep_head(gf,1)],axis=0),win)
            for h in range(2):
                head=2*pr+h
                d=pltpu.roll(both[h*BT:(h+1)*BT],(head*TAPS+SLOT-LEAD+KERNEL//2-BT+1)%128,1,stride=1,stride_axis=0)
                d=jnp.where((lane>=head*TAPS+SLOT)&(lane<head*TAPS+SLOT+KERNEL),d,0.0)
                acc=d if acc is None else acc+d
            bands=jnp.concatenate([band_ref[i,2*pr],band_ref[i,2*pr+1]],axis=0)
            gcin_ref[i*BT:i*BT+128,pr*128:(pr+1)*128]+=dot_l(bands,jnp.concatenate([keep_head(g,0),keep_head(g,1)],axis=0))
        logits.append(acc)
    gk=jnp.concatenate(logits,axis=0)
    gh=gk.astype(bf16); glo=(gk-gh.astype(f32)).astype(bf16)
    gk=(dot_l(gh,anti)+dot_l(glo,anti))[0:LANES,:].reshape(HEADS,TAPS,SEQ)*tap_valid_t(b_ref)[None]
    ks=ks_ref[...].reshape(HEADS,TAPS,SEQ)
    gl=(ks*(gk-jnp.sum(gk*ks,axis=1,keepdims=True))).reshape(LANES,SEQ)
    kbg_ref[...]+=gl[:,0:128]+gl[:,128:256]+gl[:,256:384]+gl[:,384:512]
    q=q_ref[...].astype(f32); kc=kc_ref[...]
    attn=kc*q
    hi=attn.astype(bf16)
    glb=gl.astype(bf16)
    kwg_ref[...]+=dot(glb,hi)
    gattn=dot_l(glb,kwt_ref[...])
    gkc=gattn*q
    gk_ref[...]=gkc.astype(bf16)
    pbg_ref[1]+=fold8(gkc)
    gqc_ref[...]=gattn*kc
    gci=gcin_ref[LEAD:LEAD+SEQ,:]
    pbg_ref[0]+=fold8(gci)
    gci_ref[...]=gci.astype(bf16)

def attend_back_kernel(b_ref,gm_ref,qkv_ref,e_ref,r_ref,ctx_ref,gqc_ref,gci_ref,gp_ref,pbg_ref,dr_ref):
    @pl.when(pl.program_id(0)==0)
    def _(): pbg_ref[...]=jnp.zeros_like(pbg_ref)
    dor=(dot(roll_matrix(b_ref,False),gm_ref[:,0:ATT])*r_ref[...])
    dol=dor.astype(bf16)
    prod=(dol.astype(f32)*ctx_ref[...].astype(f32)).astype(bf16)
    minus=jnp.full((HALF,128),-1.0,bf16)
    minus=jnp.concatenate([keep_head(minus,0),keep_head(minus,1)],axis=0)
    def heads(x): return jnp.concatenate([keep_head(x,0),keep_head(x,1)],axis=0)
    for a in range(2):
        rs=slice(a*HALF,(a+1)*HALF)
        for pr in range(HEADS//2):
            cs=slice(pr*128,(pr+1)*128)
            Q=qkv_ref[rs,pr*128:(pr+1)*128]; K=qkv_ref[rs,ATT+pr*128:ATT+(pr+1)*128]; V=qkv_ref[rs,2*ATT+pr*128:2*ATT+(pr+1)*128]
            G=dol[rs,cs]
            dp=dot_t(jnp.concatenate([G,prod[rs,cs]],axis=1),jnp.concatenate([heads(V),minus],axis=1))
            es=[e_ref[a,2*pr+h] for h in range(2)]
            ds=[(es[h].astype(f32)*dp[:,h*HALF:(h+1)*HALF]).astype(bf16) for h in range(2)]
            dq=dot(jnp.concatenate(ds,axis=1),heads(K))*0.125
            dk=dot_l(jnp.concatenate(ds,axis=0),heads(Q))
            dv=dot_l(jnp.concatenate(es,axis=0),heads(G))
            dr_ref[rs,cs]=dq.astype(bf16)
            dr_ref[rs,ATT+pr*128:ATT+(pr+1)*128]=dk.astype(bf16)
            dr_ref[rs,2*ATT+pr*128:2*ATT+(pr+1)*128]=dv.astype(bf16)
    un=dot(roll_matrix(b_ref,True),dr_ref[...])
    gq=un[:,0:ATT]+gqc_ref[...]
    pbg_ref[0]+=fold8(gq); pbg_ref[1]+=fold8(un[:,2*ATT:])
    gp_ref[:,0:ATT]=gq.astype(bf16)
    gp_ref[:,ATT:3*ATT]=un[:,ATT:].astype(bf16)
    gp_ref[:,3*ATT:]=gci_ref[...]

def span_back_call(bounds,gm,q,kc,ks,band,cin,kwt,after=()):
    n=gm.shape[0]; R=n//SEQ; NT=SEQ//BT
    row=lambda w_:pl.BlockSpec((SEQ,w_),lambda i,b:(i,0))
    full=lambda s:pl.BlockSpec(s,lambda i,b:(0,)*len(s))
    lead=lambda s:pl.BlockSpec((None,)+s,lambda i,b:(i,)+(0,)*len(s))
    S=lambda s,d:jax.ShapeDtypeStruct(s,d)
    return pl.pallas_call(ordered(span_back_kernel,8,after),
        grid_spec=pltpu.PrefetchScalarGridSpec(num_scalar_prefetch=1,grid=(R,),
        in_specs=[row(D),row(ATT),row(ATT),lead((LANES,SEQ)),lead((NT,HEADS,BT,128)),lead((CPAD,ATT)),full((LANES,ATT))]+waits(after),
        out_specs=[row(ATT),row(ATT),row(ATT),full((LANES,ATT)),full((LANES,128)),full((2,8,ATT))],
        scratch_shapes=[pltpu.VMEM((CPAD,ATT),f32),pltpu.VMEM((SEQ,SEQ),bf16)]),
        out_shape=[S((n,ATT),bf16),S((n,ATT),f32),S((n,ATT),bf16),S((LANES,ATT),f32),S((LANES,128),f32),S((2,8,ATT),f32)],
        compiler_params=pltpu.CompilerParams(vmem_limit_bytes=60<<20),
        cost_estimate=LIGHT,
        name="span_back")(bounds,gm,q,kc,ks,band,cin,kwt,*after)
def attend_back_call(bounds,gm,qkv,E,r,ctx,gqc,gci,after=()):
    n=gm.shape[0]; R=n//SEQ
    row=lambda w_:pl.BlockSpec((SEQ,w_),lambda i,b:(i,0))
    full=lambda s:pl.BlockSpec(s,lambda i,b:(0,)*len(s))
    lead=lambda s:pl.BlockSpec((None,)+s,lambda i,b:(i,)+(0,)*len(s))
    S=lambda s,d:jax.ShapeDtypeStruct(s,d)
    return pl.pallas_call(ordered(attend_back_kernel,8,after),
        grid_spec=pltpu.PrefetchScalarGridSpec(num_scalar_prefetch=1,grid=(R,),
        in_specs=[row(D),row(3*ATT),lead((2,HEADS,HALF,HALF)),row(ATT),row(ATT),row(ATT),row(ATT)]+waits(after),
        out_specs=[row(4*ATT),full((2,8,ATT))],
        scratch_shapes=[pltpu.VMEM((SEQ,3*ATT),bf16)]),
        out_shape=[S((n,4*ATT),bf16),S((2,8,ATT),f32)],
        compiler_params=pltpu.CompilerParams(vmem_limit_bytes=60<<20),
        cost_estimate=LIGHT,
        name="attend_back")(bounds,gm,qkv,E,r,ctx,gqc,gci,*after)

def depth_back_kernel(b_ref,tok_ref,gk_ref,gone_ref,w_ref,cd_ref,out_ref,cdg_ref,gd_ref):
    @pl.when(pl.program_id(0)==0)
    def _(): cdg_ref[...]=jnp.zeros_like(cdg_ref)
    gd_ref[...]=dot_t(gk_ref[...],w_ref[...]).astype(bf16)
    side=[j for j in range(KERNEL) if j!=KERNEL//2]
    for r in range(0,SEQ,BAND):
        lo,bands=tap_bands(b_ref,r)
        stack=jnp.concatenate([bands[j] for j in side],axis=0)
        for c in range(0,D,256):
            cs=slice(c,c+256)
            x=tok_ref[r:r+BAND,cs].astype(f32)
            moved=dot(stack,gd_ref[lo:lo+2*BAND,cs])
            acc=gone_ref[r:r+BAND,cs]
            for j in range(KERNEL):
                m=KERNEL-1-j
                if j==KERNEL//2:
                    v=gd_ref[r:r+BAND,cs].astype(f32)
                else:
                    i=side.index(j)
                    v=moved[i*BAND:(i+1)*BAND]
                acc=acc+v*cd_ref[m:m+1,cs]
                cdg_ref[m,:,cs]+=fold8(v*x)
            out_ref[r:r+BAND,cs]=acc
def depth_back_call(bounds,tok,gk,gone,w,cd,after=()):
    n=tok.shape[0]
    row=lambda w_:pl.BlockSpec((SEQ,w_),lambda i,b:(i,0))
    full=lambda s:pl.BlockSpec(s,lambda i,b:(0,)*len(s))
    S=lambda s,d:jax.ShapeDtypeStruct(s,d)
    return pl.pallas_call(ordered(depth_back_kernel,6,after),
        grid_spec=pltpu.PrefetchScalarGridSpec(num_scalar_prefetch=1,grid=(n//SEQ,),
        in_specs=[row(D),row(ATT),row(D),pl.BlockSpec((D,ATT),lambda i,b:(0,4)),full((KERNEL,D))]+waits(after),
        out_specs=[row(D),full((KERNEL,8,D))],
        scratch_shapes=[pltpu.VMEM((SEQ,D),bf16)]),
        out_shape=[S((n,D),f32),S((KERNEL,8,D),f32)],
        compiler_params=pltpu.CompilerParams(vmem_limit_bytes=60<<20),
        cost_estimate=LIGHT,
        name="depth_taps_back")(bounds,tok,gk,gone,w,cd,*after)
def input_kernel(gp_ref,part_ref,w_ref,out_ref):
    out_ref[...]=part_ref[...]+dot_t(gp_ref[...],w_ref[...])
def input_call(gp,part,w,first,rows,into=None):
    n=gp.shape[0]
    row=lambda w_:pl.BlockSpec((SEQ,w_),lambda i:(i+first,0))
    extra=() if into is None else (into,)
    return pl.pallas_call(ordered(input_kernel,3,extra),grid=(rows,),
        in_specs=[row(4*ATT),row(D),pl.BlockSpec((D,4*ATT),lambda i:(0,0))]+waits(extra),
        out_specs=row(D),
        out_shape=jax.ShapeDtypeStruct((n,D),f32),
        input_output_aliases={} if into is None else {3:0},
        compiler_params=pltpu.CompilerParams(vmem_limit_bytes=60<<20),
        cost_estimate=LIGHT,
        name="input_grad")(gp,part,w,*extra)

SMALL=112
def pack_kernel(att_ref,span_ref,low_ref,kw_ref,kb_ref,norm_ref,up_ref,out_ref,wide_ref):
    wide_ref[...]=jnp.zeros_like(wide_ref)
    wide_ref[0:2,:]=jnp.sum(att_ref[...],axis=1)
    wide_ref[2:4,:]=jnp.sum(span_ref[...],axis=1)
    taps=jnp.sum(low_ref[...],axis=1)
    wide_ref[4:13,:]=taps[:,0:ATT]
    wide_ref[13:22,:]=taps[:,ATT:]
    for h in range(HEADS):
        wide_ref[22+h*KERNEL:22+(h+1)*KERNEL,:]=kw_ref[h*TAPS+SLOT:h*TAPS+SLOT+KERNEL,:]
    norms=jnp.sum(norm_ref[...],axis=1)
    wide_ref[76:82,:]=norms[:,0:ATT]
    wide_ref[82:88,:]=norms[:,ATT:]
    wide_ref[88:96,:]=up_ref[...]
    kb=jnp.concatenate([kb_ref[...],jnp.zeros((128-LANES,128),f32)],axis=0).T
    wide_ref[96:97,0:128]=jnp.sum(kb,axis=0,keepdims=True)
    out_ref[...]=wide_ref[...].astype(bf16)
def pack_call(att,span,low,kw,kb,norm,up):
    return pl.pallas_call(pack_kernel,
        out_shape=jax.ShapeDtypeStruct((SMALL,ATT),bf16),
        scratch_shapes=[pltpu.VMEM((SMALL,ATT),f32)],
        cost_estimate=LIGHT,
        name="pack_small")(att,span,low,kw,kb,norm,up)
def unpack_kernel(count,*refs):
    got=refs[:count]
    proj_ref,depth_ref,kw_ref,kb_ref,hid_ref,up_ref,gain_ref,wide_ref=refs[count:]
    x=got[0][...].astype(f32)
    for g in got[1:]: x=x+g[...].astype(f32)
    wide_ref[...]=x
    proj_ref[...]=wide_ref[0:4,:]
    depth_ref[:,0:ATT]=wide_ref[4:13,:]
    depth_ref[:,ATT:]=wide_ref[13:22,:]
    kw_ref[...]=wide_ref[22:76,:]
    hid_ref[:,0:ATT]=wide_ref[76:80,:]
    hid_ref[:,ATT:]=wide_ref[82:86,:]
    gain_ref[:,0:ATT]=wide_ref[80:82,:]
    gain_ref[:,ATT:]=wide_ref[86:88,:]
    for i in range(FF//ATT): up_ref[0:1,i*ATT:(i+1)*ATT]=wide_ref[88+i:89+i,:]
    for h in range(HEADS): kb_ref[0:1,h*KERNEL:(h+1)*KERNEL]=wide_ref[96:97,h*TAPS+SLOT:h*TAPS+SLOT+KERNEL]
def unpack_call(got):
    S=lambda *s:jax.ShapeDtypeStruct(s,f32)
    out=pl.pallas_call(functools.partial(unpack_kernel,len(got)),
        out_shape=[S(4,ATT),S(KERNEL,D),S(HEADS*KERNEL,ATT),S(1,HEADS*KERNEL),S(4,D),S(1,FF),S(2,D)],
        scratch_shapes=[pltpu.VMEM((SMALL,ATT),f32)],
        cost_estimate=LIGHT,
        name="unpack_small")(*got)
    return [out[0],out[1],out[2].T,out[3].reshape(-1),out[4],out[5].reshape(-1),out[6]]


def digits(axis, size):
    out, bit = [], 1
    while bit < size:
        ways = 4 if size // bit % 4 == 0 else 2
        out.append((axis, size, [d * bit for d in range(ways)]))
        bit *= ways
    return out

def send_xor(x, stage, d):
    axis, size, xors = stage
    return lax.ppermute(x, axis, [(i, i ^ xors[d]) for i in range(size)])

def gather_send(x, stage, less=0):
    return [x] + [send_xor(x, stage, d) for d in range(1, len(stage[2]) - less)]

def gather_order(got, stage):
    axis, _, xors = stage
    ways = len(xors)
    mine = (lax.axis_index(axis) // xors[1]) % ways
    x = got[0]
    parts = []
    for place in range(ways):
        rel = mine ^ place
        part = got[0]
        for d in range(1, ways):
            part = jnp.where(rel == d, got[d], part)
        parts.append(part)
    return jnp.stack(parts, axis=1).reshape((x.shape[0] * ways,) + x.shape[1:])

def gather_near(got):
    return jnp.concatenate(got, axis=0)

def gather_stages(sizes):
    return digits("dp", sizes[0])[::-1] + digits("fsdp", sizes[1])[::-1]

def near_stages(sizes):
    ahead = gather_stages(sizes)
    return ahead, ahead[::-1]

def near_owners(sizes):
    nd, nf = sizes
    table = [0]
    for axis, _, xors in near_stages(sizes)[0]:
        step = nf if axis == "dp" else 1
        table = [x * step + t for x in xors for t in table]
    place = [0] * len(table)
    for i, t in enumerate(table):
        place[t] = i
    me = lax.axis_index("dp") * nf + lax.axis_index("fsdp")
    owners = jnp.asarray(table, jnp.int32) ^ me
    places = jnp.asarray(place, jnp.int32)[jnp.arange(nd * nf) ^ me]
    return owners, places

def scatter_send(g, stage):
    ways = len(stage[2])
    parts = g if isinstance(g, (list, tuple)) else jnp.split(g, ways, axis=0)
    return [parts[0]] + [send_xor(parts[d], stage, d) for d in range(1, ways)]

def scatter_total(got):
    total = got[0].astype(jnp.float32)
    for r in got[1:]:
        total = total + r.astype(jnp.float32)
    return total

def scatter_add(got):
    return scatter_total(got).astype(jnp.bfloat16)

def sum_send(x, stage):
    return [x] + [send_xor(x, stage, d) for d in range(1, len(stage[2]))]

def together(*arrays):
    return lax.optimization_barrier(arrays)


def body(
    tokens,
    segment_ids,
    cotangent,
    w_proj,
    w_point,
    w_out,
    w_up,
    w_down,
    proj_bias,
    conv_depth,
    kernel_weight,
    kernel_bias,
    hidden_bias,
    up_bias,
    norm_gain,
    *,
    sizes,
):
    rows, seq = segment_ids.shape
    nd, nf = sizes
    mid = FF // GROUPS
    shard_rows, ff_rows = D // (nd * nf), mid // (nd * nf)
    tok = tokens.reshape(rows * seq, D)
    cot = cotangent.reshape(rows * seq, D)

    ahead = gather_stages(sizes)
    owners, places = near_owners(sizes)
    first = jnp.concatenate([w_proj, w_point], axis=1).astype(bf16)[None]
    second = jnp.concatenate([jnp.swapaxes(w_up, 1, 2), w_down], axis=2).reshape(GROUPS * ff_rows, D)
    second = jnp.concatenate([second, w_out], axis=0).astype(bf16)[None]
    bounds = find_bounds(segment_ids)
    kernel_rows, kernel_shift = pack_kernel_weight(kernel_weight, kernel_bias)
    up_near = jnp.take(up_bias.reshape(GROUPS, nd * nf, ff_rows), owners, axis=1).reshape(1, FF)
    near, away = near_stages(sizes)
    direct = ff_rows % 16 == 0 and shard_rows % 8 == 0 and len(near) == 3 and sizes[1] == 2
    first = gather_order(gather_send(first, ahead[0]), ahead[0])
    first, second = together(first, second)
    got_first = gather_send(first, ahead[1])
    got_second = gather_send(second, near[0], 1)
    bounds, up_near, kernel_rows, kernel_shift = together(bounds, up_near, kernel_rows, kernel_shift)
    depth = depth_call(bounds, tok, conv_depth)
    *got_second, depth = together(*got_second, depth)
    got_second += gather_send(got_second[0], near[0])[len(got_second) :]
    *got_first, depth = together(*got_first, depth)
    first = gather_order(got_first, ahead[1])
    second = gather_near(got_second)
    got_second = gather_send(second, near[1])
    for stage in ahead[2:]:
        first = gather_order(gather_send(first, stage), stage)
    first = first.reshape(D, 5 * ATT)
    mixed, qkv, expo, recip, context, queries, key_conv, soft, bands, conv_in = mix_call(
        bounds, tok, depth, first, proj_bias, kernel_rows, kernel_shift
    )
    *got_second, mixed = together(*got_second, mixed)
    if direct:
        weights = got_second + [send_xor(piece, near[2], 1) for piece in got_second]
        weight_owners = owners
    else:
        second = gather_near(got_second)
        for stage in near[2:]:
            second = gather_near(gather_send(second, stage))
        ff_full = second[:, : GROUPS * ff_rows].reshape(nd * nf, GROUPS, ff_rows, D)
        ff_full = jnp.swapaxes(ff_full, 0, 1).reshape(GROUPS * mid, D)
        out_full = jnp.take(second[:, GROUPS * ff_rows :], places, axis=0).reshape(D, D)
        weights = [jnp.concatenate([ff_full, out_full], axis=0)[None]]
        weight_owners = jnp.zeros((1,), jnp.int32)
    layer_out, grad_one, grad_mixed, act, raised_low, first_low, two_low, one_low, norm_sums, up_sums = ff_call(
        weight_owners, weights, mixed, tok, cot, hidden_bias, up_near, norm_gain
    )

    if direct:
        parts = ffw_call(owners, act, raised_low, first_low, two_low, mixed, one_low, 2, shard_rows)
    else:
        halves = ffw_call(jnp.arange(2), act, raised_low, first_low, two_low, mixed, one_low, 2, D // 2, True)
        share = jnp.stack(halves)[:, 0]
        out_share = share[:, FF // 2 :].reshape(nd * nf, shard_rows, D)
        share = share[:, : FF // 2].reshape(2, GROUPS, nd * nf // 2, ff_rows, D).swapaxes(1, 2)
        share = share.reshape(nd * nf, GROUPS * ff_rows, D)
        share = jnp.concatenate([share, jnp.take(out_share, owners, axis=0)], axis=1)
        parts = jnp.split(share, len(away[0][2]), axis=0)
    *parts, grad_mixed = together(*parts, grad_mixed)
    if direct:
        got = scatter_send(parts[:2], away[0]) + scatter_send(parts[2:], away[0])
    else:
        got = scatter_send(parts, away[0])
    grad_key, query_part, conv_part, kw_sums, kb_sums, span_sums = span_back_call(
        bounds, grad_mixed, queries, key_conv, soft, bands, conv_in, kernel_rows[:LANES]
    )
    *got, query_part = together(*got, query_part)
    if direct:
        share = turn_call(got, len(away[1][2]), ff_rows)
    else:
        share = jnp.split(scatter_add(got), len(away[1][2]), axis=0)
    *share, query_part = together(*share, query_part)
    got = scatter_send(share, away[1])
    grad_proj, proj_sums = attend_back_call(bounds, grad_mixed, qkv, expo, recip, context, query_part, conv_part)
    grad_key, grad_proj = together(grad_key, grad_proj)
    part, depth_sums = depth_back_call(bounds, tok, grad_key, grad_one, first, conv_depth)
    *got, part, grad_proj = together(*got, part, grad_proj)
    for stage in away[2:-1]:
        got = scatter_send(scatter_add(got), stage)
    share = scatter_add(got)
    up_sums = jnp.take(jnp.sum(up_sums, axis=0).reshape(GROUPS, nd * nf, ff_rows), places, axis=1)
    small = pack_call(
        proj_sums, span_sums, depth_sums, kw_sums, kb_sums, norm_sums, up_sums.reshape(FF // ATT, ATT)
    )
    share, small, grad_proj = together(share, small, grad_proj)
    got_share = scatter_send(share, away[-1])
    got_small = sum_send(small, away[0])
    if direct:
        parts = feature_weights_call(owners, tok, grad_proj, depth, grad_key, 2)
    else:
        halves = feature_weights_call(jnp.arange(2), tok, grad_proj, depth, grad_key, 2)
        late = jnp.concatenate(halves, axis=0).reshape(nd * nf, shard_rows, 5 * ATT)
        parts = jnp.split(jnp.take(late, owners, axis=0), len(away[0][2]), axis=0)
    tied = together(*got_share, *got_small, *parts, part)
    n_share, n_small = len(got_share), len(got_share) + len(got_small)
    got_share, got_small, parts, part = tied[:n_share], tied[n_share:n_small], tied[n_small:-1], tied[-1]
    share = scatter_total(got_share)[0]
    ff_share = share[: GROUPS * ff_rows].reshape(GROUPS, ff_rows, D)
    out_share = share[GROUPS * ff_rows :]
    small = scatter_add(got_small)
    small, part = together(small, part)
    got = scatter_send(parts, away[0])
    got_small = sum_send(small, away[1])
    late = scatter_add(got)
    small = scatter_add(got_small)
    for stage in away[2:-1]:
        small = scatter_add(sum_send(small, stage))
    late, part = together(late, part)
    got = scatter_send(late, away[1])
    axis, size, xors = away[-1]
    bits = [(axis, size, [0, x]) for x in xors[1:] if x & (x - 1) == 0][::-1]
    got_small = sum_send(small, bits[0])
    tokens_grad = input_call(grad_proj, part, first, 0, rows)
    up_share = jnp.swapaxes(ff_share[..., : D // GROUPS], 1, 2)
    down_share = ff_share[..., D // GROUPS :]
    *got, tokens_grad, up_share, down_share = together(*got, tokens_grad, up_share, down_share)
    *got_small, tokens_grad, out_share = together(*got_small, tokens_grad, out_share)
    for stage in away[2:-1]:
        got = scatter_send(scatter_add(got), stage)
    late = scatter_add(got)
    if len(bits) > 1:
        small = scatter_add(got_small)
    late, small = together(late, small)
    got = scatter_send(late, away[-1])
    if len(bits) > 1:
        got_small = sum_send(small, bits[1])
    smalls = unpack_call(got_small)
    proj_share = scatter_total([g[0, :, : 4 * ATT] for g in got])
    point_share = scatter_total([g[0, :, 4 * ATT :] for g in got])
    return (
        layer_out.reshape(rows, seq, D),
        tokens_grad.reshape(rows, seq, D),
        proj_share,
        point_share,
        out_share,
        up_share,
        down_share,
        *smalls,
    )


def solution(mesh):
    whole, split = P(), ("dp", "fsdp")
    rows3, rows2 = P(split, None, None), P(split, None)
    up, down = P(None, None, split), P(None, split, None)
    return jax.shard_map(
        functools.partial(body, sizes=(mesh.shape["dp"], mesh.shape["fsdp"])),
        mesh=mesh,
        in_specs=(rows3, rows2, rows3, rows2, rows2, rows2, up, down) + (whole,) * 7,
        out_specs=(rows3, rows3, rows2, rows2, rows2, up, down) + (whole,) * 7,
        check_vma=False,
    )
```

```python
import functools

import jax
import jax.numpy as jnp
from jax import lax
from jax.experimental import pallas as pl
from jax.experimental.pallas import tpu as pltpu
from jax.sharding import PartitionSpec as P

f32=jnp.float32
bf16=jnp.bfloat16
D=768; FF=3072; HEADS=6; HEAD_DIM=64; KERNEL=9; GROUPS=2; ATT=384
norm_eps=1e-12
LIGHT=pl.CostEstimate(flops=1,bytes_accessed=1,transcendentals=0)
def dot(a,b): return lax.dot_general(a,b,(((1,),(0,)),((),())),preferred_element_type=f32)
def dot_t(a,b): return lax.dot_general(a,b,(((1,),(1,)),((),())),preferred_element_type=f32)
def dot_l(a,b): return lax.dot_general(a,b,(((0,),(0,)),((),())),preferred_element_type=f32)
def fold8(x):
    return jnp.sum(x.reshape(x.shape[0]//8,8,x.shape[1]),axis=0)
def row_mean(x): return jnp.sum(x,axis=-1,keepdims=True)*(1.0/x.shape[-1])

def ordered(kernel,lead,after):
    extra=len(after)
    return lambda *refs: kernel(*refs[:lead],*refs[lead+extra:])
def waits(after):
    return [pl.BlockSpec(memory_space=pl.ANY) for _ in after]

def gelu_parts(x):
    phi=0.5+0.5*lax.erf(x*0.7071067811865476)
    return x*phi, phi+x*(jnp.exp(x*x*-0.5)*0.3989422804014327)

CH=512
PARTS=2
LAG=0
def ff_kernel(pieces,own_ref,*refs):
    w_refs=refs[:pieces]
    (mixed_ref,tok_ref,cot_ref,hb_ref,ub_ref,gain_ref,
     out_ref,gone_ref,gmix_ref,act_ref,gr_ref,xlow_ref,g2low_ref,g1low_ref,sums_ref,ups_ref,
     dg_ref,wup_ref,wdn_ref,wide_ref,wout_ref,keep_ref)=refs[pieces:]
    half=D//GROUPS; mid=FF//GROUPS
    @pl.when(pl.program_id(0)==0)
    def _():
        sums_ref[...]=jnp.zeros_like(sums_ref); ups_ref[...]=jnp.zeros_like(ups_ref)
        at=0
        total=sum(w.shape[0] for w in w_refs)
        rows,share=mid//total,D//total
        for w_ref in w_refs:
            n=w_ref.shape[0]
            for g in range(GROUPS):
                span=slice(at*rows,(at+n)*rows); part=slice(g*rows,(g+1)*rows)
                wup_ref[g,span,:]=w_ref[:,part,0:half].reshape(n*rows,half)
                wdn_ref[g,span,:]=w_ref[:,part,half:].reshape(n*rows,half)
            for i in range(n):
                place=pl.multiple_of(own_ref[at+i]*share,8)
                wide_ref[pl.ds(place,share),:]=w_ref[i,GROUPS*rows:GROUPS*rows+share,:].astype(f32)
            at+=n
        wout_ref[...]=wide_ref[...].astype(bf16)
    spans=[(g,c,slice(g*mid+c,g*mid+c+CH)) for g in range(GROUPS) for c in range(0,mid,CH)]
    gain1,gain2=gain_ref[0:1,:],gain_ref[1:2,:]

    def tokens_part(rs):
        res=dot(mixed_ref[rs,:],wout_ref[...])
        yield
        res=res+hb_ref[0:1,:]+tok_ref[rs,:].astype(f32)
        mean=row_mean(res); cen=res-mean
        inv1=lax.rsqrt(row_mean(cen*cen)+norm_eps)
        n1=cen*inv1
        first=n1*gain1+hb_ref[1:2,:]
        xlow_ref[rs,:]=first.astype(bf16)
        gone_ref[rs,:]=n1
        yield
        def raise_(g,c,cs):
            return dot_t(xlow_ref[rs,g*half:(g+1)*half],wup_ref[g,c:c+CH,:])+ub_ref[0:1,cs]
        lows=[]
        ahead=raise_(*spans[0])
        for i,(g,c,cs) in enumerate(spans):
            raised=ahead
            if i+1<len(spans): ahead=raise_(*spans[i+1])
            yield
            a,dg=gelu_parts(raised)
            act_ref[rs,cs]=a.astype(bf16)
            dg_ref[rs,cs]=dg
            yield
            if c+CH==mid:
                lows.append(dot(act_ref[rs,g*mid:(g+1)*mid],wdn_ref[g]))
                yield
        n1=gone_ref[rs,:]
        res=jnp.concatenate(lows,axis=1)+hb_ref[2:3,:]+(n1*gain1+hb_ref[1:2,:])
        mean=row_mean(res); cen=res-mean
        inv2=lax.rsqrt(row_mean(cen*cen)+norm_eps)
        n2=cen*inv2
        out_ref[rs,:]=(n2*gain2+hb_ref[3:4,:]).astype(bf16)
        yield
        e=cot_ref[rs,:].astype(f32)
        eg=e*gain2
        g2=inv2*(eg-row_mean(eg)-n2*row_mean(eg*n2))
        sums_ref[3]+=fold8(e); sums_ref[5]+=fold8(e*n2); sums_ref[2]+=fold8(g2)
        g2low_ref[rs,:]=g2.astype(bf16)
        keep_ref[rs,:]=g2
        yield
        def fall(g,c,cs):
            return dot_t(g2low_ref[rs,g*half:(g+1)*half],wdn_ref[g,c:c+CH,:])
        parts=[]
        ahead=fall(*spans[0])
        for i,(g,c,cs) in enumerate(spans):
            ga=ahead
            if i+1<len(spans): ahead=fall(*spans[i+1])
            yield
            gr=ga*dg_ref[rs,cs]
            ups_ref[:,cs]+=fold8(gr)
            gr_ref[rs,cs]=gr.astype(bf16)
            yield
            if c+CH==mid:
                parts.append(dot(gr_ref[rs,g*mid:(g+1)*mid],wup_ref[g]))
                yield
        gf=jnp.concatenate(parts,axis=1)+keep_ref[rs,:]
        n1=gone_ref[rs,:]
        sums_ref[1]+=fold8(gf); sums_ref[4]+=fold8(gf*n1)
        yield
        eg=gf*gain1
        g1=inv1*(eg-row_mean(eg)-n1*row_mean(eg*n1))
        sums_ref[0]+=fold8(g1)
        gone_ref[rs,:]=g1
        g1low_ref[rs,:]=g1.astype(bf16)
        yield
        gmix_ref[rs,:]=dot_t(g1low_ref[rs,:],wout_ref[...]).astype(bf16)
    total=mixed_ref.shape[0]; piece=total//PARTS
    running=[tokens_part(slice(i*piece,(i+1)*piece)) for i in range(PARTS)]
    waiting=[i*LAG for i in range(PARTS)]
    while any(part is not None for part in running):
        for i,part in enumerate(running):
            if waiting[i]>0:
                waiting[i]-=1
            elif part is not None and next(part,StopIteration) is StopIteration:
                running[i]=None

def ff_call(owners,weights,mixed,tok,cot,hb,ub,gain,T=512,after=()):
    n=tok.shape[0]
    row=lambda w,:pl.BlockSpec((T,w),lambda i,o:(i,0))
    full=lambda s:pl.BlockSpec(s,lambda i,o:(0,)*len(s),pipeline_mode=pl.Buffered(1))
    S=lambda s,d:jax.ShapeDtypeStruct(s,d)
    W=(GROUPS,FF//GROUPS,D//GROUPS)
    return pl.pallas_call(ordered(functools.partial(ff_kernel,len(weights)),7+len(weights),after),
        grid_spec=pltpu.PrefetchScalarGridSpec(num_scalar_prefetch=1,grid=(n//T,),
        in_specs=[full(w.shape) for w in weights]+[row(D),row(D),row(D),full((4,D)),full((1,FF)),full((2,D))]+waits(after),
        out_specs=[row(D),row(D),row(D),row(FF),row(FF),row(D),row(D),row(D),full((6,8,D)),full((8,FF))],
        scratch_shapes=[pltpu.VMEM((T,FF),f32),pltpu.VMEM(W,bf16),pltpu.VMEM(W,bf16),pltpu.VMEM((D,D),f32),pltpu.VMEM((D,D),bf16),pltpu.VMEM((T,D),f32)]),
        out_shape=[S((n,D),bf16),S((n,D),f32),S((n,D),bf16),S((n,FF),bf16),S((n,FF),bf16),S((n,D),bf16),S((n,D),bf16),S((n,D),bf16),S((6,8,D),f32),S((8,FF),f32)],
        compiler_params=pltpu.CompilerParams(vmem_limit_bytes=60<<20),
        cost_estimate=LIGHT,
        name="feed_forward",
    )(owners,*weights,mixed,tok,cot,hb,ub,gain,*after)

def fetch(pairs,sems):
    copies=[pltpu.make_async_copy(src,dst,sems.at[i]) for i,(src,dst) in enumerate(pairs)]
    for copy in copies: copy.start()
    return copies
def by_owner(own_ref,wide_ref,width,outs,rows,columns):
    per=outs[0].shape[0]; share=rows.stop-rows.start
    for p,out in enumerate(outs):
        for i in range(per):
            place=pl.multiple_of(own_ref[p*per+i]*share,8)
            out[i,rows,columns]=wide_ref[pl.ds(place,share),0:width].astype(bf16)

def ffw_kernel(parts,share,turned,own_ref,act_ref,gr_ref,xlow_ref,g2low_ref,mix_ref,g1_ref,*refs):
    count=parts if turned else 2*parts
    outs=refs[:count]
    act,gr,xlow,g2low,mix,g1,wide,sems=refs[count:count+8]
    blocks=refs[count+8:2*count+8]
    out_sem=refs[-1]
    half=D//GROUPS; mid=FF//GROUPS; C=mid//parts
    jobs=[(p,g) for p in range(parts) for g in range(GROUPS)]
    cols=[slice(g*mid+p*C,g*mid+(p+1)*C) for p,g in jobs]
    pairs=[(xlow_ref,xlow)]+[(gr_ref.at[:,cols[0]],gr.at[0]),(g2low_ref,g2low),(act_ref.at[:,cols[0]],act.at[0])]
    for j in range(1,len(jobs)):
        pairs+=[(gr_ref.at[:,cols[j]],gr.at[j]),(act_ref.at[:,cols[j]],act.at[j])]
    pairs+=[(mix_ref,mix),(g1_ref,g1)]
    copies=fetch(pairs,sems)
    done=[]
    def put(p,g,down,x):
        if turned:
            per=blocks[p].shape[0]; rows=(blocks[p].shape[1]-share)//GROUPS
            blocks[p][:,g*rows:(g+1)*rows,down*half:(down+1)*half]=x.T.astype(bf16).reshape(per,rows,half)
        else:
            blocks[p][2*g+down]=x.astype(bf16)
    def send(i):
        done.append(pltpu.make_async_copy(blocks[i],outs[i],out_sem.at[i]))
        done[-1].start()
    for j,(p,g) in enumerate(jobs):
        gs=slice(g*half,(g+1)*half)
        if j==0: copies[0].wait()
        copies[1 if j==0 else 2+2*j].wait()
        put(p,g,0,dot_l(xlow[:,gs],gr[j]))
        if j==0: copies[2].wait()
        copies[3+2*j].wait()
        put(p,g,1,dot_l(g2low[:,gs],act[j]))
        if g==GROUPS-1 and not turned: send(p)
    copies[-2].wait(); copies[-1].wait()
    wide[...]=dot_l(mix[...],g1[...])
    if turned:
        rows=blocks[0].shape[1]-share
        by_owner(own_ref,wide,D,blocks,slice(rows,rows+share),slice(0,D))
    else:
        by_owner(own_ref,wide,D,blocks[parts:],slice(0,share),slice(0,D))
    for i in range(0 if turned else parts,count): send(i)
    for copy in done: copy.wait()
def ffw_call(owners,act,gr,xlow,g2low,mixed,g1,parts,share,turned=False,after=()):
    n=act.shape[0]; blocks=owners.shape[0]; mid=FF//GROUPS; C=mid//parts
    if turned:
        shapes=[(blocks//parts,FF//blocks+share,D)]*parts
    else:
        shapes=[(2*GROUPS,D//GROUPS,C)]*parts+[(blocks//parts,share,D)]*parts
    any_=pl.BlockSpec(memory_space=pl.ANY)
    jobs=parts*GROUPS
    return pl.pallas_call(ordered(functools.partial(ffw_kernel,parts,share,turned),7,after),
        grid_spec=pltpu.PrefetchScalarGridSpec(num_scalar_prefetch=1,grid=(1,),
        in_specs=[any_]*6+waits(after),out_specs=[any_]*len(shapes),
        scratch_shapes=[pltpu.VMEM((jobs,n,C),bf16)]*2+[pltpu.VMEM((n,D),bf16)]*4+[pltpu.VMEM((D,D),f32),pltpu.SemaphoreType.DMA((2*jobs+4,))]
            +[pltpu.VMEM(s,bf16) for s in shapes]+[pltpu.SemaphoreType.DMA((len(shapes),))]),
        out_shape=[jax.ShapeDtypeStruct(s,bf16) for s in shapes],
        compiler_params=pltpu.CompilerParams(vmem_limit_bytes=60<<20),
        cost_estimate=LIGHT,
        name="feed_forward_weights",
    )(owners,act,gr,xlow,g2low,mixed,g1,*after)

def turn_kernel(rows,ka_ref,ra_ref,kb_ref,rb_ref,*outs):
    half=D//GROUPS
    per=outs[0].shape[0]
    x=(ka_ref[...].astype(f32)+ra_ref[...].astype(f32)).astype(bf16).T
    for i in range(2*GROUPS):
        g,down=i//2,i%2
        @pl.when(pl.program_id(0)==i)
        def _(g=g,down=down):
            for p,out in enumerate(outs):
                out[:,g*rows:(g+1)*rows,down*half:(down+1)*half]=x[p*per*rows:(p+1)*per*rows].reshape(per,rows,half)
    low=GROUPS*rows
    @pl.when(pl.program_id(0)==0)
    def _():
        for p,out in enumerate(outs):
            s=slice(p*per,(p+1)*per)
            out[:,low:,:]=(kb_ref[s].astype(f32)+rb_ref[s].astype(f32)).astype(bf16)
def turn_call(got,parts,rows):
    ka,ra,kb,rb=got
    shape=(kb.shape[0]//parts,GROUPS*rows+kb.shape[1],D)
    one=pl.BlockSpec((None,)+ka.shape[1:],lambda i:(i,0,0))
    full=lambda s:pl.BlockSpec(s,lambda i:(0,0,0))
    return pl.pallas_call(functools.partial(turn_kernel,rows),grid=(2*GROUPS,),
        in_specs=[one,one,full(kb.shape),full(kb.shape)],out_specs=[full(shape)]*parts,
        out_shape=[jax.ShapeDtypeStruct(shape,bf16)]*parts,
        compiler_params=pltpu.CompilerParams(vmem_limit_bytes=60<<20),
        cost_estimate=LIGHT,
        name="add_and_turn")(ka,ra,kb,rb)

def feature_weights_kernel(parts,own_ref,tok_ref,gp_ref,dep_ref,gk_ref,*refs):
    outs=refs[:parts]
    tok,gp,dep,gk,wide,sems=refs[parts:parts+6]
    blocks=refs[parts+6:parts+6+parts]
    out_sem=refs[-1]
    copies=fetch([(gk_ref,gk),(dep_ref,dep),(tok_ref,tok),(gp_ref.at[:,0:2*ATT],gp.at[0]),(gp_ref.at[:,2*ATT:],gp.at[1])],sems)
    rows=slice(0,blocks[0].shape[1])
    copies[0].wait(); copies[1].wait()
    wide[:,0:ATT]=dot_l(dep[...],gk[...])
    by_owner(own_ref,wide,ATT,blocks,rows,slice(4*ATT,5*ATT))
    copies[2].wait()
    for j in range(2):
        copies[3+j].wait()
        wide[...]=dot_l(tok[...],gp[j])
        by_owner(own_ref,wide,D,blocks,rows,slice(j*D,(j+1)*D))
    done=fetch([(blocks[p],outs[p]) for p in range(parts)],out_sem)
    for copy in done: copy.wait()
def feature_weights_call(owners,tok,gp,dep,gk,parts,after=()):
    n=tok.shape[0]; blocks=owners.shape[0]
    shape=(blocks//parts,D//blocks,5*ATT)
    any_=pl.BlockSpec(memory_space=pl.ANY)
    return pl.pallas_call(ordered(functools.partial(feature_weights_kernel,parts),5,after),
        grid_spec=pltpu.PrefetchScalarGridSpec(num_scalar_prefetch=1,grid=(1,),
        in_specs=[any_]*4+waits(after),out_specs=[any_]*parts,
        scratch_shapes=[pltpu.VMEM((n,D),bf16),pltpu.VMEM((2,n,2*ATT),bf16),pltpu.VMEM((n,D),bf16),pltpu.VMEM((n,ATT),bf16),pltpu.VMEM((D,D),f32),pltpu.SemaphoreType.DMA((5,))]
            +[pltpu.VMEM(shape,bf16)]*parts+[pltpu.SemaphoreType.DMA((parts,))]),
        out_shape=[jax.ShapeDtypeStruct(shape,bf16)]*parts,
        compiler_params=pltpu.CompilerParams(vmem_limit_bytes=60<<20),
        cost_estimate=LIGHT,
        name="feature_weights",
    )(owners,tok,gp,dep,gk,*after)

TAPS=16
LANES=HEADS*TAPS
BT=64
LEAD=16
SLOT=4
HALF=256
SEQ=512
NEG=-1000000000.0

def doc_of(pos,b_ref,first=0):
    row=pl.program_id(0)+first
    return ((pos>=b_ref[row,0]).astype(jnp.int32)+(pos>=b_ref[row,1]).astype(jnp.int32)+(pos>=b_ref[row,2]).astype(jnp.int32))
def tap_valid_t(b_ref):
    tap=lax.broadcasted_iota(jnp.int32,(TAPS,SEQ),0); t=lax.broadcasted_iota(jnp.int32,(TAPS,SEQ),1)
    u=t+tap-KERNEL//2-SLOT
    ok=(u>=0)&(u<SEQ)&(doc_of(u,b_ref)==doc_of(t,b_ref))&(tap>=SLOT)&(tap<SLOT+KERNEL)
    return ok.astype(f32)
def roll_matrix(b_ref,back):
    start=b_ref[pl.program_id(0),3]
    a=lax.broadcasted_iota(jnp.int32,(SEQ,SEQ),1 if back else 0); t=lax.broadcasted_iota(jnp.int32,(SEQ,SEQ),0 if back else 1)
    d=a+start-t
    return jnp.where((d==0)|(d==SEQ),1.0,0.0).astype(bf16)
def head_lanes(shape,h):
    lane=lax.broadcasted_iota(jnp.int32,shape,len(shape)-1)
    return (lane<HEAD_DIM) if h==0 else (lane>=HEAD_DIM)
def keep_head(x,h):
    return jnp.where(head_lanes(x.shape,h),x,jnp.zeros_like(x))

BAND=128
def tap_bands(b_ref,r,first=0):
    lo=min(max(r-BAND//2,0),SEQ-2*BAND)
    row=lax.broadcasted_iota(jnp.int32,(BAND,2*BAND),0)+r; col=lax.broadcasted_iota(jnp.int32,(BAND,2*BAND),1)+lo
    step=jnp.where(doc_of(row,b_ref,first)==doc_of(col,b_ref,first),col-row,SEQ)
    return lo,[jnp.where(step==j-KERNEL//2,1.0,0.0).astype(bf16) for j in range(KERNEL)]

def depth_kernel(b_ref,tok_ref,cd_ref,out_ref):
    side=[j for j in range(KERNEL) if j!=KERNEL//2]
    for r in range(0,SEQ,BAND):
        lo,bands=tap_bands(b_ref,r)
        stack=jnp.concatenate([bands[j] for j in side],axis=0)
        for c in range(0,D,256):
            cs=slice(c,c+256)
            moved=dot(stack,tok_ref[lo:lo+2*BAND,cs])
            acc=tok_ref[r:r+BAND,cs].astype(f32)*cd_ref[KERNEL//2:KERNEL//2+1,cs]
            for i,j in enumerate(side):
                acc=acc+moved[i*BAND:(i+1)*BAND]*cd_ref[j:j+1,cs]
            out_ref[r:r+BAND,cs]=acc.astype(bf16)
def depth_call(bounds,tok,cd):
    n=tok.shape[0]
    row=pl.BlockSpec((SEQ,D),lambda i,b:(i,0))
    return pl.pallas_call(depth_kernel,
        grid_spec=pltpu.PrefetchScalarGridSpec(num_scalar_prefetch=1,grid=(n//SEQ,),
        in_specs=[row,pl.BlockSpec((KERNEL,D),lambda i,b:(0,0))],
        out_specs=row),
        out_shape=jax.ShapeDtypeStruct((n,D),bf16),
        compiler_params=pltpu.CompilerParams(vmem_limit_bytes=60<<20),
        cost_estimate=LIGHT,
        name="depth_taps")(bounds,tok,cd)

def mix_kernel(b_ref,tok_ref,dep_ref,w_ref,pb_ref,kw_ref,kb_ref,
               mixed_ref,qkv_ref,e_ref,r_ref,ctx_ref,q_ref,kc_ref,ks_ref,band_ref,cin_ref):
    tok=tok_ref[...]
    p=dot(tok,w_ref[:,0:4*ATT])
    q=(p[:,0:ATT]+pb_ref[0:1,:]).astype(bf16)
    k=p[:,ATT:2*ATT].astype(bf16)
    v=(p[:,2*ATT:3*ATT]+pb_ref[1:2,:]).astype(bf16)
    cin=(p[:,3*ATT:]+pb_ref[2:3,:]).astype(bf16)
    q_ref[...]=q
    rolled=dot(roll_matrix(b_ref,False),jnp.concatenate([q*jnp.bfloat16(0.125),k,v],axis=1)).astype(bf16)
    qkv_ref[...]=rolled
    key_conv=dot(dep_ref[...],w_ref[:,4*ATT:])+pb_ref[3:4,:]
    kc_ref[...]=key_conv
    attn=key_conv*q.astype(f32)
    hi=attn.astype(bf16); lo=(attn-hi.astype(f32)).astype(bf16)
    both=dot_t(kw_ref[...],hi)
    logits=both[:LANES]+both[LANES:]+dot_t(kw_ref[0:LANES,:],lo)+kb_ref[...]
    logits=logits.reshape(HEADS,TAPS,SEQ)
    tap=lax.broadcasted_iota(jnp.int32,(HEADS,TAPS,SEQ),1)
    logits=jnp.where((tap>=SLOT)&(tap<SLOT+KERNEL),logits,-1e30)
    ex=jnp.exp(logits-jnp.max(logits,axis=1,keepdims=True))
    ks=ex/jnp.sum(ex,axis=1,keepdims=True)
    ks_ref[...]=ks.reshape(LANES,SEQ)
    km=(ks*tap_valid_t(b_ref)[None]).reshape(LANES,SEQ)
    km=jnp.concatenate([km,jnp.zeros((128-LANES,SEQ),f32)],axis=0).T
    cin_ref[0:LEAD,:]=jnp.zeros((LEAD,ATT),bf16); cin_ref[LEAD+SEQ:,:]=jnp.zeros((128-LEAD-BT,ATT),bf16)
    cin_ref[LEAD:LEAD+SEQ,:]=cin
    row=lax.broadcasted_iota(jnp.int32,(BT,128),0); lane=lax.broadcasted_iota(jnp.int32,(BT,128),1)
    off=lane-row-(LEAD-KERNEL//2)
    on_band=(off>=0)&(off<KERNEL)
    for i in range(SEQ//BT):
        kmi=km[i*BT:(i+1)*BT,:]
        bands=[]
        for h in range(HEADS):
            x=pltpu.roll(kmi,(LEAD-KERNEL//2-SLOT-h*TAPS)%128,1,stride=1,stride_axis=0)
            x=jnp.where(on_band,x,0.0).astype(bf16)
            band_ref[i,h]=x
            bands.append(x)
        for pr in range(HEADS//2):
            win=cin_ref[i*BT:i*BT+128,pr*128:(pr+1)*128]
            o=dot(jnp.concatenate(bands[2*pr:2*pr+2],axis=1),jnp.concatenate([keep_head(win,0),keep_head(win,1)],axis=0))
            mixed_ref[i*BT:(i+1)*BT,ATT+pr*128:ATT+(pr+1)*128]=o.astype(bf16)
    start=b_ref[pl.program_id(0),3]
    def rolled_doc(axis):
        t=lax.broadcasted_iota(jnp.int32,(HALF,HALF),axis)+start+HALF
        return doc_of(jnp.where(t>=SEQ,t-SEQ,t),b_ref)
    same=rolled_doc(0)==rolled_doc(1)
    ones=jnp.ones((HALF,128),bf16)
    for a in range(2):
        rs=slice(a*HALF,(a+1)*HALF)
        for pr in range(HEADS//2):
            Q=rolled[rs,pr*128:(pr+1)*128]; K=rolled[rs,ATT+pr*128:ATT+(pr+1)*128]; V=rolled[rs,2*ATT+pr*128:2*ATT+(pr+1)*128]
            es=[];vs=[]
            both=dot_t(Q,jnp.concatenate([keep_head(K,0),keep_head(K,1)],axis=0))
            for h in range(2):
                s=both[:,h*HALF:(h+1)*HALF]
                if a==1: s=jnp.where(same,s,NEG)
                e=jnp.exp(s-jnp.max(s,axis=-1,keepdims=True)).astype(bf16)
                e_ref[a,2*pr+h]=e
                es.append(e); vs.append(jnp.concatenate([keep_head(V,h),keep_head(ones,h)],axis=1))
            o=dot(jnp.concatenate(es,axis=1),jnp.concatenate(vs,axis=0))
            r=1.0/o[:,128:]
            r_ref[rs,pr*128:(pr+1)*128]=r
            ctx_ref[rs,pr*128:(pr+1)*128]=(o[:,:128]*r).astype(bf16)
    mixed_ref[:,0:ATT]=dot(roll_matrix(b_ref,True),ctx_ref[...]).astype(bf16)

CPAD=SEQ+128-BT
def mix_call(bounds,tok,dep,w,pb,kw,kb,after=()):
    n=tok.shape[0]; R=n//SEQ
    row=lambda w_:pl.BlockSpec((SEQ,w_),lambda i,b:(i,0))
    full=lambda s:pl.BlockSpec(s,lambda i,b:(0,)*len(s))
    lead=lambda s:pl.BlockSpec((None,)+s,lambda i,b:(i,)+(0,)*len(s))
    S=lambda s,d:jax.ShapeDtypeStruct(s,d)
    NT=SEQ//BT
    return pl.pallas_call(ordered(mix_kernel,7,after),
        grid_spec=pltpu.PrefetchScalarGridSpec(num_scalar_prefetch=1,grid=(R,),
        in_specs=[row(D),row(D),full((D,5*ATT)),full((4,ATT)),full((2*LANES,ATT)),full((LANES,1))]+waits(after),
        out_specs=[row(D),row(3*ATT),lead((2,HEADS,HALF,HALF)),row(ATT),row(ATT),row(ATT),row(ATT),lead((LANES,SEQ)),lead((NT,HEADS,BT,128)),lead((CPAD,ATT))]),
        out_shape=[S((n,D),bf16),S((n,3*ATT),bf16),S((R,2,HEADS,HALF,HALF),bf16),S((n,ATT),f32),S((n,ATT),bf16),S((n,ATT),bf16),S((n,ATT),f32),S((R,LANES,SEQ),f32),S((R,NT,HEADS,BT,128),bf16),S((R,CPAD,ATT),bf16)],
        compiler_params=pltpu.CompilerParams(vmem_limit_bytes=60<<20),
        cost_estimate=LIGHT,
        name="attend_and_span")(bounds,tok,dep,w,pb,kw,kb,*after)


def pack_kernel_weight(kw,kb):
    k=kw.T.reshape(HEADS,KERNEL,ATT)
    k=jnp.pad(k,((0,0),(SLOT,TAPS-KERNEL-SLOT),(0,0))).reshape(LANES,ATT)
    hi=lax.reduce_precision(k,8,7); lo=(k-hi).astype(bf16); hi=hi.astype(bf16)
    b=jnp.pad(kb.reshape(HEADS,KERNEL),((0,0),(SLOT,TAPS-KERNEL-SLOT))).reshape(LANES,1)
    return jnp.concatenate([hi,lo],axis=0),b

def find_bounds(seg):
    counts=jnp.stack([jnp.sum(seg==i,axis=1) for i in range(4)],axis=1)
    begin=jnp.cumsum(counts,axis=1)-counts
    which=jnp.argmax(counts==HALF,axis=1)
    start=jnp.take_along_axis(begin,which[:,None],axis=1)
    return jnp.concatenate([begin[:,1:],start],axis=1).astype(jnp.int32)

def span_back_kernel(b_ref,gm_ref,q_ref,kc_ref,ks_ref,band_ref,cin_ref,kwt_ref,
                gk_ref,gqc_ref,gci_ref,kwg_ref,kbg_ref,pbg_ref,gcin_ref,anti_ref):
    @pl.when(pl.program_id(0)==0)
    def _():
        anti=lax.broadcasted_iota(jnp.int32,(SEQ,SEQ),0)+lax.broadcasted_iota(jnp.int32,(SEQ,SEQ),1)
        anti_ref[...]=jnp.where(anti==SEQ-1,1.0,0.0).astype(bf16)
        kwg_ref[...]=jnp.zeros_like(kwg_ref); kbg_ref[...]=jnp.zeros_like(kbg_ref); pbg_ref[...]=jnp.zeros_like(pbg_ref)
    gcin_ref[...]=jnp.zeros_like(gcin_ref)
    lane=lax.broadcasted_iota(jnp.int32,(BT,128),1)
    anti=anti_ref[...]
    falling=dot(anti,gm_ref[:,ATT:]).astype(bf16)
    logits=[]
    for i in range(SEQ//BT):
        acc=None
        f=SEQ//BT-1-i
        for pr in range(HEADS//2):
            g=gm_ref[i*BT:(i+1)*BT,ATT+pr*128:ATT+(pr+1)*128]
            gf=falling[i*BT:(i+1)*BT,pr*128:(pr+1)*128]
            win=cin_ref[f*BT:f*BT+128,pr*128:(pr+1)*128]
            both=dot_t(jnp.concatenate([keep_head(gf,0),keep_head(gf,1)],axis=0),win)
            for h in range(2):
                head=2*pr+h
                d=pltpu.roll(both[h*BT:(h+1)*BT],(head*TAPS+SLOT-LEAD+KERNEL//2-BT+1)%128,1,stride=1,stride_axis=0)
                d=jnp.where((lane>=head*TAPS+SLOT)&(lane<head*TAPS+SLOT+KERNEL),d,0.0)
                acc=d if acc is None else acc+d
            bands=jnp.concatenate([band_ref[i,2*pr],band_ref[i,2*pr+1]],axis=0)
            gcin_ref[i*BT:i*BT+128,pr*128:(pr+1)*128]+=dot_l(bands,jnp.concatenate([keep_head(g,0),keep_head(g,1)],axis=0))
        logits.append(acc)
    gk=jnp.concatenate(logits,axis=0)
    gh=gk.astype(bf16); glo=(gk-gh.astype(f32)).astype(bf16)
    gk=(dot_l(gh,anti)+dot_l(glo,anti))[0:LANES,:].reshape(HEADS,TAPS,SEQ)*tap_valid_t(b_ref)[None]
    ks=ks_ref[...].reshape(HEADS,TAPS,SEQ)
    gl=(ks*(gk-jnp.sum(gk*ks,axis=1,keepdims=True))).reshape(LANES,SEQ)
    kbg_ref[...]+=gl[:,0:128]+gl[:,128:256]+gl[:,256:384]+gl[:,384:512]
    q=q_ref[...].astype(f32); kc=kc_ref[...]
    attn=kc*q
    hi=attn.astype(bf16)
    glb=gl.astype(bf16)
    kwg_ref[...]+=dot(glb,hi)
    gattn=dot_l(glb,kwt_ref[...])
    gkc=gattn*q
    gk_ref[...]=gkc.astype(bf16)
    pbg_ref[1]+=fold8(gkc)
    gqc_ref[...]=gattn*kc
    gci=gcin_ref[LEAD:LEAD+SEQ,:]
    pbg_ref[0]+=fold8(gci)
    gci_ref[...]=gci.astype(bf16)

def attend_back_kernel(b_ref,gm_ref,qkv_ref,e_ref,r_ref,ctx_ref,gqc_ref,gci_ref,gp_ref,pbg_ref,dr_ref):
    @pl.when(pl.program_id(0)==0)
    def _(): pbg_ref[...]=jnp.zeros_like(pbg_ref)
    dor=(dot(roll_matrix(b_ref,False),gm_ref[:,0:ATT])*r_ref[...])
    dol=dor.astype(bf16)
    prod=(dol.astype(f32)*ctx_ref[...].astype(f32)).astype(bf16)
    minus=jnp.full((HALF,128),-1.0,bf16)
    minus=jnp.concatenate([keep_head(minus,0),keep_head(minus,1)],axis=0)
    def heads(x): return jnp.concatenate([keep_head(x,0),keep_head(x,1)],axis=0)
    for a in range(2):
        rs=slice(a*HALF,(a+1)*HALF)
        for pr in range(HEADS//2):
            cs=slice(pr*128,(pr+1)*128)
            Q=qkv_ref[rs,pr*128:(pr+1)*128]; K=qkv_ref[rs,ATT+pr*128:ATT+(pr+1)*128]; V=qkv_ref[rs,2*ATT+pr*128:2*ATT+(pr+1)*128]
            G=dol[rs,cs]
            dp=dot_t(jnp.concatenate([G,prod[rs,cs]],axis=1),jnp.concatenate([heads(V),minus],axis=1))
            es=[e_ref[a,2*pr+h] for h in range(2)]
            ds=[(es[h].astype(f32)*dp[:,h*HALF:(h+1)*HALF]).astype(bf16) for h in range(2)]
            dq=dot(jnp.concatenate(ds,axis=1),heads(K))*0.125
            dk=dot_l(jnp.concatenate(ds,axis=0),heads(Q))
            dv=dot_l(jnp.concatenate(es,axis=0),heads(G))
            dr_ref[rs,cs]=dq.astype(bf16)
            dr_ref[rs,ATT+pr*128:ATT+(pr+1)*128]=dk.astype(bf16)
            dr_ref[rs,2*ATT+pr*128:2*ATT+(pr+1)*128]=dv.astype(bf16)
    un=dot(roll_matrix(b_ref,True),dr_ref[...])
    gq=un[:,0:ATT]+gqc_ref[...]
    pbg_ref[0]+=fold8(gq); pbg_ref[1]+=fold8(un[:,2*ATT:])
    gp_ref[:,0:ATT]=gq.astype(bf16)
    gp_ref[:,ATT:3*ATT]=un[:,ATT:].astype(bf16)
    gp_ref[:,3*ATT:]=gci_ref[...]

def span_back_call(bounds,gm,q,kc,ks,band,cin,kwt,after=()):
    n=gm.shape[0]; R=n//SEQ; NT=SEQ//BT
    row=lambda w_:pl.BlockSpec((SEQ,w_),lambda i,b:(i,0))
    full=lambda s:pl.BlockSpec(s,lambda i,b:(0,)*len(s))
    lead=lambda s:pl.BlockSpec((None,)+s,lambda i,b:(i,)+(0,)*len(s))
    S=lambda s,d:jax.ShapeDtypeStruct(s,d)
    return pl.pallas_call(ordered(span_back_kernel,8,after),
        grid_spec=pltpu.PrefetchScalarGridSpec(num_scalar_prefetch=1,grid=(R,),
        in_specs=[row(D),row(ATT),row(ATT),lead((LANES,SEQ)),lead((NT,HEADS,BT,128)),lead((CPAD,ATT)),full((LANES,ATT))]+waits(after),
        out_specs=[row(ATT),row(ATT),row(ATT),full((LANES,ATT)),full((LANES,128)),full((2,8,ATT))],
        scratch_shapes=[pltpu.VMEM((CPAD,ATT),f32),pltpu.VMEM((SEQ,SEQ),bf16)]),
        out_shape=[S((n,ATT),bf16),S((n,ATT),f32),S((n,ATT),bf16),S((LANES,ATT),f32),S((LANES,128),f32),S((2,8,ATT),f32)],
        compiler_params=pltpu.CompilerParams(vmem_limit_bytes=60<<20),
        cost_estimate=LIGHT,
        name="span_back")(bounds,gm,q,kc,ks,band,cin,kwt,*after)
def attend_back_call(bounds,gm,qkv,E,r,ctx,gqc,gci,after=()):
    n=gm.shape[0]; R=n//SEQ
    row=lambda w_:pl.BlockSpec((SEQ,w_),lambda i,b:(i,0))
    full=lambda s:pl.BlockSpec(s,lambda i,b:(0,)*len(s))
    lead=lambda s:pl.BlockSpec((None,)+s,lambda i,b:(i,)+(0,)*len(s))
    S=lambda s,d:jax.ShapeDtypeStruct(s,d)
    return pl.pallas_call(ordered(attend_back_kernel,8,after),
        grid_spec=pltpu.PrefetchScalarGridSpec(num_scalar_prefetch=1,grid=(R,),
        in_specs=[row(D),row(3*ATT),lead((2,HEADS,HALF,HALF)),row(ATT),row(ATT),row(ATT),row(ATT)]+waits(after),
        out_specs=[row(4*ATT),full((2,8,ATT))],
        scratch_shapes=[pltpu.VMEM((SEQ,3*ATT),bf16)]),
        out_shape=[S((n,4*ATT),bf16),S((2,8,ATT),f32)],
        compiler_params=pltpu.CompilerParams(vmem_limit_bytes=60<<20),
        cost_estimate=LIGHT,
        name="attend_back")(bounds,gm,qkv,E,r,ctx,gqc,gci,*after)

def depth_back_kernel(b_ref,tok_ref,gk_ref,gone_ref,w_ref,cd_ref,out_ref,cdg_ref,gd_ref):
    @pl.when(pl.program_id(0)==0)
    def _(): cdg_ref[...]=jnp.zeros_like(cdg_ref)
    gd_ref[...]=dot_t(gk_ref[...],w_ref[...]).astype(bf16)
    side=[j for j in range(KERNEL) if j!=KERNEL//2]
    for r in range(0,SEQ,BAND):
        lo,bands=tap_bands(b_ref,r)
        stack=jnp.concatenate([bands[j] for j in side],axis=0)
        for c in range(0,D,256):
            cs=slice(c,c+256)
            x=tok_ref[r:r+BAND,cs].astype(f32)
            moved=dot(stack,gd_ref[lo:lo+2*BAND,cs])
            acc=gone_ref[r:r+BAND,cs]
            for j in range(KERNEL):
                m=KERNEL-1-j
                if j==KERNEL//2:
                    v=gd_ref[r:r+BAND,cs].astype(f32)
                else:
                    i=side.index(j)
                    v=moved[i*BAND:(i+1)*BAND]
                acc=acc+v*cd_ref[m:m+1,cs]
                cdg_ref[m,:,cs]+=fold8(v*x)
            out_ref[r:r+BAND,cs]=acc
def depth_back_call(bounds,tok,gk,gone,w,cd,after=()):
    n=tok.shape[0]
    row=lambda w_:pl.BlockSpec((SEQ,w_),lambda i,b:(i,0))
    full=lambda s:pl.BlockSpec(s,lambda i,b:(0,)*len(s))
    S=lambda s,d:jax.ShapeDtypeStruct(s,d)
    return pl.pallas_call(ordered(depth_back_kernel,6,after),
        grid_spec=pltpu.PrefetchScalarGridSpec(num_scalar_prefetch=1,grid=(n//SEQ,),
        in_specs=[row(D),row(ATT),row(D),pl.BlockSpec((D,ATT),lambda i,b:(0,4)),full((KERNEL,D))]+waits(after),
        out_specs=[row(D),full((KERNEL,8,D))],
        scratch_shapes=[pltpu.VMEM((SEQ,D),bf16)]),
        out_shape=[S((n,D),f32),S((KERNEL,8,D),f32)],
        compiler_params=pltpu.CompilerParams(vmem_limit_bytes=60<<20),
        cost_estimate=LIGHT,
        name="depth_taps_back")(bounds,tok,gk,gone,w,cd,*after)
def input_kernel(gp_ref,part_ref,w_ref,out_ref):
    out_ref[...]=part_ref[...]+dot_t(gp_ref[...],w_ref[...])
def input_call(gp,part,w,first,rows,into=None):
    n=gp.shape[0]
    row=lambda w_:pl.BlockSpec((SEQ,w_),lambda i:(i+first,0))
    extra=() if into is None else (into,)
    return pl.pallas_call(ordered(input_kernel,3,extra),grid=(rows,),
        in_specs=[row(4*ATT),row(D),pl.BlockSpec((D,4*ATT),lambda i:(0,0))]+waits(extra),
        out_specs=row(D),
        out_shape=jax.ShapeDtypeStruct((n,D),f32),
        input_output_aliases={} if into is None else {3:0},
        compiler_params=pltpu.CompilerParams(vmem_limit_bytes=60<<20),
        cost_estimate=LIGHT,
        name="input_grad")(gp,part,w,*extra)

SMALL=112
def pack_kernel(att_ref,span_ref,low_ref,kw_ref,kb_ref,norm_ref,up_ref,out_ref,wide_ref):
    wide_ref[...]=jnp.zeros_like(wide_ref)
    wide_ref[0:2,:]=jnp.sum(att_ref[...],axis=1)
    wide_ref[2:4,:]=jnp.sum(span_ref[...],axis=1)
    taps=jnp.sum(low_ref[...],axis=1)
    wide_ref[4:13,:]=taps[:,0:ATT]
    wide_ref[13:22,:]=taps[:,ATT:]
    for h in range(HEADS):
        wide_ref[22+h*KERNEL:22+(h+1)*KERNEL,:]=kw_ref[h*TAPS+SLOT:h*TAPS+SLOT+KERNEL,:]
    norms=jnp.sum(norm_ref[...],axis=1)
    wide_ref[76:82,:]=norms[:,0:ATT]
    wide_ref[82:88,:]=norms[:,ATT:]
    wide_ref[88:96,:]=up_ref[...]
    kb=jnp.concatenate([kb_ref[...],jnp.zeros((128-LANES,128),f32)],axis=0).T
    wide_ref[96:97,0:128]=jnp.sum(kb,axis=0,keepdims=True)
    out_ref[...]=wide_ref[...].astype(bf16)
def pack_call(att,span,low,kw,kb,norm,up):
    return pl.pallas_call(pack_kernel,
        out_shape=jax.ShapeDtypeStruct((SMALL,ATT),bf16),
        scratch_shapes=[pltpu.VMEM((SMALL,ATT),f32)],
        cost_estimate=LIGHT,
        name="pack_small")(att,span,low,kw,kb,norm,up)
def unpack_kernel(count,*refs):
    got=refs[:count]
    proj_ref,depth_ref,kw_ref,kb_ref,hid_ref,up_ref,gain_ref,wide_ref=refs[count:]
    x=got[0][...].astype(f32)
    for g in got[1:]: x=x+g[...].astype(f32)
    wide_ref[...]=x
    proj_ref[...]=wide_ref[0:4,:]
    depth_ref[:,0:ATT]=wide_ref[4:13,:]
    depth_ref[:,ATT:]=wide_ref[13:22,:]
    kw_ref[...]=wide_ref[22:76,:]
    hid_ref[:,0:ATT]=wide_ref[76:80,:]
    hid_ref[:,ATT:]=wide_ref[82:86,:]
    gain_ref[:,0:ATT]=wide_ref[80:82,:]
    gain_ref[:,ATT:]=wide_ref[86:88,:]
    for i in range(FF//ATT): up_ref[0:1,i*ATT:(i+1)*ATT]=wide_ref[88+i:89+i,:]
    for h in range(HEADS): kb_ref[0:1,h*KERNEL:(h+1)*KERNEL]=wide_ref[96:97,h*TAPS+SLOT:h*TAPS+SLOT+KERNEL]
def unpack_call(got):
    S=lambda *s:jax.ShapeDtypeStruct(s,f32)
    out=pl.pallas_call(functools.partial(unpack_kernel,len(got)),
        out_shape=[S(4,ATT),S(KERNEL,D),S(HEADS*KERNEL,ATT),S(1,HEADS*KERNEL),S(4,D),S(1,FF),S(2,D)],
        scratch_shapes=[pltpu.VMEM((SMALL,ATT),f32)],
        cost_estimate=LIGHT,
        name="unpack_small")(*got)
    return [out[0],out[1],out[2].T,out[3].reshape(-1),out[4],out[5].reshape(-1),out[6]]


def digits(axis, size):
    out, bit = [], 1
    while bit < size:
        ways = 4 if size // bit % 4 == 0 else 2
        out.append((axis, size, [d * bit for d in range(ways)]))
        bit *= ways
    return out

def send_xor(x, stage, d):
    axis, size, xors = stage
    return lax.ppermute(x, axis, [(i, i ^ xors[d]) for i in range(size)])

def gather_send(x, stage, less=0):
    return [x] + [send_xor(x, stage, d) for d in range(1, len(stage[2]) - less)]

def gather_order(got, stage):
    axis, _, xors = stage
    ways = len(xors)
    mine = (lax.axis_index(axis) // xors[1]) % ways
    x = got[0]
    parts = []
    for place in range(ways):
        rel = mine ^ place
        part = got[0]
        for d in range(1, ways):
            part = jnp.where(rel == d, got[d], part)
        parts.append(part)
    return jnp.stack(parts, axis=1).reshape((x.shape[0] * ways,) + x.shape[1:])

def gather_near(got):
    return jnp.concatenate(got, axis=0)

def gather_stages(sizes):
    return digits("dp", sizes[0])[::-1] + digits("fsdp", sizes[1])[::-1]

def near_stages(sizes):
    ahead = gather_stages(sizes)
    return ahead, ahead[::-1]

def near_owners(sizes):
    nd, nf = sizes
    table = [0]
    for axis, _, xors in near_stages(sizes)[0]:
        step = nf if axis == "dp" else 1
        table = [x * step + t for x in xors for t in table]
    place = [0] * len(table)
    for i, t in enumerate(table):
        place[t] = i
    me = lax.axis_index("dp") * nf + lax.axis_index("fsdp")
    owners = jnp.asarray(table, jnp.int32) ^ me
    places = jnp.asarray(place, jnp.int32)[jnp.arange(nd * nf) ^ me]
    return owners, places

def scatter_send(g, stage):
    ways = len(stage[2])
    parts = g if isinstance(g, (list, tuple)) else jnp.split(g, ways, axis=0)
    return [parts[0]] + [send_xor(parts[d], stage, d) for d in range(1, ways)]

def scatter_total(got):
    total = got[0].astype(jnp.float32)
    for r in got[1:]:
        total = total + r.astype(jnp.float32)
    return total

def scatter_add(got):
    return scatter_total(got).astype(jnp.bfloat16)

def sum_send(x, stage):
    return [x] + [send_xor(x, stage, d) for d in range(1, len(stage[2]))]

def together(*arrays):
    return lax.optimization_barrier(arrays)


def body(
    tokens,
    segment_ids,
    cotangent,
    w_proj,
    w_point,
    w_out,
    w_up,
    w_down,
    proj_bias,
    conv_depth,
    kernel_weight,
    kernel_bias,
    hidden_bias,
    up_bias,
    norm_gain,
    *,
    sizes,
):
    rows, seq = segment_ids.shape
    nd, nf = sizes
    mid = FF // GROUPS
    shard_rows, ff_rows = D // (nd * nf), mid // (nd * nf)
    tok = tokens.reshape(rows * seq, D)
    cot = cotangent.reshape(rows * seq, D)

    ahead = gather_stages(sizes)
    owners, places = near_owners(sizes)
    first = jnp.concatenate([w_proj, w_point], axis=1).astype(bf16)[None]
    second = jnp.concatenate([jnp.swapaxes(w_up, 1, 2), w_down], axis=2).reshape(GROUPS * ff_rows, D)
    second = jnp.concatenate([second, w_out], axis=0).astype(bf16)[None]
    bounds = find_bounds(segment_ids)
    kernel_rows, kernel_shift = pack_kernel_weight(kernel_weight, kernel_bias)
    up_near = jnp.take(up_bias.reshape(GROUPS, nd * nf, ff_rows), owners, axis=1).reshape(1, FF)
    near, away = near_stages(sizes)
    direct = ff_rows % 16 == 0 and shard_rows % 8 == 0 and len(near) == 3 and sizes[1] == 2
    first = gather_order(gather_send(first, ahead[0]), ahead[0])
    first, second = together(first, second)
    got_first = gather_send(first, ahead[1])
    got_second = gather_send(second, near[0], 1)
    bounds, up_near, kernel_rows, kernel_shift = together(bounds, up_near, kernel_rows, kernel_shift)
    depth = depth_call(bounds, tok, conv_depth)
    *got_second, depth = together(*got_second, depth)
    got_second += gather_send(got_second[0], near[0])[len(got_second) :]
    *got_first, depth = together(*got_first, depth)
    first = gather_order(got_first, ahead[1])
    second = gather_near(got_second)
    got_second = gather_send(second, near[1])
    for stage in ahead[2:]:
        first = gather_order(gather_send(first, stage), stage)
    first = first.reshape(D, 5 * ATT)
    mixed, qkv, expo, recip, context, queries, key_conv, soft, bands, conv_in = mix_call(
        bounds, tok, depth, first, proj_bias, kernel_rows, kernel_shift
    )
    *got_second, mixed = together(*got_second, mixed)
    if direct:
        weights = got_second + [send_xor(piece, near[2], 1) for piece in got_second]
        weight_owners = owners
    else:
        second = gather_near(got_second)
        for stage in near[2:]:
            second = gather_near(gather_send(second, stage))
        ff_full = second[:, : GROUPS * ff_rows].reshape(nd * nf, GROUPS, ff_rows, D)
        ff_full = jnp.swapaxes(ff_full, 0, 1).reshape(GROUPS * mid, D)
        out_full = jnp.take(second[:, GROUPS * ff_rows :], places, axis=0).reshape(D, D)
        weights = [jnp.concatenate([ff_full, out_full], axis=0)[None]]
        weight_owners = jnp.zeros((1,), jnp.int32)
    layer_out, grad_one, grad_mixed, act, raised_low, first_low, two_low, one_low, norm_sums, up_sums = ff_call(
        weight_owners, weights, mixed, tok, cot, hidden_bias, up_near, norm_gain
    )

    if direct:
        parts = ffw_call(owners, act, raised_low, first_low, two_low, mixed, one_low, 2, shard_rows)
    else:
        halves = ffw_call(jnp.arange(2), act, raised_low, first_low, two_low, mixed, one_low, 2, D // 2, True)
        share = jnp.stack(halves)[:, 0]
        out_share = share[:, FF // 2 :].reshape(nd * nf, shard_rows, D)
        share = share[:, : FF // 2].reshape(2, GROUPS, nd * nf // 2, ff_rows, D).swapaxes(1, 2)
        share = share.reshape(nd * nf, GROUPS * ff_rows, D)
        share = jnp.concatenate([share, jnp.take(out_share, owners, axis=0)], axis=1)
        parts = jnp.split(share, len(away[0][2]), axis=0)
    *parts, grad_mixed = together(*parts, grad_mixed)
    if direct:
        got = scatter_send(parts[:2], away[0]) + scatter_send(parts[2:], away[0])
    else:
        got = scatter_send(parts, away[0])
    grad_key, query_part, conv_part, kw_sums, kb_sums, span_sums = span_back_call(
        bounds, grad_mixed, queries, key_conv, soft, bands, conv_in, kernel_rows[:LANES]
    )
    *got, query_part = together(*got, query_part)
    if direct:
        share = turn_call(got, len(away[1][2]), ff_rows)
    else:
        share = jnp.split(scatter_add(got), len(away[1][2]), axis=0)
    *share, query_part = together(*share, query_part)
    got = scatter_send(share, away[1])
    grad_proj, proj_sums = attend_back_call(bounds, grad_mixed, qkv, expo, recip, context, query_part, conv_part)
    grad_key, grad_proj = together(grad_key, grad_proj)
    part, depth_sums = depth_back_call(bounds, tok, grad_key, grad_one, first, conv_depth)
    *got, part, grad_proj = together(*got, part, grad_proj)
    for stage in away[2:-1]:
        got = scatter_send(scatter_add(got), stage)
    share = scatter_add(got)
    up_sums = jnp.take(jnp.sum(up_sums, axis=0).reshape(GROUPS, nd * nf, ff_rows), places, axis=1)
    small = pack_call(
        proj_sums, span_sums, depth_sums, kw_sums, kb_sums, norm_sums, up_sums.reshape(FF // ATT, ATT)
    )
    share, grad_proj = together(share, grad_proj)
    got_share = scatter_send(share, away[-1])
    got_small = sum_send(small, away[0])
    if direct:
        parts = feature_weights_call(owners, tok, grad_proj, depth, grad_key, 2)
    else:
        halves = feature_weights_call(jnp.arange(2), tok, grad_proj, depth, grad_key, 2)
        late = jnp.concatenate(halves, axis=0).reshape(nd * nf, shard_rows, 5 * ATT)
        parts = jnp.split(jnp.take(late, owners, axis=0), len(away[0][2]), axis=0)
    tied = together(*got_share, *got_small, *parts, part)
    n_share, n_small = len(got_share), len(got_share) + len(got_small)
    got_share, got_small, parts, part = tied[:n_share], tied[n_share:n_small], tied[n_small:-1], tied[-1]
    share = scatter_total(got_share)[0]
    ff_share = share[: GROUPS * ff_rows].reshape(GROUPS, ff_rows, D)
    out_share = share[GROUPS * ff_rows :]
    small = scatter_add(got_small)
    small, part = together(small, part)
    got = scatter_send(parts, away[0])
    got_small = sum_send(small, away[1])
    late = scatter_add(got)
    small = scatter_add(got_small)
    for stage in away[2:-1]:
        small = scatter_add(sum_send(small, stage))
    late, part = together(late, part)
    got = scatter_send(late, away[1])
    axis, size, xors = away[-1]
    bits = [(axis, size, [0, x]) for x in xors[1:] if x & (x - 1) == 0][::-1]
    got_small = sum_send(small, bits[0])
    tokens_grad = input_call(grad_proj, part, first, 0, rows)
    up_share = jnp.swapaxes(ff_share[..., : D // GROUPS], 1, 2)
    down_share = ff_share[..., D // GROUPS :]
    *got, tokens_grad, up_share, down_share = together(*got, tokens_grad, up_share, down_share)
    *got_small, tokens_grad, out_share = together(*got_small, tokens_grad, out_share)
    for stage in away[2:-1]:
        got = scatter_send(scatter_add(got), stage)
    late = scatter_add(got)
    if len(bits) > 1:
        small = scatter_add(got_small)
    late, small = together(late, small)
    got = scatter_send(late, away[-1])
    if len(bits) > 1:
        got_small = sum_send(small, bits[1])
    smalls = unpack_call(got_small)
    proj_share = scatter_total([g[0, :, : 4 * ATT] for g in got])
    point_share = scatter_total([g[0, :, 4 * ATT :] for g in got])
    return (
        layer_out.reshape(rows, seq, D),
        tokens_grad.reshape(rows, seq, D),
        proj_share,
        point_share,
        out_share,
        up_share,
        down_share,
        *smalls,
    )


def solution(mesh):
    whole, split = P(), ("dp", "fsdp")
    rows3, rows2 = P(split, None, None), P(split, None)
    up, down = P(None, None, split), P(None, split, None)
    return jax.shard_map(
        functools.partial(body, sizes=(mesh.shape["dp"], mesh.shape["fsdp"])),
        mesh=mesh,
        in_specs=(rows3, rows2, rows3, rows2, rows2, rows2, up, down) + (whole,) * 7,
        out_specs=(rows3, rows3, rows2, rows2, rows2, up, down) + (whole,) * 7,
        check_vma=False,
    )
```
